32 devices in a mesh: dp: 4 (over x, core), row: 4 (over z), col: 2 (over y).
Axes of the slice: x: 2, y: 2, z: 4, core: 2. Of those that a mesh axis runs over, the one named last changes fastest.
Arguments:
- tokens: bfloat16 [2, 10240, 2048], P(None, ('dp', 'row'), 'col'), may hold values from -6 to 6
- out_grad: bfloat16 [2, 10240, 2048], P(None, ('dp', 'row'), 'col'), may hold values from -6 to 6
- path: int32 [2, 10240, 3], P(None, 'dp'), may hold values from 0 to 103, as said below
- positions: int32 [2, 10240], P(None, 'dp'), may hold values from 0 to 1343, as said below
- w_query: bfloat16 [2048, 2048], P('col', 'row'), may hold values from -0.125 to 0.125
- w_key: bfloat16 [2048, 1024], P('col', 'row'), may hold values from -0.125 to 0.125
- w_value: bfloat16 [2048, 1024], P('col', 'row'), may hold values from -0.125 to 0.125
- w_out: bfloat16 [2048, 2048], P('row', 'col'), may hold values from -1.5 to 1.5
- w_gate: bfloat16 [2048, 8192], P('col', 'row'), may hold values from -0.125 to 0.125
- w_up: bfloat16 [2048, 8192], P('col', 'row'), may hold values from -0.125 to 0.125
- w_down: bfloat16 [8192, 2048], P('row', 'col'), may hold values from -0.0625 to 0.0625
- gain_attn: float32 [2048], P('col'), may hold values from 0.25 to 1.75
- gain_ffn: float32 [2048], P('col'), may hold values from 0.25 to 1.75
Outputs:
- output: bfloat16 [2, 10240, 2048], P(None, ('dp', 'row'), 'col')
- token_grad: bfloat16 [2, 10240, 2048], P(None, ('dp', 'row'), 'col')
- w_query_grad: float32 [2048, 2048], P('col', 'row')
- w_key_grad: float32 [2048, 1024], P('col', 'row')
- w_value_grad: float32 [2048, 1024], P('col', 'row')
- w_out_grad: float32 [2048, 2048], P('row', 'col')
- w_gate_grad: float32 [2048, 8192], P('col', 'row')
- w_up_grad: float32 [2048, 8192], P('col', 'row')
- w_down_grad: float32 [8192, 2048], P('row', 'col')
- gain_attn_grad: float32 [2048], P('col')
- gain_ffn_grad: float32 [2048], P('col')
The draws below stay inside these ranges and needn't reach their ends.
Inputs may be any that keep to these rules, and one draw needn't show every extreme that they name: Each tree fills 2560 consecutive tokens of a micro-batch, one tree for each index of dp: a trunk of 1024 tokens, then 4 branches of 128 tokens, each a child of the trunk, then 8 leaves, leaf j a child of branch j // 2, of 64 to 192 tokens that sum to 1024; leaf 0 has exactly 192 tokens and leaf 4 exactly 64. path holds a token's segment label, its parent's and its grandparent's, repeating the top label where there is none; each of the 13 segments of a tree has its own label, and labels of different trees differ. `positions`: A trunk token's position is its index in the trunk, a branch token's 1024 plus its index in the branch, a leaf token's 1024 + 128 plus its index in the leaf.
All inputs are finite; a program needn't handle non-finite values.
Results may differ from the reference program's by a relative error of at most 0.02.
Values may be sent and summed in bfloat16 or wider, within the bound.
No kernel may reach another device: no remote copies, remote signals or barrier semaphores. Data moves between devices by JAX's collectives and lax.ppermute only.
A program may use at most 448 MiB of HBM per device.

```python
import math
import jax
import jax.numpy as jnp
from jax import lax

D = 2048
HEADS = 16
KV_HEADS = 8
HEAD = 128
FF = 8192
TRUNK = 1024
BRANCH = 128
LEAF = 128
MICRO = 2
TREE_LEN = 2560
TOK_MB = 10240
TREES = 8


def tree_tables(key):
    tree_keys = jax.random.split(jax.random.fold_in(key, 7), TREES)

    def one_tree(tree_key, tree):
        shift_key, label_key = jax.random.split(tree_key)
        half = LEAF // 2
        others = jax.random.randint(shift_key, (3,), -half, half + 1).astype(jnp.int32)
        shifts = jnp.concatenate([jnp.full((1,), half, jnp.int32), others])
        lengths = LEAF + jnp.concatenate([shifts, -shifts])
        starts = jnp.concatenate([jnp.zeros((1,), jnp.int32), jnp.cumsum(lengths)[:-1].astype(jnp.int32)])
        token = jnp.arange(TREE_LEN, dtype=jnp.int32)
        leaf_begin = TRUNK + 4 * BRANCH
        in_branch = (token >= TRUNK) & (token < leaf_begin)
        in_leaf = token >= leaf_begin
        branch_index = jnp.clip((token - TRUNK) // BRANCH, 0, 3)
        leaf_offset = token - leaf_begin
        leaf_index = jnp.sum((leaf_offset[:, None] >= starts[None, 1:]).astype(jnp.int32), axis=1)
        own = jnp.where(in_leaf, 5 + leaf_index, jnp.where(in_branch, 1 + branch_index, 0))
        parent = jnp.where(in_leaf, 1 + leaf_index // 2, 0)
        place = jnp.where(in_leaf, TRUNK + BRANCH + leaf_offset - starts[leaf_index], jnp.where(in_branch, TRUNK + (token - TRUNK) % BRANCH, token))
        labels = jax.random.permutation(label_key, 13).astype(jnp.int32) + tree * 13
        top = jnp.zeros_like(own)
        tree_path = jnp.stack([labels[own], labels[parent], labels[top]], axis=-1)
        return (tree_path, place.astype(jnp.int32))
    paths, places = jax.vmap(one_tree)(tree_keys, jnp.arange(TREES, dtype=jnp.int32))
    return (paths.reshape(MICRO, TOK_MB, 3), places.reshape(MICRO, TOK_MB))


def draw_path(key, part):
    return tree_tables(key)[0]


def draw_positions(key, part):
    return tree_tables(key)[1]


def block_scale(rng, extent, cuts, smallest, largest):
    factor_of = 1.0
    for axis_at, blocks in cuts:
        steps = jax.random.uniform(jax.random.fold_in(jax.random.fold_in(rng, 6), axis_at), (blocks,), jnp.float32, smallest / len(cuts), largest / len(cuts))
        factor_of = factor_of * jnp.repeat(jnp.exp(steps), extent[axis_at] // blocks).reshape((-1,) + (1,) * (len(extent) - 1 - axis_at))
    return factor_of


def bell_draw(rng, extent, spread, bound, cuts=(), kind=jnp.bfloat16):
    level = block_scale(rng, extent, cuts, -0.22, 0.18) if cuts else 1.0
    values = jax.random.normal(rng, extent, jnp.float32) * spread * level
    return jnp.minimum(jnp.maximum(values, -bound), bound).astype(kind)


def setup_inputs(seed: int = 0) -> dict:
    key_of = jax.random.split(jax.random.key(seed), 14)
    return {
        "tokens": bell_draw(key_of[0], (MICRO, TOK_MB, D), 1.0, 6.0, ((1, 16), (2, 2))),
        "out_grad": bell_draw(key_of[1], (MICRO, TOK_MB, D), 1.0, 6.0, ((1, 16), (2, 2))),
        "path": draw_path(jax.random.fold_in(key_of[13], 71), 0),
        "positions": draw_positions(jax.random.fold_in(key_of[13], 71), 0),
        "w_query": bell_draw(key_of[4], (D, HEADS * HEAD), D ** -0.5, 0.125, ((0, 2), (1, 4))),
        "w_key": bell_draw(key_of[5], (D, KV_HEADS * HEAD), D ** -0.5, 0.125, ((0, 2), (1, 4))),
        "w_value": bell_draw(key_of[6], (D, KV_HEADS * HEAD), D ** -0.5, 0.125, ((0, 2), (1, 4))),
        "w_out": bell_draw(key_of[7], (HEADS * HEAD, D), (max(D // 128, 1)) ** -0.5, 1.5, ((0, 4), (1, 2))),
        "w_gate": bell_draw(key_of[8], (D, FF), D ** -0.5, 0.125, ((0, 2), (1, 4))),
        "w_up": bell_draw(key_of[9], (D, FF), D ** -0.5, 0.125, ((0, 2), (1, 4))),
        "w_down": bell_draw(key_of[10], (FF, D), FF ** -0.5, 0.0625, ((0, 4), (1, 2))),
        "gain_attn": jnp.clip(1.0 + 0.15 * jax.random.normal(key_of[11], (D,), jnp.float32), 0.25, 1.75),
        "gain_ffn": jnp.clip(1.0 + 0.15 * jax.random.normal(key_of[12], (D,), jnp.float32), 0.25, 1.75),
    }


@jax.custom_vjp
def low(v):
    return lax.optimization_barrier(v.astype(jnp.bfloat16)).astype(jnp.float32)

@jax.custom_vjp
def low_back(v):
    return v

def low_keep(v):
    return (low(v), None)

def low_pass(kept, grad):
    return (grad,)

def back_keep(v):
    return (v, None)

def back_low(kept, grad):
    return (low(grad),)
low.defvjp(low_keep, low_pass)
low_back.defvjp(back_keep, back_low)
EPSILON = 1e-05
THETA = 1000000.0
HIGHEST = lax.Precision.HIGHEST

def matmul(left, right):
    return jnp.dot(left, right, precision=HIGHEST, preferred_element_type=jnp.float32)

def rope_tables(positions):
    half = HEAD // 2
    frequency = jnp.power(THETA, -2.0 * jnp.arange(half, dtype=jnp.float32) / HEAD)
    angles = positions.astype(jnp.float32)[:, None] * frequency[None, :]
    angles = jnp.concatenate([angles, angles], axis=1)
    return (jnp.cos(angles), jnp.sin(angles))

def rotate(values, cosine, sine):
    half = values.shape[-1] // 2
    turned = jnp.concatenate([-values[..., half:], values[..., :half]], axis=-1)
    return values * cosine[:, None, :] + turned * sine[:, None, :]

def rms_norm(values, gain):
    ratio = lax.rsqrt(lax.optimization_barrier(jnp.mean(values * values, axis=-1, keepdims=True)) + EPSILON)
    return values * ratio * gain

def tree_attention(operands):
    query, keys, values, path = operands
    length = query.shape[0]
    groups = query.reshape(length, KV_HEADS, HEADS // KV_HEADS, HEAD)
    scores = jnp.einsum('ikgd,jkd->kgij', groups, keys, precision=HIGHEST) * (1.0 / math.sqrt(HEAD))
    scores = low_back(scores)
    place = jnp.arange(length, dtype=jnp.int32)
    labels = path[:, 0]
    same_path = (labels[None, :] == path[:, 0:1]) | (labels[None, :] == path[:, 1:2]) | (labels[None, :] == path[:, 2:3])
    visible = same_path & (place[None, :] <= place[:, None])
    scores = jnp.where(visible[None, None], scores, -jnp.inf)
    weights = low(jax.nn.softmax(scores, axis=-1))
    mixed = jnp.einsum('kgij,jkd->ikgd', weights, values, precision=HIGHEST)
    return mixed.reshape(length, HEADS * HEAD)

def layer(inputs, w_query, w_key, w_value, w_out, w_gate, w_up, w_down, gain_attn, gain_ffn, cosine, sine, path):
    rows = inputs.shape[0]
    trees = rows // TREE_LEN
    normed = low(rms_norm(inputs, gain_attn))
    query = low_back(matmul(normed, w_query)).reshape(rows, HEADS, HEAD)
    keys = low_back(matmul(normed, w_key)).reshape(rows, KV_HEADS, HEAD)
    values = low(low_back(matmul(normed, w_value))).reshape(rows, KV_HEADS, HEAD)
    query = low(rotate(query, cosine, sine))
    keys = low(rotate(keys, cosine, sine))
    mixed = lax.map(jax.checkpoint(tree_attention), (query.reshape(trees, TREE_LEN, HEADS, HEAD), keys.reshape(trees, TREE_LEN, KV_HEADS, HEAD), values.reshape(trees, TREE_LEN, KV_HEADS, HEAD), path.reshape(trees, TREE_LEN, 3)))
    attn = low(low_back(mixed.reshape(rows, HEADS * HEAD)))
    middle = inputs + low_back(matmul(attn, w_out))
    normed_ffn = low(rms_norm(middle, gain_ffn))
    gate = low_back(matmul(normed_ffn, w_gate))
    upper = low_back(matmul(normed_ffn, w_up))
    hidden = low(jax.nn.silu(gate) * upper)
    return middle + matmul(hidden, w_down)

def reference(tokens, out_grad, path, positions, w_query, w_key, w_value, w_out, w_gate, w_up, w_down, gain_attn, gain_ffn):
    weights = tuple((w.astype(jnp.float32) for w in (w_query, w_key, w_value, w_out, w_gate, w_up, w_down)))
    weights = weights + (gain_attn.astype(jnp.float32), gain_ffn.astype(jnp.float32))

    def one_batch(carry, batch):
        block, cotangent, block_path, block_place = batch
        cosine, sine = rope_tables(block_place)

        def forward(inputs, *params):
            return layer(inputs, *params, cosine, sine, block_path)
        result, pull = jax.vjp(forward, block.astype(jnp.float32), *weights)
        grads = pull(cotangent.astype(jnp.float32))
        carry = tuple((total + part for total, part in zip(carry, grads[1:])))
        return (carry, (result.astype(jnp.bfloat16), grads[0].astype(jnp.bfloat16)))
    start = tuple((jnp.zeros(w.shape, jnp.float32) for w in weights))
    sums, (outputs, input_grads) = lax.scan(one_batch, start, (tokens, out_grad, path, positions))
    return (outputs, input_grads) + sums
```

```python
import functools
import math

import jax
import jax.numpy as jnp
from jax import lax
from jax.experimental import pallas as pl
from jax.experimental.pallas import tpu as pltpu
from jax.sharding import PartitionSpec as P

D = 2048
HEADS = 16
KV_HEADS = 8
HEAD = 128


EPSILON = 1e-05
THETA = 1000000.0


def contract_rows(left, right):
    return lax.dot_general(
        left, right, (((0,), (0,)), ((), ())), preferred_element_type=jnp.float32
    )


def contract_cols(left, right):
    return lax.dot_general(
        left, right, (((1,), (1,)), ((), ())), preferred_element_type=jnp.float32
    )


def rows_gather(values):
    return lax.all_gather(values, "row", axis=0, tiled=True)


def cols_gather(values):
    return lax.all_gather(values, "col", axis=0, tiled=True)


def cols_reduce(part_fn, rows):
    return lax.psum_scatter(
        part_fn(jnp.int32(0), rows * lax.axis_size("col")), "col", scatter_dimension=0, tiled=True
    )


def rows_reduce(part_fn, rows):
    return lax.psum_scatter(
        part_fn(jnp.int32(0), rows * lax.axis_size("row")).astype(jnp.bfloat16),
        "row",
        scatter_dimension=0,
        tiled=True,
    ).astype(jnp.float32)


def feature_sums(values):
    return lax.psum(jnp.sum(values, axis=1), "col")


def sliced_product(whole, weight, transpose):

    def part_fn(start, count):
        if transpose:
            return contract_cols(whole, weight)
        return jnp.dot(whole, weight, preferred_element_type=jnp.float32)

    return part_fn


def rope_tables(positions):
    half = HEAD // 2
    frequency = jnp.power(THETA, -2.0 * jnp.arange(half, dtype=jnp.float32) / HEAD)
    angles = positions.astype(jnp.float32)[:, None] * frequency[None, :]
    angles = jnp.concatenate([angles, angles], axis=1)
    return (jnp.cos(angles), jnp.sin(angles))


def rotate(values, cosine, sine):
    half = values.shape[-1] // 2
    turned = jnp.concatenate([-values[..., half:], values[..., :half]], axis=-1)
    return values * cosine[:, None, :] + turned * sine[:, None, :]


def rotate_back(grads, cosine, sine):
    half = grads.shape[-1] // 2
    scaled = grads * sine[:, None, :]
    turned = jnp.concatenate([scaled[..., half:], -scaled[..., :half]], axis=-1)
    return grads * cosine[:, None, :] + turned


def norm_forward(values, gain):
    ratio = lax.rsqrt(feature_sums(values * values) / D + EPSILON)[:, None]
    normed = values * ratio
    return (ratio, normed, (normed * gain).astype(jnp.bfloat16))


def norm_backward(grad, ratio, normed, gain):
    scaled = grad * gain
    inner = feature_sums(scaled * normed)[:, None] / D
    return (ratio * (scaled - normed * inner), jnp.sum(grad * normed, axis=0))


def body(
    tokens,
    out_grad,
    path,
    positions,
    w_query,
    w_key,
    w_value,
    w_out,
    w_gate,
    w_up,
    w_down,
    gain_attn,
    gain_ffn,
):
    query_width = w_query.shape[1]
    key_width = w_key.shape[1]
    hidden_width = w_gate.shape[1]
    local_heads = key_width // HEAD
    group = HEADS // KV_HEADS
    scale = 1.0 / math.sqrt(HEAD)
    block_rows = path.shape[1]
    local_rows = tokens.shape[1]
    query_rows = block_rows // lax.axis_size("col")
    first = lax.axis_index("col") * query_rows
    w_project = jnp.concatenate([w_query, w_key, w_value], axis=1)
    w_pair = jnp.concatenate([w_gate, w_up], axis=1)
    project_start = jnp.zeros(w_project.shape, jnp.float32)
    pair_start = jnp.zeros(w_pair.shape, jnp.float32)
    down_start = jnp.zeros(w_down.shape, jnp.float32)

    def micro_step(carry, batch):
        grad_project, grad_out, grad_pair, grad_down, grad_gain_attn, grad_gain_ffn = carry
        block, cotangent, block_path, block_place = batch
        inputs = block.astype(jnp.float32)
        cosine, sine = rope_tables(lax.dynamic_slice_in_dim(block_place, first, query_rows, 0))
        query_path = lax.dynamic_slice_in_dim(block_path, first, query_rows, 0)
        key_labels = block_path[:, 0]
        query_place = first + jnp.arange(query_rows, dtype=jnp.int32)
        key_place = jnp.arange(block_rows, dtype=jnp.int32)
        same_path = (
            (key_labels[None, :] == query_path[:, 0:1])
            | (key_labels[None, :] == query_path[:, 1:2])
            | (key_labels[None, :] == query_path[:, 2:3])
        )
        visible = same_path & (key_place[None, :] <= query_place[:, None])
        ratio_attn, normed_attn, input_attn = norm_forward(inputs, gain_attn)
        gathered_attn = rows_gather(input_attn)
        projected = cols_reduce(sliced_product(gathered_attn, w_project, False), query_rows)
        query = rotate(
            projected[:, :query_width].reshape(query_rows, -1, HEAD), cosine, sine
        ).astype(jnp.bfloat16)
        keys = rotate(
            projected[:, query_width : query_width + key_width].reshape(query_rows, -1, HEAD),
            cosine,
            sine,
        ).astype(jnp.bfloat16)
        values = projected[:, query_width + key_width :].astype(jnp.bfloat16)
        keys_all, values_all = (
            lax.all_gather(keys.reshape(query_rows, key_width), "col", axis=0, tiled=True),
            lax.all_gather(values, "col", axis=0, tiled=True),
        )
        query_groups = query.reshape(query_rows, local_heads, group, HEAD)
        key_heads = keys_all.reshape(block_rows, local_heads, HEAD)
        value_heads = values_all.reshape(block_rows, local_heads, HEAD)
        scores = (
            jnp.einsum(
                "ikgd,jkd->kgij", query_groups, key_heads, preferred_element_type=jnp.float32
            )
            * scale
        )
        scores = jnp.where(visible[None, None], scores, -jnp.inf)
        weights = jax.nn.softmax(scores, axis=-1)
        weights_low = weights.astype(jnp.bfloat16)
        mixed = jnp.einsum(
            "kgij,jkd->ikgd", weights_low, value_heads, preferred_element_type=jnp.float32
        )
        attn_low = mixed.reshape(query_rows, query_width).astype(jnp.bfloat16)
        attn_all = cols_gather(attn_low)
        branch_attn = rows_reduce(sliced_product(attn_all, w_out, False), local_rows)
        middle = inputs + branch_attn
        ratio_ffn, normed_ffn, input_ffn = norm_forward(middle, gain_ffn)
        gathered_ffn = rows_gather(input_ffn)
        pair = cols_reduce(sliced_product(gathered_ffn, w_pair, False), query_rows)
        gate = pair[:, :hidden_width]
        upper = pair[:, hidden_width:]
        sigma = jax.nn.sigmoid(gate)
        silu_value = gate * sigma
        hidden = (silu_value * upper).astype(jnp.bfloat16)
        hidden_all = cols_gather(hidden)
        branch_ffn = rows_reduce(sliced_product(hidden_all, w_down, False), local_rows)
        output = (middle + branch_ffn).astype(jnp.bfloat16)
        cotangent_all = rows_gather(cotangent)
        hidden_grad = cols_reduce(sliced_product(cotangent_all, w_down, True), query_rows)
        grad_down = grad_down + contract_rows(hidden_all, cotangent_all)
        gate_grad = hidden_grad * upper * sigma * (1.0 + gate * (1.0 - sigma))
        upper_grad = hidden_grad * silu_value
        pair_grad = jnp.concatenate([gate_grad, upper_grad], axis=1).astype(jnp.bfloat16)
        pair_all = cols_gather(pair_grad)
        normed_ffn_grad = rows_reduce(sliced_product(pair_all, w_pair, True), local_rows)
        grad_pair = grad_pair + contract_rows(gathered_ffn, pair_all)
        middle_back, gain_ffn_step = norm_backward(normed_ffn_grad, ratio_ffn, normed_ffn, gain_ffn)
        middle_grad = cotangent.astype(jnp.float32) + middle_back
        middle_low = middle_grad.astype(jnp.bfloat16)
        middle_all = rows_gather(middle_low)
        attn_grad = cols_reduce(sliced_product(middle_all, w_out, True), query_rows).astype(
            jnp.bfloat16
        )
        grad_out = grad_out + contract_rows(attn_all, middle_all)
        attn_heads = attn_grad.reshape(query_rows, local_heads, group, HEAD)
        weight_grad = jnp.einsum(
            "ikgd,jkd->kgij", attn_heads, value_heads, preferred_element_type=jnp.float32
        )
        score_grad = (
            weights * (weight_grad - jnp.sum(weights * weight_grad, axis=-1, keepdims=True))
        ).astype(jnp.bfloat16)
        query_grad = (
            jnp.einsum("kgij,jkd->ikgd", score_grad, key_heads, preferred_element_type=jnp.float32)
            * scale
        )
        key_part = (
            jnp.einsum(
                "kgij,ikgd->jkd", score_grad, query_groups, preferred_element_type=jnp.float32
            )
            * scale
        )
        value_part = jnp.einsum(
            "kgij,ikgd->jkd", weights_low, attn_heads, preferred_element_type=jnp.float32
        )
        key_grad, value_grad = (
            lax.psum_scatter(
                key_part.reshape(block_rows, key_width).astype(jnp.bfloat16),
                "col",
                scatter_dimension=0,
                tiled=True,
            ).astype(jnp.float32),
            lax.psum_scatter(
                value_part.reshape(block_rows, key_width).astype(jnp.bfloat16),
                "col",
                scatter_dimension=0,
                tiled=True,
            ).astype(jnp.float32),
        )
        query_back = rotate_back(query_grad.reshape(query_rows, -1, HEAD), cosine, sine).reshape(
            query_rows, query_width
        )
        key_back = rotate_back(key_grad.reshape(query_rows, -1, HEAD), cosine, sine).reshape(
            query_rows, key_width
        )
        projected_grad = jnp.concatenate([query_back, key_back, value_grad], axis=1).astype(
            jnp.bfloat16
        )
        projected_all = cols_gather(projected_grad)
        normed_attn_grad = rows_reduce(sliced_product(projected_all, w_project, True), local_rows)
        grad_project = grad_project + contract_rows(gathered_attn, projected_all)
        input_back, gain_attn_step = norm_backward(
            normed_attn_grad, ratio_attn, normed_attn, gain_attn
        )
        input_grad = (middle_grad + input_back).astype(jnp.bfloat16)
        carry = (
            grad_project,
            grad_out,
            grad_pair,
            grad_down,
            grad_gain_attn + gain_attn_step,
            grad_gain_ffn + gain_ffn_step,
        )
        return (carry, (output, input_grad))

    start = (
        project_start,
        jnp.zeros(w_out.shape, jnp.float32),
        pair_start,
        down_start,
        jnp.zeros(gain_attn.shape, jnp.float32),
        jnp.zeros(gain_ffn.shape, jnp.float32),
    )
    sums, (outputs, input_grads) = lax.scan(micro_step, start, (tokens, out_grad, path, positions))
    grad_project, grad_out, grad_pair, grad_down, grad_gain_attn, grad_gain_ffn = sums
    grad_project, grad_out, grad_pair, grad_down = (
        lax.psum(grad_project.astype(jnp.bfloat16), "dp").astype(jnp.float32),
        lax.psum(grad_out.astype(jnp.bfloat16), "dp").astype(jnp.float32),
        lax.psum(grad_pair.astype(jnp.bfloat16), "dp").astype(jnp.float32),
        lax.psum(grad_down.astype(jnp.bfloat16), "dp").astype(jnp.float32),
    )
    grad_gain_attn, grad_gain_ffn = lax.psum((grad_gain_attn, grad_gain_ffn), ("dp", "row"))
    query_part = grad_project[:, :query_width]
    key_part_grad = grad_project[:, query_width : query_width + key_width]
    value_part_grad = grad_project[:, query_width + key_width :]
    return (
        outputs,
        input_grads,
        query_part,
        key_part_grad,
        value_part_grad,
        grad_out,
        grad_pair[:, :hidden_width],
        grad_pair[:, hidden_width:],
        grad_down,
        grad_gain_attn,
        grad_gain_ffn,
    )


CORE_SWAP = [(0, 1), (1, 0), (2, 3), (3, 2)]
X_SWAP = [(0, 2), (2, 0), (1, 3), (3, 1)]
COL_SWAP = [(0, 1), (1, 0)]
LOG2E = 1.4426950408889634
TRUNK = 1024
LEAF_BEGIN = TRUNK + 4 * 128
VMEM_LIMIT = 58 * 1024 * 1024
NT = (((1,), (1,)), ((), ()))
TN = (((0,), (0,)), ((), ()))
NN = (((1,), (0,)), ((), ()))


def swap_core(a):
    return lax.ppermute(a, "dp", CORE_SWAP)


def swap_x(a):
    return lax.ppermute(a, "dp", X_SWAP)


def swap_col(a):
    return lax.ppermute(a, "col", COL_SWAP)


def mxu(a, b, dims):
    return lax.dot_general(a, b, dims, preferred_element_type=jnp.float32)


def low(a):
    return a.astype(jnp.bfloat16)


def wide(a):
    return a.astype(jnp.float32)


def rows_call(fn, block, row_ins, full_ins, outs, flops, name, scratch=()):
    rows = row_ins[0].shape[0]
    in_specs = [pl.BlockSpec((block, a.shape[1]), lambda i: (i, 0)) for a in row_ins]
    for a in full_ins:
        in_specs.append(
            pl.BlockSpec(
                a.shape, lambda i, nd=a.ndim: (0,) * nd, pipeline_mode=pl.Buffered(1)
            )
        )
    moved = sum(a.size * a.dtype.itemsize for a in (*row_ins, *full_ins))
    moved += sum(rows * w * jnp.dtype(dt).itemsize for w, dt in outs)
    return pl.pallas_call(
        fn,
        grid=(rows // block,),
        in_specs=in_specs,
        out_specs=[pl.BlockSpec((block, w), lambda i: (i, 0)) for w, _ in outs],
        out_shape=[jax.ShapeDtypeStruct((rows, w), dt) for w, dt in outs],
        scratch_shapes=list(scratch),
        compiler_params=pltpu.CompilerParams(vmem_limit_bytes=VMEM_LIMIT),
        cost_estimate=pl.CostEstimate(flops=flops, bytes_accessed=moved, transcendentals=0),
        name=name,
    )(*row_ins, *full_ins)


def turn(u, cosine, sine_signed):
    return u * cosine + pltpu.roll(u, HEAD // 2, 1) * sine_signed


def turn_back(u, cosine, sine_signed):
    return u * cosine - pltpu.roll(u, HEAD // 2, 1) * sine_signed


def project_kernel(x0, x1, x2, x3, cos_ref, sin_ref, gain_ref, w_ref, xn_ref, qkv_ref, r_ref):
    pieces = [wide(r[...]) for r in (x0, x1, x2, x3)]
    width = pieces[0].shape[1]
    total = sum(jnp.sum(p * p, axis=1, keepdims=True) for p in pieces)
    ratio = lax.rsqrt(total / (4 * width) + EPSILON)
    r_ref[...] = ratio
    for i, p in enumerate(pieces):
        cols = slice(i * width, (i + 1) * width)
        xn_ref[:, cols] = low(p * ratio * gain_ref[:, cols])
    normed = xn_ref[...]
    cosine = cos_ref[...]
    sine = sin_ref[...]
    span = w_ref.shape[2]
    heads = span // HEAD
    for g in range(w_ref.shape[0]):
        acc = mxu(normed, w_ref[g], NN)
        for h in range(heads):
            u = acc[:, h * HEAD : (h + 1) * HEAD]
            if h < heads - 1:
                u = turn(u, cosine, sine)
            at = g * span + h * HEAD
            qkv_ref[:, at : at + HEAD] = low(u)


def segments_of(kind, trunk, leaf_begin, block):
    if kind == "branch":
        return [(0, trunk, None), (None, block, "own")]
    if kind == "leaf":
        return [(0, trunk, None), (trunk, leaf_begin - trunk, "parent"), (None, 2 * block, "own")]
    return [(0, kind, "causal")]


def attention_blocks(qb, block, trunk, leaf_begin, run):
    half = trunk // 2

    @pl.when(qb < half // block)
    def _():
        run(half, 0)

    @pl.when((qb >= half // block) & (qb < trunk // block))
    def _():
        run(trunk, 0)

    @pl.when((qb >= trunk // block) & (qb < leaf_begin // block))
    def _():
        run("branch", pl.multiple_of(qb * block, block))

    @pl.when(qb >= leaf_begin // block)
    def _():
        run("leaf", pl.multiple_of(qb * block - block, block))


def key_rows(start, window, length):
    if start is None:
        return pl.ds(window, length)
    return pl.ds(start, length)


def score_segment(s, start, window, length, mask, qb, block, lab_ref, own_row, parent_row):
    if mask is None:
        return s
    rows = s.shape[0]
    cols = s.shape[1]
    if mask == "parent":
        return jnp.where(lab_ref[key_rows(start, window, length), :] == parent_row, s, -jnp.inf)
    base = window if start is None else start
    key_at = base + lax.broadcasted_iota(jnp.int32, (rows, 1), 0)
    lane = lax.broadcasted_iota(jnp.int32, (1, cols), 1)
    query_at = qb * block + jnp.where(lane >= block, lane - block, lane)
    seen = key_at <= query_at
    if mask == "own":
        seen = seen & (lab_ref[key_rows(start, window, length), :] == own_row)
    return jnp.where(seen, s, -jnp.inf)


def attend_kernel(trunk, leaf_begin, block, q_ref, k_ref, v_ref, lab_ref, row_ref, o_ref, lse_ref, vt_ref):
    qb = pl.program_id(1)
    factor = LOG2E / math.sqrt(HEAD)

    @pl.when(qb == 0)
    def _():
        vt_ref[...] = v_ref[...].T

    queries = jnp.concatenate([q_ref[:, :HEAD], q_ref[:, HEAD:]], axis=0)
    own = row_ref[0:1, :]
    parent = row_ref[1:2, :]
    own_row = jnp.concatenate([own, own], axis=1)
    parent_row = jnp.concatenate([parent, parent], axis=1)

    def run(kind, window):
        scores = []
        segs = segments_of(kind, trunk, leaf_begin, block)
        for start, length, mask in segs:
            s = mxu(k_ref[key_rows(start, window, length), :], queries, NT)
            s = score_segment(
                s, start, window, length, mask, qb, block, lab_ref, own_row, parent_row
            )
            scores.append(s)
        top = scores[0].max(axis=0, keepdims=True)
        for s in scores[1:]:
            top = jnp.maximum(top, s.max(axis=0, keepdims=True))
        total = jnp.zeros_like(top)
        mixed = jnp.zeros((HEAD, 2 * block), jnp.float32)
        shift = top * factor
        for (start, length, mask), s in zip(segs, scores):
            p = jnp.exp2(s * factor - shift)
            total = total + p.sum(axis=0, keepdims=True)
            mixed = mixed + mxu(vt_ref[:, key_rows(start, window, length)], low(p), NN)
        lse_ref[...] = shift + jnp.log2(total)
        mixed = mixed / total
        o_ref[:, :HEAD] = low(mixed[:, :block].T)
        o_ref[:, HEAD:] = low(mixed[:, block:].T)

    attention_blocks(qb, block, trunk, leaf_begin, run)


def attend_back_kernel(
    trunk, leaf_begin, block, blocks, q_ref, k_ref, v_ref, o_ref, do_ref, lab_ref, row_ref, lse_ref,
    cos_ref, sin_ref, out_ref, kt_ref, dk_ref, dv_ref,
):
    qb = pl.program_id(1)
    scale = 1.0 / math.sqrt(HEAD)
    factor = LOG2E * scale

    @pl.when(qb == 0)
    def _():
        kt_ref[...] = k_ref[...].T
        dk_ref[...] = jnp.zeros_like(dk_ref)
        dv_ref[...] = jnp.zeros_like(dv_ref)

    queries = jnp.concatenate([q_ref[:, :HEAD], q_ref[:, HEAD:]], axis=0)
    grads = jnp.concatenate([do_ref[:, :HEAD], do_ref[:, HEAD:]], axis=0)
    outs = jnp.concatenate([o_ref[:, :HEAD], o_ref[:, HEAD:]], axis=0)
    inner = (wide(grads) * wide(outs)).T.sum(axis=0, keepdims=True)
    lse = lse_ref[...]
    own = row_ref[0:1, :]
    parent = row_ref[1:2, :]
    own_row = jnp.concatenate([own, own], axis=1)
    parent_row = jnp.concatenate([parent, parent], axis=1)
    q_rows = pl.ds(pl.multiple_of(qb * block, block), block)

    def run(kind, window):
        dq = jnp.zeros((HEAD, 2 * block), jnp.float32)
        for start, length, mask in segments_of(kind, trunk, leaf_begin, block):
            keys = key_rows(start, window, length)
            s = mxu(k_ref[keys, :], queries, NT)
            s = score_segment(
                s, start, window, length, mask, qb, block, lab_ref, own_row, parent_row
            )
            p = jnp.exp2(s * factor - lse)
            dp = mxu(v_ref[keys, :], grads, NT)
            ds = low(p * (dp - inner))
            dv_ref[keys, :] += mxu(low(p), grads, NN)
            dk_ref[keys, :] += mxu(ds, queries, NN)
            dq = dq + mxu(kt_ref[:, keys], ds, NN)
        dq = dq * scale
        cosine = cos_ref[q_rows, :]
        sine = sin_ref[q_rows, :]
        for h in range(2):
            part = dq[:, h * block : (h + 1) * block].T
            out_ref[q_rows, h * HEAD : (h + 1) * HEAD] = low(turn_back(part, cosine, sine))

    attention_blocks(qb, block, trunk, leaf_begin, run)

    @pl.when(qb == blocks - 1)
    def _():
        dk = dk_ref[...] * scale
        out_ref[:, 2 * HEAD : 3 * HEAD] = low(turn_back(dk, cos_ref[...], sin_ref[...]))
        out_ref[:, 3 * HEAD :] = low(dv_ref[...])


def attention_specs(rows, block, groups):
    q_spec = pl.BlockSpec((block, 2 * HEAD), lambda g, i: (i, 2 * g))
    k_spec = pl.BlockSpec((rows, HEAD), lambda g, i: (0, 4 * g + 2))
    v_spec = pl.BlockSpec((rows, HEAD), lambda g, i: (0, 4 * g + 3))
    lab_spec = pl.BlockSpec((rows, 1), lambda g, i: (0, 0))
    row_spec = pl.BlockSpec((8, block), lambda g, i: (0, i))
    o_spec = pl.BlockSpec((block, 2 * HEAD), lambda g, i: (i, g))
    lse_spec = pl.BlockSpec((None, None, 1, 2 * block), lambda g, i: (g, i, 0, 0))
    return q_spec, k_spec, v_spec, lab_spec, row_spec, o_spec, lse_spec


def attend(qkv, label_col, label_rows, trunk, leaf_begin, block):
    rows = qkv.shape[0]
    groups = qkv.shape[1] // (4 * HEAD)
    blocks = rows // block
    q_spec, k_spec, v_spec, lab_spec, row_spec, o_spec, lse_spec = attention_specs(rows, block, groups)
    pairs = groups * 2 * rows * rows // 2
    return pl.pallas_call(
        functools.partial(attend_kernel, trunk, leaf_begin, block),
        grid=(groups, blocks),
        in_specs=[q_spec, k_spec, v_spec, lab_spec, row_spec],
        out_specs=[o_spec, lse_spec],
        out_shape=[
            jax.ShapeDtypeStruct((rows, groups * 2 * HEAD), jnp.bfloat16),
            jax.ShapeDtypeStruct((groups, blocks, 1, 2 * block), jnp.float32),
        ],
        scratch_shapes=[pltpu.VMEM((HEAD, rows), jnp.bfloat16)],
        compiler_params=pltpu.CompilerParams(vmem_limit_bytes=VMEM_LIMIT),
        cost_estimate=pl.CostEstimate(
            flops=4 * 4 * pairs * HEAD, bytes_accessed=20 * rows * HEAD * 2, transcendentals=pairs
        ),
        name="attend",
    )(qkv, qkv, qkv, label_col, label_rows)


def attend_back(qkv, attn, attn_grad, label_col, label_rows, lse, cosine, sine, trunk, leaf_begin, block):
    rows = qkv.shape[0]
    groups = qkv.shape[1] // (4 * HEAD)
    blocks = rows // block
    q_spec, k_spec, v_spec, lab_spec, row_spec, o_spec, lse_spec = attention_specs(rows, block, groups)
    table = pl.BlockSpec((rows, HEAD), lambda g, i: (0, 0))
    pairs = groups * 2 * rows * rows // 2
    return pl.pallas_call(
        functools.partial(attend_back_kernel, trunk, leaf_begin, block, blocks),
        grid=(groups, blocks),
        in_specs=[q_spec, k_spec, v_spec, o_spec, o_spec, lab_spec, row_spec, lse_spec, table, table],
        out_specs=pl.BlockSpec((rows, 4 * HEAD), lambda g, i: (0, g)),
        out_shape=jax.ShapeDtypeStruct((rows, groups * 4 * HEAD), jnp.bfloat16),
        scratch_shapes=[
            pltpu.VMEM((HEAD, rows), jnp.bfloat16),
            pltpu.VMEM((rows, HEAD), jnp.float32),
            pltpu.VMEM((rows, HEAD), jnp.float32),
        ],
        compiler_params=pltpu.CompilerParams(vmem_limit_bytes=VMEM_LIMIT),
        cost_estimate=pl.CostEstimate(
            flops=10 * 4 * pairs * HEAD, bytes_accessed=40 * rows * HEAD * 2, transcendentals=pairs
        ),
        name="attend_back",
    )(qkv, qkv, qkv, attn, attn_grad, label_col, label_rows, lse, cosine, sine)


def halves_out(acc, own_ref, send_ref):
    half = own_ref.shape[1]
    own_ref[...] = low(acc[:, :half])
    send_ref[...] = low(acc[:, half:])


def out_kernel(a_ref, w_ref, own_ref, send_ref):
    halves_out(mxu(a_ref[...], w_ref[...], NN), own_ref, send_ref)


def two_out_kernel(a_ref, b_ref, wa_ref, wb_ref, own_ref, send_ref):
    acc = mxu(a_ref[...], wa_ref[...], NN) + mxu(b_ref[...], wb_ref[...], NN)
    halves_out(acc, own_ref, send_ref)


def project_back_kernel(d_ref, w_ref, own_ref, send_ref):
    groups = w_ref.shape[0]
    span = w_ref.shape[2]
    acc = sum(mxu(d_ref[:, g * span : (g + 1) * span], w_ref[g], NT) for g in range(groups))
    halves_out(acc, own_ref, send_ref)


def attn_grad_kernel(h0, h1, h2, h3, w_ref, out_ref):
    width = h0.shape[1]
    acc = sum(
        mxu(h[...], w_ref[:, i * width : (i + 1) * width], NT)
        for i, h in enumerate((h0, h1, h2, h3))
    )
    out_ref[...] = low(acc)


def hidden_kernel(
    x0, x1, x2, x3, g0, g1, g2, g3, wa_ref, wb_ref, da_ref, db_ref, ha_ref, hb_ref, pa_ref, pb_ref,
    xs_ref, gs_ref,
):
    width = x0.shape[1]
    for i, (x, g) in enumerate(zip((x0, x1, x2, x3), (g0, g1, g2, g3))):
        xs_ref[:, i * width : (i + 1) * width] = x[...]
        gs_ref[:, i * width : (i + 1) * width] = g[...]
    normed = xs_ref[...]
    grads = gs_ref[...]
    for w_ref, d_ref, h_ref, p_ref in ((wa_ref, da_ref, ha_ref, pa_ref), (wb_ref, db_ref, hb_ref, pb_ref)):
        parts = w_ref.shape[0]
        unit = w_ref.shape[1] // 2
        for z in range(parts):
            pair = mxu(normed, w_ref[z], NT)
            hidden_grad = mxu(grads, d_ref[z], NT)
            gate = pair[:, :unit]
            upper = pair[:, unit:]
            sigma = jax.nn.sigmoid(gate)
            silu_value = gate * sigma
            h_ref[:, z * unit : (z + 1) * unit] = low(silu_value * upper)
            at = 2 * z * unit
            p_ref[:, at : at + unit] = low(
                hidden_grad * upper * sigma * (1.0 + gate * (1.0 - sigma))
            )
            p_ref[:, at + unit : at + 2 * unit] = low(hidden_grad * silu_value)


def weight_grad_kernel(count, joined, *refs):
    a_ref = refs[0]
    b_refs = refs[1 : 1 + count]
    o_refs = refs[1 + count :]
    left = a_ref[...].T
    for i, b in enumerate(b_refs):
        width = b.shape[1]
        acc = low(mxu(left, b[...], NN))
        if joined:
            o_refs[0][:, i * width : (i + 1) * width] = acc
        else:
            o_refs[i][...] = acc


def weight_grad(a, bs, joined, block, name):
    rows, m = a.shape
    n = sum(b.shape[1] for b in bs)
    widths = [n] if joined else [b.shape[1] for b in bs]
    in_specs = [pl.BlockSpec((rows, block), lambda i: (0, i))]
    for b in bs:
        in_specs.append(
            pl.BlockSpec(b.shape, lambda i: (0, 0), pipeline_mode=pl.Buffered(1))
        )
    return pl.pallas_call(
        functools.partial(weight_grad_kernel, len(bs), joined),
        grid=(m // block,),
        in_specs=in_specs,
        out_specs=[pl.BlockSpec((block, w), lambda i: (i, 0)) for w in widths],
        out_shape=[jax.ShapeDtypeStruct((m, w), jnp.bfloat16) for w in widths],
        compiler_params=pltpu.CompilerParams(vmem_limit_bytes=VMEM_LIMIT),
        cost_estimate=pl.CostEstimate(
            flops=2 * rows * m * n, bytes_accessed=2 * (rows * m + rows * n + m * n), transcendentals=0
        ),
        name=name,
    )(a, *bs)


def take(a, index, axis):
    return lax.dynamic_index_in_dim(a, index, axis, keepdims=False)


def in_order(index, mine, other, axis=0):
    first = jnp.where(index == 0, mine, other)
    second = jnp.where(index == 0, other, mine)
    return jnp.stack([first, second], axis=axis)


def spread(a):
    b = swap_col(a)
    return [a, b, swap_core(a), swap_core(b)]


def collect(own, send):
    quarter = own.shape[1] // 2
    got = swap_core(send)
    outgoing = low(wide(own[:, quarter:]) + wide(got[:, quarter:]))
    back = swap_col(outgoing)
    return wide(own[:, :quarter]) + wide(got[:, :quarter]) + wide(back)


def small_sum(v):
    v = v + swap_core(v)
    return v + swap_col(v)


def tree_body(
    tokens,
    out_grad,
    path,
    positions,
    w_query,
    w_key,
    w_value,
    w_out,
    w_gate,
    w_up,
    w_down,
    gain_attn,
    gain_ffn,
):
    dp = lax.axis_index("dp")
    x = dp // 2
    c = lax.rem(dp, 2)
    z = lax.axis_index("row")
    y = lax.axis_index("col")
    micro, local_rows, half = tokens.shape
    quarter = half // 2
    rows = path.shape[1]
    planes = lax.axis_size("row")
    features = 2 * half
    block = 256
    trunk = TRUNK
    leaf_begin = LEAF_BEGIN

    def to_tree(a):
        parts = a.reshape(micro, local_rows, 2, quarter)
        mine = take(parts, c, 2)
        other = swap_core(take(parts, 1 - c, 2))
        trees = in_order(c, mine, other).reshape(planes * local_rows, quarter)
        return lax.all_to_all(trees, "row", 0, 0, tiled=True)

    def from_tree(a):
        trees = lax.all_to_all(a, "row", 0, 0, tiled=True)
        trees = trees.reshape(2, micro, local_rows, quarter)
        mine = take(trees, c, 0)
        other = swap_core(take(trees, 1 - c, 0))
        return in_order(c, mine, other, 2).reshape(micro, local_rows, half)

    def of_tree(a):
        both = in_order(c, a, swap_core(a))
        return take(both.reshape((2 * micro,) + a.shape[1:]), z, 0)

    tree_path = of_tree(path)
    tree_place = of_tree(positions)
    cosine, sine = rope_tables(tree_place)
    sign = jnp.where(jnp.arange(HEAD) < HEAD // 2, -1.0, 1.0).astype(jnp.float32)
    sine = sine * sign[None, :]
    label_col = tree_path[:, 0:1]
    label_rows = jnp.pad(tree_path.T, ((0, 5), (0, 0)))

    block_in = to_tree(tokens)

    key_width = w_key.shape[1]
    groups = key_width // HEAD
    share = quarter // 2
    first_row = c * quarter + x * share

    def group_cols(g):
        return jnp.concatenate(
            [
                lax.dynamic_slice_in_dim(w_query, g * 2 * HEAD, 2 * HEAD, 1),
                lax.dynamic_slice_in_dim(w_key, g * HEAD, HEAD, 1),
                lax.dynamic_slice_in_dim(w_value, g * HEAD, HEAD, 1),
            ],
            axis=1,
        )

    def own_rows(a):
        return lax.dynamic_slice_in_dim(a, first_row, share, 0)

    def spread_attn(kept, sent):
        piece = jnp.stack([kept, swap_col(sent)])
        mine = lax.all_gather(piece, "row", axis=0)
        both = in_order(x, mine, swap_x(mine), 2)
        pairs = both.reshape((2, planes // 2) + both.shape[1:])
        own = take(pairs, c, 0)
        other = swap_core(take(pairs, 1 - c, 0))
        return jnp.stack([own, other], axis=1)

    w_project = spread_attn(own_rows(group_cols(y)), own_rows(group_cols(1 - y)))
    w_project = w_project.reshape(groups, features, 4 * HEAD)

    def head_rows(g):
        at = (g * 2 + x) * HEAD
        return lax.dynamic_slice(w_out, (at, c * quarter), (HEAD, quarter))

    w_mix = spread_attn(head_rows(y), head_rows(1 - y))
    w_mix = jnp.transpose(w_mix, (0, 3, 4, 1, 2, 5)).reshape(groups * 2 * HEAD, features)

    hidden_width = w_gate.shape[1]
    unit = hidden_width // 8

    def unit_at(j):
        return (2 * j + c) * 2 * unit + x * unit

    def by_core(a):
        parts = a.reshape(unit, 2, quarter)
        return jnp.where(c == 0, parts, parts[:, ::-1])

    def hidden_pieces(j):
        at = unit_at(j)
        gate = lax.dynamic_slice_in_dim(w_gate, at, unit, 1).T
        upper = lax.dynamic_slice_in_dim(w_up, at, unit, 1).T
        return jnp.stack([by_core(gate), by_core(upper)]), by_core(
            lax.dynamic_slice_in_dim(w_down, at, unit, 0)
        )

    pair_kept, down_kept = hidden_pieces(y)
    pair_sent, down_sent = hidden_pieces(1 - y)
    pair_piece = jnp.stack([pair_kept, swap_col(pair_sent)], axis=3).reshape(2 * unit, features)
    down_piece = jnp.stack([down_kept, swap_col(down_sent)], axis=2).reshape(unit, features)
    pair_mine = lax.all_gather(pair_piece, "row", axis=0)
    down_mine = lax.all_gather(down_piece, "row", axis=0)
    pair_other = swap_x(pair_mine)
    down_other = swap_x(down_mine)

    def gain_order(gain):
        kept = gain.reshape(2, quarter)
        both = jnp.stack([kept, swap_col(kept)], axis=1)
        both = jnp.where(c == 0, both, both[::-1])
        return both.reshape(1, features)

    gain_attn_all = gain_order(gain_attn)
    gain_attn_own = gain_attn_all[:, :quarter]
    gain_ffn_own = lax.dynamic_slice_in_dim(gain_ffn, c * quarter, quarter, 0)[None, :]

    pieces = spread(block_in)
    normed_attn, qkv, ratio_attn = rows_call(
        project_kernel,
        block,
        [*pieces, cosine, sine],
        [gain_attn_all, w_project],
        [(features, jnp.bfloat16), (groups * 4 * HEAD, jnp.bfloat16), (1, jnp.float32)],
        2 * rows * features * groups * 4 * HEAD,
        "project",
    )
    attn, lse = attend(qkv, label_col, label_rows, trunk, leaf_begin, block)
    own, send = rows_call(
        out_kernel,
        2 * block,
        [attn],
        [w_mix],
        [(half, jnp.bfloat16), (half, jnp.bfloat16)],
        2 * rows * features * groups * 2 * HEAD,
        "mix",
    )
    middle = wide(block_in) + collect(own, send)
    square = small_sum(jnp.sum(middle * middle, axis=1))
    ratio_ffn = lax.rsqrt(square / features + EPSILON)[:, None]
    normed_ffn = middle * ratio_ffn
    ffn_pieces = spread(low(normed_ffn * gain_ffn_own))

    cotangent = to_tree(out_grad)
    grad_pieces = spread(cotangent)
    hid_mine, hid_other, pair_grad_mine, pair_grad_other = rows_call(
        hidden_kernel,
        block,
        [*ffn_pieces, *grad_pieces],
        [pair_mine, pair_other, down_mine, down_other],
        [
            (planes * unit, jnp.bfloat16),
            (planes * unit, jnp.bfloat16),
            (2 * planes * unit, jnp.bfloat16),
            (2 * planes * unit, jnp.bfloat16),
        ],
        2 * rows * features * 6 * planes * unit,
        "hidden",
        [pltpu.VMEM((block, features), jnp.bfloat16)] * 2,
    )
    down_mine = down_mine.reshape(planes * unit, features)
    down_other = down_other.reshape(planes * unit, features)
    pair_mine = pair_mine.reshape(2 * planes * unit, features)
    pair_other = pair_other.reshape(2 * planes * unit, features)

    own, send = rows_call(
        two_out_kernel,
        2 * block,
        [pair_grad_mine, pair_grad_other],
        [pair_mine, pair_other],
        [(half, jnp.bfloat16), (half, jnp.bfloat16)],
        2 * rows * features * 4 * planes * unit,
        "pair_back",
    )
    normed_ffn_grad = collect(own, send)

    def to_z(grad_mine, grad_other):
        total = low(wide(grad_mine) + wide(swap_x(grad_other)))
        return lax.psum_scatter(total, "row", scatter_dimension=0, tiled=True)

    down_grad_other = weight_grad(hid_other, grad_pieces, True, 2 * block, "down_grad_other")[0]
    down_grad_mine = weight_grad(hid_mine, grad_pieces, True, 2 * block, "down_grad_mine")[0]
    down_sum = to_z(down_grad_mine, down_grad_other)
    pair_w_other = weight_grad(pair_grad_other, ffn_pieces, True, 2 * block, "pair_grad_other")[0]
    pair_w_mine = weight_grad(pair_grad_mine, ffn_pieces, True, 2 * block, "pair_grad_mine")[0]
    pair_sum = to_z(pair_w_mine, pair_w_other)

    own, send = rows_call(
        two_out_kernel,
        2 * block,
        [hid_mine, hid_other],
        [down_mine, down_other],
        [(half, jnp.bfloat16), (half, jnp.bfloat16)],
        2 * rows * features * 2 * planes * unit,
        "down",
    )
    output = from_tree(low(middle + collect(own, send)))

    def norm_back(grad, ratio, normed, gain):
        scaled = grad * gain
        inner = small_sum(jnp.sum(scaled * normed, axis=1))[:, None] / features
        return ratio * (scaled - normed * inner), jnp.sum(grad * normed, axis=0)

    middle_back, gain_ffn_part = norm_back(normed_ffn_grad, ratio_ffn, normed_ffn, gain_ffn_own)
    middle_grad = wide(cotangent) + middle_back
    middle_pieces = spread(low(middle_grad))
    attn_grad = rows_call(
        attn_grad_kernel,
        2 * block,
        middle_pieces,
        [w_mix],
        [(groups * 2 * HEAD, jnp.bfloat16)],
        2 * rows * features * groups * 2 * HEAD,
        "attn_grad",
    )[0]
    mix_grad = weight_grad(attn, middle_pieces, True, groups * 2 * HEAD, "mix_grad")[0]
    qkv_grad = attend_back(
        qkv, attn, attn_grad, label_col, label_rows, lse, cosine, sine, trunk, leaf_begin, block
    )
    own, send = rows_call(
        project_back_kernel,
        2 * block,
        [qkv_grad],
        [w_project],
        [(half, jnp.bfloat16), (half, jnp.bfloat16)],
        2 * rows * features * groups * 4 * HEAD,
        "project_back",
    )
    normed_attn_grad = collect(own, send)
    project_grad = weight_grad(normed_attn, [qkv_grad], True, 2 * block, "project_grad")[0]
    normed_attn_own = wide(block_in) * ratio_attn
    input_back, gain_attn_part = norm_back(
        normed_attn_grad, ratio_attn, normed_attn_own, gain_attn_own
    )
    input_grad = from_tree(low(middle_grad + input_back))

    def ffn_home(total):
        parts = total.reshape(-1, unit, 2, 2, quarter)
        cols = in_order(y, parts[:, :, :, 0], swap_col(parts[:, :, :, 1]))
        both = in_order(x, cols, swap_x(cols))
        both = jnp.where(c == 0, both, both[:, :, :, :, ::-1])
        whole = in_order(c, both, swap_core(both))
        whole = jnp.transpose(whole, (3, 2, 0, 1, 4, 5, 6))
        return wide(whole.reshape(-1, 8 * unit, half))

    down_out = ffn_home(down_sum)[0]
    pair_out = ffn_home(pair_sum)
    gate_out = pair_out[0].T
    up_out = pair_out[1].T

    def attn_home(parts):
        kept = take(parts, x, 3)
        total = low(wide(kept) + wide(swap_x(take(parts, 1 - x, 3))))
        mine = total[:, 0]
        other = swap_core(total[:, 1])
        planes_all = in_order(c, mine, other).reshape((planes,) + mine.shape[1:])
        summed = lax.psum_scatter(planes_all, "row", scatter_dimension=0, tiled=False)
        cols = in_order(y, summed[0], swap_col(summed[1]))
        both = in_order(x, cols, swap_x(cols))
        return in_order(c, both, swap_core(both))

    mix_parts = mix_grad.reshape(groups, 2, HEAD, 2, 2, quarter)
    mix_home = attn_home(jnp.transpose(mix_parts, (0, 3, 4, 1, 2, 5)))
    out_out = wide(jnp.transpose(mix_home, (2, 1, 3, 0, 4)).reshape(groups * 2 * HEAD, half))
    project_parts = project_grad.reshape(2, 2, 2, share, groups, 4 * HEAD)
    project_home = attn_home(jnp.transpose(project_parts, (4, 0, 1, 2, 3, 5)))
    project_home = jnp.transpose(project_home, (0, 1, 3, 2, 4)).reshape(half, groups, 4 * HEAD)
    query_out = wide(project_home[:, :, : 2 * HEAD].reshape(half, groups * 2 * HEAD))
    key_out = wide(project_home[:, :, 2 * HEAD : 3 * HEAD].reshape(half, groups * HEAD))
    value_out = wide(project_home[:, :, 3 * HEAD :].reshape(half, groups * HEAD))

    def gain_home(part):
        filled = lax.dynamic_update_slice(
            jnp.zeros((half,), jnp.float32), part, (c * quarter,)
        )
        return filled

    gain_attn_out, gain_ffn_out = lax.psum(
        (gain_home(gain_attn_part), gain_home(gain_ffn_part)), ("dp", "row")
    )
    return (
        output,
        input_grad,
        query_out,
        key_out,
        value_out,
        out_out,
        gate_out,
        up_out,
        down_out,
        gain_attn_out,
        gain_ffn_out,
    )


def solution(mesh):
    in_specs = (
        P(None, ("dp", "row"), "col"),
        P(None, ("dp", "row"), "col"),
        P(None, "dp", None),
        P(None, "dp"),
        P("col", "row"),
        P("col", "row"),
        P("col", "row"),
        P("row", "col"),
        P("col", "row"),
        P("col", "row"),
        P("row", "col"),
        P("col"),
        P("col"),
    )
    out_specs = (
        P(None, ("dp", "row"), "col"),
        P(None, ("dp", "row"), "col"),
        P("col", "row"),
        P("col", "row"),
        P("col", "row"),
        P("row", "col"),
        P("col", "row"),
        P("col", "row"),
        P("row", "col"),
        P("col"),
        P("col"),
    )
    sizes = dict(mesh.shape)
    fits = sizes == {"dp": 4, "row": 4, "col": 2}
    chosen = tree_body if fits else body
    return jax.shard_map(chosen, mesh=mesh, in_specs=in_specs, out_specs=out_specs, check_vma=False)
```

```python
import functools
import math

import jax
import jax.numpy as jnp
from jax import lax
from jax.experimental import pallas as pl
from jax.experimental.pallas import tpu as pltpu
from jax.sharding import PartitionSpec as P

D = 2048
HEADS = 16
KV_HEADS = 8
HEAD = 128


EPSILON = 1e-05
THETA = 1000000.0


def contract_rows(left, right):
    return lax.dot_general(
        left, right, (((0,), (0,)), ((), ())), preferred_element_type=jnp.float32
    )


def contract_cols(left, right):
    return lax.dot_general(
        left, right, (((1,), (1,)), ((), ())), preferred_element_type=jnp.float32
    )


def rows_gather(values):
    return lax.all_gather(values, "row", axis=0, tiled=True)


def cols_gather(values):
    return lax.all_gather(values, "col", axis=0, tiled=True)


def cols_reduce(part_fn, rows):
    return lax.psum_scatter(
        part_fn(jnp.int32(0), rows * lax.axis_size("col")), "col", scatter_dimension=0, tiled=True
    )


def rows_reduce(part_fn, rows):
    return lax.psum_scatter(
        part_fn(jnp.int32(0), rows * lax.axis_size("row")).astype(jnp.bfloat16),
        "row",
        scatter_dimension=0,
        tiled=True,
    ).astype(jnp.float32)


def feature_sums(values):
    return lax.psum(jnp.sum(values, axis=1), "col")


def sliced_product(whole, weight, transpose):

    def part_fn(start, count):
        if transpose:
            return contract_cols(whole, weight)
        return jnp.dot(whole, weight, preferred_element_type=jnp.float32)

    return part_fn


def rope_tables(positions):
    half = HEAD // 2
    frequency = jnp.power(THETA, -2.0 * jnp.arange(half, dtype=jnp.float32) / HEAD)
    angles = positions.astype(jnp.float32)[:, None] * frequency[None, :]
    angles = jnp.concatenate([angles, angles], axis=1)
    return (jnp.cos(angles), jnp.sin(angles))


def rotate(values, cosine, sine):
    half = values.shape[-1] // 2
    turned = jnp.concatenate([-values[..., half:], values[..., :half]], axis=-1)
    return values * cosine[:, None, :] + turned * sine[:, None, :]


def rotate_back(grads, cosine, sine):
    half = grads.shape[-1] // 2
    scaled = grads * sine[:, None, :]
    turned = jnp.concatenate([scaled[..., half:], -scaled[..., :half]], axis=-1)
    return grads * cosine[:, None, :] + turned


def norm_forward(values, gain):
    ratio = lax.rsqrt(feature_sums(values * values) / D + EPSILON)[:, None]
    normed = values * ratio
    return (ratio, normed, (normed * gain).astype(jnp.bfloat16))


def norm_backward(grad, ratio, normed, gain):
    scaled = grad * gain
    inner = feature_sums(scaled * normed)[:, None] / D
    return (ratio * (scaled - normed * inner), jnp.sum(grad * normed, axis=0))


def body(
    tokens,
    out_grad,
    path,
    positions,
    w_query,
    w_key,
    w_value,
    w_out,
    w_gate,
    w_up,
    w_down,
    gain_attn,
    gain_ffn,
):
    query_width = w_query.shape[1]
    key_width = w_key.shape[1]
    hidden_width = w_gate.shape[1]
    local_heads = key_width // HEAD
    group = HEADS // KV_HEADS
    scale = 1.0 / math.sqrt(HEAD)
    block_rows = path.shape[1]
    local_rows = tokens.shape[1]
    query_rows = block_rows // lax.axis_size("col")
    first = lax.axis_index("col") * query_rows
    w_project = jnp.concatenate([w_query, w_key, w_value], axis=1)
    w_pair = jnp.concatenate([w_gate, w_up], axis=1)
    project_start = jnp.zeros(w_project.shape, jnp.float32)
    pair_start = jnp.zeros(w_pair.shape, jnp.float32)
    down_start = jnp.zeros(w_down.shape, jnp.float32)

    def micro_step(carry, batch):
        grad_project, grad_out, grad_pair, grad_down, grad_gain_attn, grad_gain_ffn = carry
        block, cotangent, block_path, block_place = batch
        inputs = block.astype(jnp.float32)
        cosine, sine = rope_tables(lax.dynamic_slice_in_dim(block_place, first, query_rows, 0))
        query_path = lax.dynamic_slice_in_dim(block_path, first, query_rows, 0)
        key_labels = block_path[:, 0]
        query_place = first + jnp.arange(query_rows, dtype=jnp.int32)
        key_place = jnp.arange(block_rows, dtype=jnp.int32)
        same_path = (
            (key_labels[None, :] == query_path[:, 0:1])
            | (key_labels[None, :] == query_path[:, 1:2])
            | (key_labels[None, :] == query_path[:, 2:3])
        )
        visible = same_path & (key_place[None, :] <= query_place[:, None])
        ratio_attn, normed_attn, input_attn = norm_forward(inputs, gain_attn)
        gathered_attn = rows_gather(input_attn)
        projected = cols_reduce(sliced_product(gathered_attn, w_project, False), query_rows)
        query = rotate(
            projected[:, :query_width].reshape(query_rows, -1, HEAD), cosine, sine
        ).astype(jnp.bfloat16)
        keys = rotate(
            projected[:, query_width : query_width + key_width].reshape(query_rows, -1, HEAD),
            cosine,
            sine,
        ).astype(jnp.bfloat16)
        values = projected[:, query_width + key_width :].astype(jnp.bfloat16)
        keys_all, values_all = (
            lax.all_gather(keys.reshape(query_rows, key_width), "col", axis=0, tiled=True),
            lax.all_gather(values, "col", axis=0, tiled=True),
        )
        query_groups = query.reshape(query_rows, local_heads, group, HEAD)
        key_heads = keys_all.reshape(block_rows, local_heads, HEAD)
        value_heads = values_all.reshape(block_rows, local_heads, HEAD)
        scores = (
            jnp.einsum(
                "ikgd,jkd->kgij", query_groups, key_heads, preferred_element_type=jnp.float32
            )
            * scale
        )
        scores = jnp.where(visible[None, None], scores, -jnp.inf)
        weights = jax.nn.softmax(scores, axis=-1)
        weights_low = weights.astype(jnp.bfloat16)
        mixed = jnp.einsum(
            "kgij,jkd->ikgd", weights_low, value_heads, preferred_element_type=jnp.float32
        )
        attn_low = mixed.reshape(query_rows, query_width).astype(jnp.bfloat16)
        attn_all = cols_gather(attn_low)
        branch_attn = rows_reduce(sliced_product(attn_all, w_out, False), local_rows)
        middle = inputs + branch_attn
        ratio_ffn, normed_ffn, input_ffn = norm_forward(middle, gain_ffn)
        gathered_ffn = rows_gather(input_ffn)
        pair = cols_reduce(sliced_product(gathered_ffn, w_pair, False), query_rows)
        gate = pair[:, :hidden_width]
        upper = pair[:, hidden_width:]
        sigma = jax.nn.sigmoid(gate)
        silu_value = gate * sigma
        hidden = (silu_value * upper).astype(jnp.bfloat16)
        hidden_all = cols_gather(hidden)
        branch_ffn = rows_reduce(sliced_product(hidden_all, w_down, False), local_rows)
        output = (middle + branch_ffn).astype(jnp.bfloat16)
        cotangent_all = rows_gather(cotangent)
        hidden_grad = cols_reduce(sliced_product(cotangent_all, w_down, True), query_rows)
        grad_down = grad_down + contract_rows(hidden_all, cotangent_all)
        gate_grad = hidden_grad * upper * sigma * (1.0 + gate * (1.0 - sigma))
        upper_grad = hidden_grad * silu_value
        pair_grad = jnp.concatenate([gate_grad, upper_grad], axis=1).astype(jnp.bfloat16)
        pair_all = cols_gather(pair_grad)
        normed_ffn_grad = rows_reduce(sliced_product(pair_all, w_pair, True), local_rows)
        grad_pair = grad_pair + contract_rows(gathered_ffn, pair_all)
        middle_back, gain_ffn_step = norm_backward(normed_ffn_grad, ratio_ffn, normed_ffn, gain_ffn)
        middle_grad = cotangent.astype(jnp.float32) + middle_back
        middle_low = middle_grad.astype(jnp.bfloat16)
        middle_all = rows_gather(middle_low)
        attn_grad = cols_reduce(sliced_product(middle_all, w_out, True), query_rows).astype(
            jnp.bfloat16
        )
        grad_out = grad_out + contract_rows(attn_all, middle_all)
        attn_heads = attn_grad.reshape(query_rows, local_heads, group, HEAD)
        weight_grad = jnp.einsum(
            "ikgd,jkd->kgij", attn_heads, value_heads, preferred_element_type=jnp.float32
        )
        score_grad = (
            weights * (weight_grad - jnp.sum(weights * weight_grad, axis=-1, keepdims=True))
        ).astype(jnp.bfloat16)
        query_grad = (
            jnp.einsum("kgij,jkd->ikgd", score_grad, key_heads, preferred_element_type=jnp.float32)
            * scale
        )
        key_part = (
            jnp.einsum(
                "kgij,ikgd->jkd", score_grad, query_groups, preferred_element_type=jnp.float32
            )
            * scale
        )
        value_part = jnp.einsum(
            "kgij,ikgd->jkd", weights_low, attn_heads, preferred_element_type=jnp.float32
        )
        key_grad, value_grad = (
            lax.psum_scatter(
                key_part.reshape(block_rows, key_width).astype(jnp.bfloat16),
                "col",
                scatter_dimension=0,
                tiled=True,
            ).astype(jnp.float32),
            lax.psum_scatter(
                value_part.reshape(block_rows, key_width).astype(jnp.bfloat16),
                "col",
                scatter_dimension=0,
                tiled=True,
            ).astype(jnp.float32),
        )
        query_back = rotate_back(query_grad.reshape(query_rows, -1, HEAD), cosine, sine).reshape(
            query_rows, query_width
        )
        key_back = rotate_back(key_grad.reshape(query_rows, -1, HEAD), cosine, sine).reshape(
            query_rows, key_width
        )
        projected_grad = jnp.concatenate([query_back, key_back, value_grad], axis=1).astype(
            jnp.bfloat16
        )
        projected_all = cols_gather(projected_grad)
        normed_attn_grad = rows_reduce(sliced_product(projected_all, w_project, True), local_rows)
        grad_project = grad_project + contract_rows(gathered_attn, projected_all)
        input_back, gain_attn_step = norm_backward(
            normed_attn_grad, ratio_attn, normed_attn, gain_attn
        )
        input_grad = (middle_grad + input_back).astype(jnp.bfloat16)
        carry = (
            grad_project,
            grad_out,
            grad_pair,
            grad_down,
            grad_gain_attn + gain_attn_step,
            grad_gain_ffn + gain_ffn_step,
        )
        return (carry, (output, input_grad))

    start = (
        project_start,
        jnp.zeros(w_out.shape, jnp.float32),
        pair_start,
        down_start,
        jnp.zeros(gain_attn.shape, jnp.float32),
        jnp.zeros(gain_ffn.shape, jnp.float32),
    )
    sums, (outputs, input_grads) = lax.scan(micro_step, start, (tokens, out_grad, path, positions))
    grad_project, grad_out, grad_pair, grad_down, grad_gain_attn, grad_gain_ffn = sums
    grad_project, grad_out, grad_pair, grad_down = (
        lax.psum(grad_project.astype(jnp.bfloat16), "dp").astype(jnp.float32),
        lax.psum(grad_out.astype(jnp.bfloat16), "dp").astype(jnp.float32),
        lax.psum(grad_pair.astype(jnp.bfloat16), "dp").astype(jnp.float32),
        lax.psum(grad_down.astype(jnp.bfloat16), "dp").astype(jnp.float32),
    )
    grad_gain_attn, grad_gain_ffn = lax.psum((grad_gain_attn, grad_gain_ffn), ("dp", "row"))
    query_part = grad_project[:, :query_width]
    key_part_grad = grad_project[:, query_width : query_width + key_width]
    value_part_grad = grad_project[:, query_width + key_width :]
    return (
        outputs,
        input_grads,
        query_part,
        key_part_grad,
        value_part_grad,
        grad_out,
        grad_pair[:, :hidden_width],
        grad_pair[:, hidden_width:],
        grad_down,
        grad_gain_attn,
        grad_gain_ffn,
    )


CORE_SWAP = [(0, 1), (1, 0), (2, 3), (3, 2)]
X_SWAP = [(0, 2), (2, 0), (1, 3), (3, 1)]
COL_SWAP = [(0, 1), (1, 0)]
CROSS_SWAP = [(2 * d + j, 2 * (d ^ 1) + 1 - j) for d in range(4) for j in range(2)]
ROW_SECOND = [(0, 2), (1, 3), (2, 0), (3, 1)]
ROW_SWAP = [(0, 1), (1, 0), (2, 3), (3, 2)]
LOG2E = 1.4426950408889634
TRUNK = 1024
LEAF_BEGIN = TRUNK + 4 * 128
SHARE_OF_COST = 8
VMEM_LIMIT = 58 * 1024 * 1024
NT = (((1,), (1,)), ((), ()))
TN = (((0,), (0,)), ((), ()))
NN = (((1,), (0,)), ((), ()))


def swap_core(a):
    return lax.ppermute(a, "dp", CORE_SWAP)


def swap_x(a):
    return lax.ppermute(a, "dp", X_SWAP)


def swap_col(a):
    return lax.ppermute(a, "col", COL_SWAP)


def shift(a, pairs):
    return lax.ppermute(a, "row", pairs)


def after(value, *deps):
    return lax.optimization_barrier((value, *deps))[0]


def cost(flops, moved):
    return pl.CostEstimate(
        flops=flops // SHARE_OF_COST, bytes_accessed=moved // SHARE_OF_COST, transcendentals=0
    )


def mxu(a, b, dims):
    return lax.dot_general(a, b, dims, preferred_element_type=jnp.float32)


def low(a):
    return a.astype(jnp.bfloat16)


def wide(a):
    return a.astype(jnp.float32)


def rows_call(fn, block, row_ins, full_ins, outs, flops, name, scratch=()):
    rows = row_ins[0].shape[0]
    in_specs = [pl.BlockSpec((block, a.shape[1]), lambda i: (i, 0)) for a in row_ins]
    for a in full_ins:
        in_specs.append(
            pl.BlockSpec(
                a.shape, lambda i, nd=a.ndim: (0,) * nd, pipeline_mode=pl.Buffered(1)
            )
        )
    moved = sum(a.size * a.dtype.itemsize for a in (*row_ins, *full_ins))
    moved += sum(rows * w * jnp.dtype(dt).itemsize for w, dt in outs)
    results = pl.pallas_call(
        fn,
        grid=(rows // block,),
        in_specs=in_specs,
        out_specs=[pl.BlockSpec((block, w), lambda i: (i, 0)) for w, _ in outs],
        out_shape=[jax.ShapeDtypeStruct((rows, w), dt) for w, dt in outs],
        scratch_shapes=list(scratch),
        compiler_params=pltpu.CompilerParams(vmem_limit_bytes=VMEM_LIMIT),
        cost_estimate=cost(flops, moved),
        name=name,
    )(*row_ins, *full_ins)
    return list(results)


def turn(u, cosine, sine_signed):
    return u * cosine + pltpu.roll(u, HEAD // 2, 1) * sine_signed


def turn_back(u, cosine, sine_signed):
    return u * cosine - pltpu.roll(u, HEAD // 2, 1) * sine_signed


def project_kernel(
    x0, x1, x2, x3, cos_ref, sin_ref, gain_ref, own_ref, far_ref, xn_ref, qkv_ref, r_ref
):
    pieces = [wide(r[...]) for r in (x0, x1, x2, x3)]
    width = pieces[0].shape[1]
    total = sum(jnp.sum(p * p, axis=1, keepdims=True) for p in pieces)
    ratio = lax.rsqrt(total / (4 * width) + EPSILON)
    r_ref[...] = ratio
    for i, p in enumerate(pieces):
        cols = slice(i * width, (i + 1) * width)
        xn_ref[:, cols] = low(p * ratio * gain_ref[:, cols])
    near = xn_ref[:, : 2 * width]
    far = xn_ref[:, 2 * width :]
    cosine = cos_ref[...]
    sine = sin_ref[...]
    span = own_ref.shape[2]
    heads = span // HEAD
    for g in range(own_ref.shape[0]):
        acc = mxu(near, own_ref[g], NN) + mxu(far, far_ref[g], NN)
        for h in range(heads):
            u = acc[:, h * HEAD : (h + 1) * HEAD]
            if h < heads - 1:
                u = turn(u, cosine, sine)
            at = g * span + h * HEAD
            qkv_ref[:, at : at + HEAD] = low(u)


def segments_of(kind, trunk, leaf_begin, block):
    if kind == "branch":
        return [(0, trunk, None), (None, block, "own")]
    if kind == "leaf":
        return [(0, trunk, None), (trunk, leaf_begin - trunk, "parent"), (None, 2 * block, "own")]
    return [(0, kind, "causal")]


def attention_blocks(qb, block, trunk, leaf_begin, run):
    half = trunk // 2

    @pl.when(qb < half // block)
    def _():
        run(half, 0)

    @pl.when((qb >= half // block) & (qb < trunk // block))
    def _():
        run(trunk, 0)

    @pl.when((qb >= trunk // block) & (qb < leaf_begin // block))
    def _():
        run("branch", pl.multiple_of(qb * block, block))

    @pl.when(qb >= leaf_begin // block)
    def _():
        run("leaf", pl.multiple_of(qb * block - block, block))


def key_rows(start, window, length):
    if start is None:
        return pl.ds(window, length)
    return pl.ds(start, length)


def score_segment(s, start, window, length, mask, qb, block, lab_ref, own_row, parent_row):
    if mask is None:
        return s
    rows = s.shape[0]
    cols = s.shape[1]
    if mask == "parent":
        return jnp.where(lab_ref[key_rows(start, window, length), :] == parent_row, s, -jnp.inf)
    base = window if start is None else start
    key_at = base + lax.broadcasted_iota(jnp.int32, (rows, 1), 0)
    lane = lax.broadcasted_iota(jnp.int32, (1, cols), 1)
    query_at = qb * block + jnp.where(lane >= block, lane - block, lane)
    seen = key_at <= query_at
    if mask == "own":
        seen = seen & (lab_ref[key_rows(start, window, length), :] == own_row)
    return jnp.where(seen, s, -jnp.inf)


def attend_kernel(trunk, leaf_begin, block, q_ref, k_ref, v_ref, lab_ref, row_ref, o_ref, lse_ref, vt_ref):
    qb = pl.program_id(1)
    factor = LOG2E / math.sqrt(HEAD)

    @pl.when(qb == 0)
    def _():
        vt_ref[...] = v_ref[...].T

    queries = jnp.concatenate([q_ref[:, :HEAD], q_ref[:, HEAD:]], axis=0)
    own = row_ref[0:1, :]
    parent = row_ref[1:2, :]
    own_row = jnp.concatenate([own, own], axis=1)
    parent_row = jnp.concatenate([parent, parent], axis=1)

    def run(kind, window):
        scores = []
        segs = segments_of(kind, trunk, leaf_begin, block)
        for start, length, mask in segs:
            s = mxu(k_ref[key_rows(start, window, length), :], queries, NT)
            s = score_segment(
                s, start, window, length, mask, qb, block, lab_ref, own_row, parent_row
            )
            scores.append(s)
        top = scores[0].max(axis=0, keepdims=True)
        for s in scores[1:]:
            top = jnp.maximum(top, s.max(axis=0, keepdims=True))
        total = jnp.zeros_like(top)
        mixed = jnp.zeros((HEAD, 2 * block), jnp.float32)
        shift = top * factor
        for (start, length, mask), s in zip(segs, scores):
            p = jnp.exp2(s * factor - shift)
            total = total + p.sum(axis=0, keepdims=True)
            mixed = mixed + mxu(vt_ref[:, key_rows(start, window, length)], low(p), NN)
        lse_ref[...] = shift + jnp.log2(total)
        mixed = mixed / total
        o_ref[:, :HEAD] = low(mixed[:, :block].T)
        o_ref[:, HEAD:] = low(mixed[:, block:].T)

    attention_blocks(qb, block, trunk, leaf_begin, run)


def attend_back_kernel(
    trunk, leaf_begin, block, blocks, q_ref, k_ref, v_ref, o_ref, do_ref, lab_ref, row_ref, lse_ref,
    cos_ref, sin_ref, out_ref, kt_ref, dk_ref, dv_ref,
):
    qb = pl.program_id(1)
    scale = 1.0 / math.sqrt(HEAD)
    factor = LOG2E * scale

    @pl.when(qb == 0)
    def _():
        kt_ref[...] = k_ref[...].T
        dk_ref[...] = jnp.zeros_like(dk_ref)
        dv_ref[...] = jnp.zeros_like(dv_ref)

    queries = jnp.concatenate([q_ref[:, :HEAD], q_ref[:, HEAD:]], axis=0)
    grads = jnp.concatenate([do_ref[:, :HEAD], do_ref[:, HEAD:]], axis=0)
    outs = jnp.concatenate([o_ref[:, :HEAD], o_ref[:, HEAD:]], axis=0)
    inner = (wide(grads) * wide(outs)).T.sum(axis=0, keepdims=True)
    lse = lse_ref[...]
    own = row_ref[0:1, :]
    parent = row_ref[1:2, :]
    own_row = jnp.concatenate([own, own], axis=1)
    parent_row = jnp.concatenate([parent, parent], axis=1)
    q_rows = pl.ds(pl.multiple_of(qb * block, block), block)

    def run(kind, window):
        dq = jnp.zeros((HEAD, 2 * block), jnp.float32)
        for start, length, mask in segments_of(kind, trunk, leaf_begin, block):
            keys = key_rows(start, window, length)
            s = mxu(k_ref[keys, :], queries, NT)
            s = score_segment(
                s, start, window, length, mask, qb, block, lab_ref, own_row, parent_row
            )
            p = jnp.exp2(s * factor - lse)
            dp = mxu(v_ref[keys, :], grads, NT)
            ds = low(p * (dp - inner))
            dv_ref[keys, :] += mxu(low(p), grads, NN)
            dk_ref[keys, :] += mxu(ds, queries, NN)
            dq = dq + mxu(kt_ref[:, keys], ds, NN)
        dq = dq * scale
        cosine = cos_ref[q_rows, :]
        sine = sin_ref[q_rows, :]
        for h in range(2):
            part = dq[:, h * block : (h + 1) * block].T
            out_ref[q_rows, h * HEAD : (h + 1) * HEAD] = low(turn_back(part, cosine, sine))

    attention_blocks(qb, block, trunk, leaf_begin, run)

    @pl.when(qb == blocks - 1)
    def _():
        dk = dk_ref[...] * scale
        out_ref[:, 2 * HEAD : 3 * HEAD] = low(turn_back(dk, cos_ref[...], sin_ref[...]))
        out_ref[:, 3 * HEAD :] = low(dv_ref[...])


def attention_specs(rows, block, groups):
    q_spec = pl.BlockSpec((block, 2 * HEAD), lambda g, i: (i, 2 * g))
    k_spec = pl.BlockSpec((rows, HEAD), lambda g, i: (0, 4 * g + 2))
    v_spec = pl.BlockSpec((rows, HEAD), lambda g, i: (0, 4 * g + 3))
    lab_spec = pl.BlockSpec((rows, 1), lambda g, i: (0, 0))
    row_spec = pl.BlockSpec((8, block), lambda g, i: (0, i))
    o_spec = pl.BlockSpec((block, 2 * HEAD), lambda g, i: (i, g))
    lse_spec = pl.BlockSpec((None, None, 1, 2 * block), lambda g, i: (g, i, 0, 0))
    return q_spec, k_spec, v_spec, lab_spec, row_spec, o_spec, lse_spec


def attend(qkv, label_col, label_rows, trunk, leaf_begin, block):
    rows = qkv.shape[0]
    groups = qkv.shape[1] // (4 * HEAD)
    blocks = rows // block
    q_spec, k_spec, v_spec, lab_spec, row_spec, o_spec, lse_spec = attention_specs(rows, block, groups)
    pairs = groups * 2 * rows * rows // 2
    return pl.pallas_call(
        functools.partial(attend_kernel, trunk, leaf_begin, block),
        grid=(groups, blocks),
        in_specs=[q_spec, k_spec, v_spec, lab_spec, row_spec],
        out_specs=[o_spec, lse_spec],
        out_shape=[
            jax.ShapeDtypeStruct((rows, groups * 2 * HEAD), jnp.bfloat16),
            jax.ShapeDtypeStruct((groups, blocks, 1, 2 * block), jnp.float32),
        ],
        scratch_shapes=[pltpu.VMEM((HEAD, rows), jnp.bfloat16)],
        compiler_params=pltpu.CompilerParams(vmem_limit_bytes=VMEM_LIMIT),
        cost_estimate=cost(4 * 4 * pairs * HEAD, 20 * rows * HEAD * 2),
        name="attend",
    )(qkv, qkv, qkv, label_col, label_rows)


def attend_back(qkv, attn, attn_grad, label_col, label_rows, lse, cosine, sine, trunk, leaf_begin, block):
    rows = qkv.shape[0]
    groups = qkv.shape[1] // (4 * HEAD)
    blocks = rows // block
    q_spec, k_spec, v_spec, lab_spec, row_spec, o_spec, lse_spec = attention_specs(rows, block, groups)
    table = pl.BlockSpec((rows, HEAD), lambda g, i: (0, 0))
    pairs = groups * 2 * rows * rows // 2
    return pl.pallas_call(
        functools.partial(attend_back_kernel, trunk, leaf_begin, block, blocks),
        grid=(groups, blocks),
        in_specs=[q_spec, k_spec, v_spec, o_spec, o_spec, lab_spec, row_spec, lse_spec, table, table],
        out_specs=pl.BlockSpec((rows, 4 * HEAD), lambda g, i: (0, g)),
        out_shape=jax.ShapeDtypeStruct((rows, groups * 4 * HEAD), jnp.bfloat16),
        scratch_shapes=[
            pltpu.VMEM((HEAD, rows), jnp.bfloat16),
            pltpu.VMEM((rows, HEAD), jnp.float32),
            pltpu.VMEM((rows, HEAD), jnp.float32),
        ],
        compiler_params=pltpu.CompilerParams(vmem_limit_bytes=VMEM_LIMIT),
        cost_estimate=cost(10 * 4 * pairs * HEAD, 40 * rows * HEAD * 2),
        name="attend_back",
    )(qkv, qkv, qkv, attn, attn_grad, label_col, label_rows, lse, cosine, sine)


def quarters_out(acc, out_refs):
    width = out_refs[0].shape[1]
    for i, ref in enumerate(out_refs):
        ref[...] = low(acc[:, i * width : (i + 1) * width])


def mix_kernel(a_ref, near_ref, far_ref, *out_refs):
    groups = near_ref.shape[0]
    span = near_ref.shape[2]
    for i, out_ref in enumerate(out_refs):
        w_ref = (near_ref, far_ref)[i // 2]
        acc = sum(
            mxu(a_ref[:, g * span : (g + 1) * span], w_ref[g, i % 2], NN) for g in range(groups)
        )
        out_ref[...] = low(acc)


def sum_out_kernel(count, *refs):
    a_refs, w_refs = refs[:count], refs[count : 2 * count]
    acc = sum(mxu(a[...], w[...], NN) for a, w in zip(a_refs, w_refs))
    quarters_out(acc, refs[2 * count :])


def project_back_kernel(d_ref, near_ref, far_ref, *out_refs):
    groups = near_ref.shape[0]
    span = near_ref.shape[2]
    for i, w_ref in enumerate((near_ref, far_ref)):
        acc = sum(mxu(d_ref[:, g * span : (g + 1) * span], w_ref[g], NT) for g in range(groups))
        quarters_out(acc, out_refs[2 * i : 2 * i + 2])


def attn_grad_kernel(h0, h1, h2, h3, near_ref, far_ref, out_ref):
    groups = near_ref.shape[0]
    span = near_ref.shape[2]
    for g in range(groups):
        acc = sum(
            mxu(h[...], (near_ref, far_ref)[i // 2][g, i % 2], NT)
            for i, h in enumerate((h0, h1, h2, h3))
        )
        out_ref[:, g * span : (g + 1) * span] = low(acc)


def gate_up_kernel(*refs):
    x_refs, w_refs, out_refs = refs[:4], refs[4:8], refs[8:12]
    xs_ref = refs[12]
    width = x_refs[0].shape[1]
    for i, x in enumerate(x_refs):
        xs_ref[:, i * width : (i + 1) * width] = x[...]
    normed = xs_ref[...]
    for w_ref, out_ref in zip(w_refs, out_refs):
        unit = 512
        for at in range(0, w_ref.shape[0], unit):
            cols = slice(at, at + unit)
            out_ref[:, cols] = low(mxu(normed, w_ref[cols, :], NT))


def hidden_kernel(*refs):
    g_refs, gate_refs, up_refs, w_refs = refs[:4], refs[4:6], refs[6:8], refs[8:10]
    out_refs = refs[10:16]
    gs_ref = refs[16]
    width = g_refs[0].shape[1]
    for i, g in enumerate(g_refs):
        gs_ref[:, i * width : (i + 1) * width] = g[...]
    grads = gs_ref[...]
    for side in range(2):
        w_ref = w_refs[side]
        dgate_ref, dup_ref, hid_ref = out_refs[3 * side : 3 * side + 3]
        unit = 256
        for at in range(0, w_ref.shape[0], unit):
            cols = slice(at, at + unit)
            gate = wide(gate_refs[side][:, cols])
            upper = wide(up_refs[side][:, cols])
            hidden_grad = mxu(grads, w_ref[cols, :], NT)
            sigma = jax.nn.sigmoid(gate)
            silu_value = gate * sigma
            hid_ref[:, cols] = low(silu_value * upper)
            dgate_ref[:, cols] = low(
                hidden_grad * upper * sigma * (1.0 + gate * (1.0 - sigma))
            )
            dup_ref[:, cols] = low(hidden_grad * silu_value)


def ffn_home_kernel(turned, where_ref, *refs):
    part_refs, out_ref = refs[:4], refs[4]
    step = pl.program_id(0)
    at_col, at_core, at_x = step // 4, lax.rem(step // 2, 2), lax.rem(step, 2)
    other_col = jnp.where(at_col == where_ref[0], 0, 1)
    want = 2 * jnp.where(at_x == where_ref[1], 0, 1) + jnp.where(at_core == where_ref[2], 0, 1)
    quarter = part_refs[0].shape[2] // 2
    for j in range(4):

        @pl.when(want == j)
        def _(part=part_refs[j]):
            for h in range(2):
                start = at_core * quarter if h == 0 else (1 - at_core) * quarter
                place = pl.ds(pl.multiple_of(start, quarter), quarter)
                values = wide(part[other_col, :, h * quarter : (h + 1) * quarter])
                if turned:
                    out_ref[place, :] = values.T
                else:
                    out_ref[:, place] = values


def ffn_home(where, parts, at, unit, turned, name):
    half = parts[0].shape[2]
    whole = pl.BlockSpec((2, unit, half), lambda i, w: (0, at, 0), pipeline_mode=pl.Buffered(1))
    if turned:
        spec, shape = pl.BlockSpec((half, unit), lambda i, w: (0, i)), (half, 8 * unit)
    else:
        spec, shape = pl.BlockSpec((unit, half), lambda i, w: (i, 0)), (8 * unit, half)
    return pl.pallas_call(
        functools.partial(ffn_home_kernel, turned),
        grid_spec=pltpu.PrefetchScalarGridSpec(
            num_scalar_prefetch=1, grid=(8,), in_specs=[whole] * 4, out_specs=spec
        ),
        out_shape=jax.ShapeDtypeStruct(shape, jnp.float32),
        compiler_params=pltpu.CompilerParams(vmem_limit_bytes=VMEM_LIMIT),
        cost_estimate=cost(0, 8 * unit * half * 6),
        name=name,
    )(where, *parts)


def weight_grad_kernel(count, split, *refs):
    a_ref = refs[0]
    b_refs = refs[1 : 1 + count]
    o_refs = refs[1 + count :]
    left = a_ref[...].T
    for i, b in enumerate(b_refs):
        width = b.shape[1]
        acc = low(mxu(left, b[...], NN))
        if split:
            for j in range(split):
                o_refs[0][j] = acc[:, j * width // split : (j + 1) * width // split]
        elif len(o_refs) == 1:
            o_refs[0][:, i * width : (i + 1) * width] = acc
        else:
            o_refs[i][...] = acc


def weight_grad(a, bs, block, name, joined=True, split=0):
    rows, m = a.shape
    n = sum(b.shape[1] for b in bs)
    in_specs = [pl.BlockSpec((rows, block), lambda i: (0, i))]
    for b in bs:
        in_specs.append(
            pl.BlockSpec(b.shape, lambda i: (0, 0), pipeline_mode=pl.Buffered(1))
        )
    if split:
        out_specs = [pl.BlockSpec((split, block, n // split), lambda i: (0, i, 0))]
        shapes = [(split, m, n // split)]
    else:
        widths = [n] if joined else [b.shape[1] for b in bs]
        out_specs = [pl.BlockSpec((block, w), lambda i: (i, 0)) for w in widths]
        shapes = [(m, w) for w in widths]
    outs = pl.pallas_call(
        functools.partial(weight_grad_kernel, len(bs), split),
        grid=(m // block,),
        in_specs=in_specs,
        out_specs=out_specs,
        out_shape=[jax.ShapeDtypeStruct(shape, jnp.bfloat16) for shape in shapes],
        compiler_params=pltpu.CompilerParams(vmem_limit_bytes=VMEM_LIMIT),
        cost_estimate=cost(2 * rows * m * n, 2 * (rows * m + rows * n + m * n)),
        name=name,
    )(a, *bs)
    return outs if len(outs) > 1 else outs[0]


def take(a, index, axis):
    return lax.dynamic_index_in_dim(a, index, axis, keepdims=False)


def in_order(index, mine, other, axis=0):
    first = jnp.where(index == 0, mine, other)
    second = jnp.where(index == 0, other, mine)
    return jnp.stack([first, second], axis=axis)


def spread(a):
    b = swap_col(a)
    return [a, b, swap_core(a), swap_core(b)]


def collect_core(parts):
    own, own_other, send, send_other = parts
    outgoing = low(wide(own_other) + wide(swap_core(send_other)))
    return own, swap_core(send), outgoing


def collect_col(own, got, outgoing):
    return wide(own) + wide(got) + wide(swap_col(outgoing))


def small_sum(v):
    cross = lax.ppermute(v, ("dp", "col"), CROSS_SWAP)
    return (v + swap_core(v)) + (swap_col(v) + cross)


def tree_body(
    tokens,
    out_grad,
    path,
    positions,
    w_query,
    w_key,
    w_value,
    w_out,
    w_gate,
    w_up,
    w_down,
    gain_attn,
    gain_ffn,
):
    dp = lax.axis_index("dp")
    x = dp // 2
    c = lax.rem(dp, 2)
    z = lax.axis_index("row")
    y = lax.axis_index("col")
    micro, local_rows, half = tokens.shape
    quarter = half // 2
    rows = path.shape[1]
    planes = lax.axis_size("row")
    features = 2 * half
    block = 256

    def to_trees(a):
        mine = lax.dynamic_slice_in_dim(a, c * quarter, quarter, 2)
        other = swap_core(lax.dynamic_slice_in_dim(a, (1 - c) * quarter, quarter, 2))
        return in_order(c, mine, other).reshape(planes * local_rows, quarter)

    def of_core(trees):
        trees = trees.reshape(2, micro, local_rows, quarter)
        return take(trees, c, 0), take(trees, 1 - c, 0)

    def by_feature(mine, other):
        return in_order(c, mine, swap_core(other), 2).reshape(micro, local_rows, half)

    groups = w_key.shape[1] // HEAD
    share = quarter // 2
    unit = w_gate.shape[1] // 8

    def project_piece(g):
        at = c * quarter + x * share
        return jnp.concatenate(
            [
                lax.dynamic_slice(w_query, (at, g * 2 * HEAD), (share, 2 * HEAD)),
                lax.dynamic_slice(w_key, (at, g * HEAD), (share, HEAD)),
                lax.dynamic_slice(w_value, (at, g * HEAD), (share, HEAD)),
            ],
            axis=1,
        )

    def mix_piece(g):
        return lax.dynamic_slice(w_out, ((g * 2 + x) * HEAD, c * quarter), (HEAD, quarter))

    def by_core(a):
        return jnp.where(c == 0, a, jnp.concatenate([a[:, quarter:], a[:, :quarter]], axis=1))

    def hidden_piece(j):
        at = ((2 * j + c) * 2 + x) * unit
        return [
            by_core(lax.dynamic_slice_in_dim(w_gate, at, unit, 1).T),
            by_core(lax.dynamic_slice_in_dim(w_up, at, unit, 1).T),
            by_core(lax.dynamic_slice_in_dim(w_down, at, unit, 0)),
        ]

    def four(kept, got):
        return jnp.concatenate(
            [kept[:, :quarter], got[:, :quarter], kept[:, quarter:], got[:, quarter:]], axis=1
        )

    project_sent = project_piece(1 - y)
    project_mine = jnp.stack([project_piece(y), swap_col(project_sent)])
    block_in = lax.all_to_all(to_trees(tokens), "row", 0, 0, tiled=True)
    sent = jnp.concatenate([*hidden_piece(1 - y), jnp.tile(mix_piece(1 - y), (1, 2))])
    got = swap_col(after(sent, project_sent))
    project_all = lax.all_gather(project_mine, "row", axis=0)

    marks = jnp.concatenate([path, positions[:, :, None]], axis=2)
    marks = jnp.transpose(marks, (2, 0, 1))
    marks = in_order(c, marks, swap_core(marks), 1).reshape(4, 2 * micro, rows)
    marks = take(marks, z, 1)
    cosine, sine = rope_tables(marks[3])
    sign = jnp.where(jnp.arange(HEAD) < HEAD // 2, -1.0, 1.0).astype(jnp.float32)
    sine = sine * sign[None, :]
    label_col = marks[0][:, None]
    label_rows = jnp.pad(marks, ((0, 4), (0, 0)))

    hidden_kept = hidden_piece(y)
    hidden_mine = [
        four(kept, got[i * unit : (i + 1) * unit]) for i, kept in enumerate(hidden_kept)
    ]
    mix_mine = jnp.stack([mix_piece(y), got[3 * unit :, :quarter]])

    def gain_order(gain):
        kept = gain.reshape(2, quarter)
        both = jnp.stack([kept, swap_col(kept)], axis=1)
        both = jnp.where(c == 0, both, both[::-1])
        return both.reshape(1, features)

    gain_attn_all = gain_order(gain_attn)
    gain_attn_own = gain_attn_all[:, :quarter]
    gain_ffn_own = lax.dynamic_slice_in_dim(gain_ffn, c * quarter, quarter, 0)[None, :]

    (
        project_all, block_in, mix_mine, gate_piece, up_piece, down_piece,
        cosine, sine, label_col, label_rows, gain_attn_all,
    ) = lax.optimization_barrier(
        (
            project_all, block_in, mix_mine, *hidden_mine,
            cosine, sine, label_col, label_rows, gain_attn_all,
        )
    )

    pieces = spread(block_in)
    mix_all = lax.all_gather(mix_mine, "row", axis=0)
    gate_mine = lax.all_gather(gate_piece, "row", axis=0, tiled=True)
    up_mine = lax.all_gather(after(up_piece, mix_all), "row", axis=0, tiled=True)
    down_mine = lax.all_gather(after(down_piece, gate_mine), "row", axis=0, tiled=True)
    gate_far, up_far, down_far = (swap_x(u) for u in (gate_mine, up_mine, down_mine))

    def of_core_pairs(mine, other):
        both = in_order(x, mine, other, 2)
        pairs = both.reshape((2, planes // 2) + both.shape[1:])
        return take(pairs, c, 0), swap_core(take(pairs, 1 - c, 0))

    near, far = of_core_pairs(project_all, swap_x(project_all))
    w_near = near.reshape(groups, half, 4 * HEAD)
    w_far = far.reshape(groups, half, 4 * HEAD)

    normed_attn, qkv, ratio_attn = rows_call(
        project_kernel,
        block,
        [*pieces, cosine, sine],
        [gain_attn_all, w_near, w_far],
        [(features, jnp.bfloat16), (groups * 4 * HEAD, jnp.bfloat16), (1, jnp.float32)],
        2 * rows * features * groups * 4 * HEAD,
        "project",
    )
    near, far = of_core_pairs(mix_all, after(swap_x(mix_all), qkv))
    attn, lse = attend(after(qkv, near), label_col, label_rows, TRUNK, LEAF_BEGIN, block)
    mix_shape = (groups, 2, 2 * HEAD, quarter)
    m_near, m_far = near.reshape(mix_shape), after(far, attn).reshape(mix_shape)
    parts = rows_call(
        mix_kernel,
        2 * block,
        [attn],
        [m_near, m_far],
        [(quarter, jnp.bfloat16)] * 4,
        2 * rows * features * groups * 2 * HEAD,
        "mix",
    )
    cotangent = lax.all_to_all(to_trees(out_grad), "row", 0, 0, tiled=True)
    parts[1] = after(parts[1], cotangent)
    own, got, outgoing = collect_core(parts)
    middle = wide(block_in) + collect_col(own, got, outgoing)
    square = small_sum(jnp.sum(middle * middle, axis=1))
    ratio_ffn = lax.rsqrt(square / features + EPSILON)[:, None]
    normed_ffn = middle * ratio_ffn
    ffn_pieces = spread(after(low(normed_ffn * gain_ffn_own), up_mine, gate_far))
    grad_near, grad_across = cotangent, swap_col(after(cotangent, ffn_pieces[1]))
    gate_m, up_m, gate_o, up_o = rows_call(
        gate_up_kernel,
        block,
        ffn_pieces,
        [gate_mine, up_mine, gate_far, up_far],
        [(planes * unit, jnp.bfloat16)] * 4,
        2 * rows * features * 4 * planes * unit,
        "gate_up",
        [pltpu.VMEM((block, features), jnp.bfloat16)],
    )
    grad_pieces = [
        grad_near,
        grad_across,
        swap_core(after(grad_near, ffn_pieces[3])),
        swap_core(after(grad_across, gate_m)),
    ]
    dgate_m, dup_m, hid_m, dgate_o, dup_o, hid_o = rows_call(
        hidden_kernel,
        block,
        [*grad_pieces, gate_m, gate_o, up_m, up_o],
        [down_mine, down_far],
        [(planes * unit, jnp.bfloat16)] * 6,
        2 * rows * features * 2 * planes * unit,
        "hidden",
        [pltpu.VMEM((block, features), jnp.bfloat16)],
    )

    def unit_grad(a, pieces_of, name, before):
        return weight_grad(after(a, before), pieces_of, 2 * block, name)

    def to_row(total):
        return lax.psum_scatter(total, "row", scatter_dimension=0, tiled=True)

    down_other = weight_grad(hid_o, grad_pieces, 2 * block, "down_grad_other")
    parts = rows_call(
        functools.partial(sum_out_kernel, 4),
        2 * block,
        [after(dgate_m, down_other), dup_m, dgate_o, dup_o],
        [gate_mine, up_mine, gate_far, up_far],
        [(quarter, jnp.bfloat16)] * 4,
        2 * rows * features * 4 * planes * unit,
        "pair_back",
    )
    gate_other = unit_grad(dgate_o, ffn_pieces, "gate_grad_other", parts[0])
    down_own = unit_grad(hid_m, grad_pieces, "down_grad_mine", gate_other)
    parts[1] = after(parts[1], down_own)
    own, got, outgoing = collect_core(parts)
    down_total = low(wide(after(down_own, outgoing)) + wide(swap_x(down_other)))
    down_sum = to_row(down_total)
    up_other = unit_grad(dup_o, ffn_pieces, "up_grad_other", down_total)
    gate_own = unit_grad(dgate_m, ffn_pieces, "gate_grad_mine", up_other)
    normed_ffn_grad = collect_col(after(own, gate_own), got, outgoing)

    def norm_back(grad, ratio, normed, gain):
        scaled = grad * gain
        inner = small_sum(jnp.sum(scaled * normed, axis=1))[:, None] / features
        return ratio * (scaled - normed * inner), jnp.sum(grad * normed, axis=0)

    middle_back, gain_ffn_part = norm_back(normed_ffn_grad, ratio_ffn, normed_ffn, gain_ffn_own)
    middle_grad = wide(cotangent) + middle_back
    middle_low = low(middle_grad)
    middle_pieces = spread(middle_low)
    up_own = unit_grad(dup_m, ffn_pieces, "up_grad_mine", middle_low)
    gate_total = low(wide(after(gate_own, up_own)) + wide(swap_x(gate_other)))
    gate_sum = to_row(gate_total)
    where = jnp.stack([y, x, c]).astype(jnp.int32)

    def unit_halves(total):
        kept = jnp.concatenate([total[:, :quarter], total[:, half : half + quarter]], axis=1)
        sent = jnp.concatenate([total[:, quarter:half], total[:, half + quarter :]], axis=1)
        return kept, sent

    def unit_parts(kept, sent):
        both = jnp.stack([kept, swap_col(sent)])
        over = swap_x(both)
        return [both, swap_core(both), over, swap_core(over)]

    out_parts = rows_call(
        functools.partial(sum_out_kernel, 2),
        2 * block,
        [after(hid_m, gate_total), hid_o],
        [down_mine, down_far],
        [(quarter, jnp.bfloat16)] * 4,
        2 * rows * features * 2 * planes * unit,
        "down",
    )
    attn_grad = rows_call(
        attn_grad_kernel,
        2 * block,
        [after(middle_pieces[0], out_parts[0]), *middle_pieces[1:]],
        [m_near, m_far],
        [(groups * 2 * HEAD, jnp.bfloat16)],
        2 * rows * features * groups * 2 * HEAD,
        "attn_grad",
    )[0]
    out_parts[1] = after(out_parts[1], attn_grad)
    out_own, out_got, out_outgoing = collect_core(out_parts)
    qkv_grad = attend_back(
        qkv, attn, after(attn_grad, out_outgoing), label_col, label_rows, lse, cosine, sine,
        TRUNK, LEAF_BEGIN, block,
    )
    output = low(after(middle, qkv_grad) + collect_col(out_own, out_got, out_outgoing))
    up_total = low(wide(after(up_own, output)) + wide(swap_x(up_other)))
    up_sum = to_row(up_total)
    parts = rows_call(
        project_back_kernel,
        2 * block,
        [after(qkv_grad, up_total)],
        [w_near, w_far],
        [(quarter, jnp.bfloat16)] * 4,
        2 * rows * features * groups * 4 * HEAD,
        "project_back",
    )
    output_tree = lax.all_to_all(output, "row", 0, 0, tiled=True)
    home_kept, home_sent = unit_halves(
        jnp.concatenate([after(down_sum, parts[0]), gate_sum])
    )
    project_grad = weight_grad(
        normed_attn, [after(qkv_grad, home_sent)], 2 * block, "project_grad", split=groups
    )
    parts[1] = after(parts[1], project_grad)
    own, got, outgoing = collect_core(parts)
    mix_grads = weight_grad(
        attn,
        [after(middle_pieces[0], outgoing), *middle_pieces[1:]],
        groups * 2 * HEAD,
        "mix_grad",
        joined=False,
    )

    project_parts = project_grad.reshape(groups, 2, 2, 2, share, 4 * HEAD)
    mix_parts = jnp.stack([m.reshape(groups, 2, HEAD, quarter) for m in mix_grads], axis=1)
    mix_parts = mix_parts.reshape(groups, 2, 2, 2, HEAD, quarter)

    def of_x(index):
        return jnp.concatenate([take(project_parts, index, 3), take(mix_parts, index, 3)], axis=3)

    attn_sent = of_x(1 - x)
    attn_kept = of_x(after(x, attn_sent))
    home_parts = unit_parts(home_kept, home_sent)
    home_parts[0] = after(home_parts[0], attn_kept)
    down_out = ffn_home(where, home_parts, 0, unit, False, "down_home")
    gate_out = ffn_home(where, home_parts, 1, unit, True, "gate_home")
    normed_attn_grad = collect_col(after(own, down_out, gate_out), got, outgoing)
    normed_attn_own = wide(block_in) * ratio_attn
    input_back, gain_attn_part = norm_back(
        normed_attn_grad, ratio_attn, normed_attn_own, gain_attn_own
    )
    input_low = low(middle_grad + input_back)
    input_tree = lax.all_to_all(input_low, "row", 0, 0, tiled=True)
    up_kept, up_sent = unit_halves(after(up_sum, input_low))
    attn_total = low(wide(after(attn_kept, up_sent)) + wide(swap_x(attn_sent)))
    by_plane = in_order(c, attn_total[:, 0], swap_core(attn_total[:, 1]))
    by_plane = by_plane.reshape((planes,) + by_plane.shape[2:])
    attn_sum = lax.psum_scatter(by_plane, "row", scatter_dimension=0, tiled=False)
    output, output_sent = of_core(after(output_tree, by_plane))
    output = by_feature(output, output_sent)
    up_parts = unit_parts(up_kept, up_sent)
    up_parts[0] = after(up_parts[0], output)
    up_out = ffn_home(where, up_parts, 0, unit, True, "up_home")
    input_grad = by_feature(*of_core(after(input_tree, up_out)))

    home = in_order(y, attn_sum[0], swap_col(attn_sum[1]))
    home = in_order(x, home, swap_x(home))
    home = in_order(c, home, swap_core(home))
    mix_home = home[:, :, :, share:]
    out_out = wide(jnp.transpose(mix_home, (2, 1, 3, 0, 4)).reshape(groups * 2 * HEAD, half))
    project_home = jnp.transpose(home[:, :, :, :share], (0, 1, 3, 2, 4))
    project_home = project_home.reshape(half, groups, 4 * HEAD)
    query_out = wide(project_home[:, :, : 2 * HEAD].reshape(half, groups * 2 * HEAD))
    key_out = wide(project_home[:, :, 2 * HEAD : 3 * HEAD].reshape(half, groups * HEAD))
    value_out = wide(project_home[:, :, 3 * HEAD :].reshape(half, groups * HEAD))

    gains = jnp.stack([gain_attn_part, gain_ffn_part])
    gains = gains + shift(gains, ROW_SECOND)
    gains = gains + shift(gains, ROW_SWAP)
    gains = gains + swap_x(gains)
    gains = in_order(c, gains, swap_core(gains), 1)
    gain_attn_out = gains[0].reshape(half)
    gain_ffn_out = gains[1].reshape(half)
    return (
        output,
        input_grad,
        query_out,
        key_out,
        value_out,
        out_out,
        gate_out,
        up_out,
        down_out,
        gain_attn_out,
        gain_ffn_out,
    )


def solution(mesh):
    in_specs = (
        P(None, ("dp", "row"), "col"),
        P(None, ("dp", "row"), "col"),
        P(None, "dp", None),
        P(None, "dp"),
        P("col", "row"),
        P("col", "row"),
        P("col", "row"),
        P("row", "col"),
        P("col", "row"),
        P("col", "row"),
        P("row", "col"),
        P("col"),
        P("col"),
    )
    out_specs = (
        P(None, ("dp", "row"), "col"),
        P(None, ("dp", "row"), "col"),
        P("col", "row"),
        P("col", "row"),
        P("col", "row"),
        P("row", "col"),
        P("col", "row"),
        P("col", "row"),
        P("row", "col"),
        P("col"),
        P("col"),
    )
    sizes = dict(mesh.shape)
    fits = sizes == {"dp": 4, "row": 4, "col": 2}
    chosen = tree_body if fits else body
    return jax.shard_map(chosen, mesh=mesh, in_specs=in_specs, out_specs=out_specs, check_vma=False)
```

```python
import functools
import math

import jax
import jax.numpy as jnp
from jax import lax
from jax.experimental import pallas as pl
from jax.experimental.pallas import tpu as pltpu
from jax.sharding import PartitionSpec as P

D = 2048
HEADS = 16
KV_HEADS = 8
HEAD = 128


EPSILON = 1e-05
THETA = 1000000.0


def contract_rows(left, right):
    return lax.dot_general(
        left, right, (((0,), (0,)), ((), ())), preferred_element_type=jnp.float32
    )


def contract_cols(left, right):
    return lax.dot_general(
        left, right, (((1,), (1,)), ((), ())), preferred_element_type=jnp.float32
    )


def rows_gather(values):
    return lax.all_gather(values, "row", axis=0, tiled=True)


def cols_gather(values):
    return lax.all_gather(values, "col", axis=0, tiled=True)


def cols_reduce(part_fn, rows):
    return lax.psum_scatter(
        part_fn(jnp.int32(0), rows * lax.axis_size("col")), "col", scatter_dimension=0, tiled=True
    )


def rows_reduce(part_fn, rows):
    return lax.psum_scatter(
        part_fn(jnp.int32(0), rows * lax.axis_size("row")).astype(jnp.bfloat16),
        "row",
        scatter_dimension=0,
        tiled=True,
    ).astype(jnp.float32)


def feature_sums(values):
    return lax.psum(jnp.sum(values, axis=1), "col")


def sliced_product(whole, weight, transpose):

    def part_fn(start, count):
        if transpose:
            return contract_cols(whole, weight)
        return jnp.dot(whole, weight, preferred_element_type=jnp.float32)

    return part_fn


def rope_tables(positions):
    half = HEAD // 2
    frequency = jnp.power(THETA, -2.0 * jnp.arange(half, dtype=jnp.float32) / HEAD)
    angles = positions.astype(jnp.float32)[:, None] * frequency[None, :]
    angles = jnp.concatenate([angles, angles], axis=1)
    return (jnp.cos(angles), jnp.sin(angles))


def rotate(values, cosine, sine):
    half = values.shape[-1] // 2
    turned = jnp.concatenate([-values[..., half:], values[..., :half]], axis=-1)
    return values * cosine[:, None, :] + turned * sine[:, None, :]


def rotate_back(grads, cosine, sine):
    half = grads.shape[-1] // 2
    scaled = grads * sine[:, None, :]
    turned = jnp.concatenate([scaled[..., half:], -scaled[..., :half]], axis=-1)
    return grads * cosine[:, None, :] + turned


def norm_forward(values, gain):
    ratio = lax.rsqrt(feature_sums(values * values) / D + EPSILON)[:, None]
    normed = values * ratio
    return (ratio, normed, (normed * gain).astype(jnp.bfloat16))


def norm_backward(grad, ratio, normed, gain):
    scaled = grad * gain
    inner = feature_sums(scaled * normed)[:, None] / D
    return (ratio * (scaled - normed * inner), jnp.sum(grad * normed, axis=0))


def body(
    tokens,
    out_grad,
    path,
    positions,
    w_query,
    w_key,
    w_value,
    w_out,
    w_gate,
    w_up,
    w_down,
    gain_attn,
    gain_ffn,
):
    query_width = w_query.shape[1]
    key_width = w_key.shape[1]
    hidden_width = w_gate.shape[1]
    local_heads = key_width // HEAD
    group = HEADS // KV_HEADS
    scale = 1.0 / math.sqrt(HEAD)
    block_rows = path.shape[1]
    local_rows = tokens.shape[1]
    query_rows = block_rows // lax.axis_size("col")
    first = lax.axis_index("col") * query_rows
    w_project = jnp.concatenate([w_query, w_key, w_value], axis=1)
    w_pair = jnp.concatenate([w_gate, w_up], axis=1)
    project_start = jnp.zeros(w_project.shape, jnp.float32)
    pair_start = jnp.zeros(w_pair.shape, jnp.float32)
    down_start = jnp.zeros(w_down.shape, jnp.float32)

    def micro_step(carry, batch):
        grad_project, grad_out, grad_pair, grad_down, grad_gain_attn, grad_gain_ffn = carry
        block, cotangent, block_path, block_place = batch
        inputs = block.astype(jnp.float32)
        cosine, sine = rope_tables(lax.dynamic_slice_in_dim(block_place, first, query_rows, 0))
        query_path = lax.dynamic_slice_in_dim(block_path, first, query_rows, 0)
        key_labels = block_path[:, 0]
        query_place = first + jnp.arange(query_rows, dtype=jnp.int32)
        key_place = jnp.arange(block_rows, dtype=jnp.int32)
        same_path = (
            (key_labels[None, :] == query_path[:, 0:1])
            | (key_labels[None, :] == query_path[:, 1:2])
            | (key_labels[None, :] == query_path[:, 2:3])
        )
        visible = same_path & (key_place[None, :] <= query_place[:, None])
        ratio_attn, normed_attn, input_attn = norm_forward(inputs, gain_attn)
        gathered_attn = rows_gather(input_attn)
        projected = cols_reduce(sliced_product(gathered_attn, w_project, False), query_rows)
        query = rotate(
            projected[:, :query_width].reshape(query_rows, -1, HEAD), cosine, sine
        ).astype(jnp.bfloat16)
        keys = rotate(
            projected[:, query_width : query_width + key_width].reshape(query_rows, -1, HEAD),
            cosine,
            sine,
        ).astype(jnp.bfloat16)
        values = projected[:, query_width + key_width :].astype(jnp.bfloat16)
        keys_all, values_all = (
            lax.all_gather(keys.reshape(query_rows, key_width), "col", axis=0, tiled=True),
            lax.all_gather(values, "col", axis=0, tiled=True),
        )
        query_groups = query.reshape(query_rows, local_heads, group, HEAD)
        key_heads = keys_all.reshape(block_rows, local_heads, HEAD)
        value_heads = values_all.reshape(block_rows, local_heads, HEAD)
        scores = (
            jnp.einsum(
                "ikgd,jkd->kgij", query_groups, key_heads, preferred_element_type=jnp.float32
            )
            * scale
        )
        scores = jnp.where(visible[None, None], scores, -jnp.inf)
        weights = jax.nn.softmax(scores, axis=-1)
        weights_low = weights.astype(jnp.bfloat16)
        mixed = jnp.einsum(
            "kgij,jkd->ikgd", weights_low, value_heads, preferred_element_type=jnp.float32
        )
        attn_low = mixed.reshape(query_rows, query_width).astype(jnp.bfloat16)
        attn_all = cols_gather(attn_low)
        branch_attn = rows_reduce(sliced_product(attn_all, w_out, False), local_rows)
        middle = inputs + branch_attn
        ratio_ffn, normed_ffn, input_ffn = norm_forward(middle, gain_ffn)
        gathered_ffn = rows_gather(input_ffn)
        pair = cols_reduce(sliced_product(gathered_ffn, w_pair, False), query_rows)
        gate = pair[:, :hidden_width]
        upper = pair[:, hidden_width:]
        sigma = jax.nn.sigmoid(gate)
        silu_value = gate * sigma
        hidden = (silu_value * upper).astype(jnp.bfloat16)
        hidden_all = cols_gather(hidden)
        branch_ffn = rows_reduce(sliced_product(hidden_all, w_down, False), local_rows)
        output = (middle + branch_ffn).astype(jnp.bfloat16)
        cotangent_all = rows_gather(cotangent)
        hidden_grad = cols_reduce(sliced_product(cotangent_all, w_down, True), query_rows)
        grad_down = grad_down + contract_rows(hidden_all, cotangent_all)
        gate_grad = hidden_grad * upper * sigma * (1.0 + gate * (1.0 - sigma))
        upper_grad = hidden_grad * silu_value
        pair_grad = jnp.concatenate([gate_grad, upper_grad], axis=1).astype(jnp.bfloat16)
        pair_all = cols_gather(pair_grad)
        normed_ffn_grad = rows_reduce(sliced_product(pair_all, w_pair, True), local_rows)
        grad_pair = grad_pair + contract_rows(gathered_ffn, pair_all)
        middle_back, gain_ffn_step = norm_backward(normed_ffn_grad, ratio_ffn, normed_ffn, gain_ffn)
        middle_grad = cotangent.astype(jnp.float32) + middle_back
        middle_low = middle_grad.astype(jnp.bfloat16)
        middle_all = rows_gather(middle_low)
        attn_grad = cols_reduce(sliced_product(middle_all, w_out, True), query_rows).astype(
            jnp.bfloat16
        )
        grad_out = grad_out + contract_rows(attn_all, middle_all)
        attn_heads = attn_grad.reshape(query_rows, local_heads, group, HEAD)
        weight_grad = jnp.einsum(
            "ikgd,jkd->kgij", attn_heads, value_heads, preferred_element_type=jnp.float32
        )
        score_grad = (
            weights * (weight_grad - jnp.sum(weights * weight_grad, axis=-1, keepdims=True))
        ).astype(jnp.bfloat16)
        query_grad = (
            jnp.einsum("kgij,jkd->ikgd", score_grad, key_heads, preferred_element_type=jnp.float32)
            * scale
        )
        key_part = (
            jnp.einsum(
                "kgij,ikgd->jkd", score_grad, query_groups, preferred_element_type=jnp.float32
            )
            * scale
        )
        value_part = jnp.einsum(
            "kgij,ikgd->jkd", weights_low, attn_heads, preferred_element_type=jnp.float32
        )
        key_grad, value_grad = (
            lax.psum_scatter(
                key_part.reshape(block_rows, key_width).astype(jnp.bfloat16),
                "col",
                scatter_dimension=0,
                tiled=True,
            ).astype(jnp.float32),
            lax.psum_scatter(
                value_part.reshape(block_rows, key_width).astype(jnp.bfloat16),
                "col",
                scatter_dimension=0,
                tiled=True,
            ).astype(jnp.float32),
        )
        query_back = rotate_back(query_grad.reshape(query_rows, -1, HEAD), cosine, sine).reshape(
            query_rows, query_width
        )
        key_back = rotate_back(key_grad.reshape(query_rows, -1, HEAD), cosine, sine).reshape(
            query_rows, key_width
        )
        projected_grad = jnp.concatenate([query_back, key_back, value_grad], axis=1).astype(
            jnp.bfloat16
        )
        projected_all = cols_gather(projected_grad)
        normed_attn_grad = rows_reduce(sliced_product(projected_all, w_project, True), local_rows)
        grad_project = grad_project + contract_rows(gathered_attn, projected_all)
        input_back, gain_attn_step = norm_backward(
            normed_attn_grad, ratio_attn, normed_attn, gain_attn
        )
        input_grad = (middle_grad + input_back).astype(jnp.bfloat16)
        carry = (
            grad_project,
            grad_out,
            grad_pair,
            grad_down,
            grad_gain_attn + gain_attn_step,
            grad_gain_ffn + gain_ffn_step,
        )
        return (carry, (output, input_grad))

    start = (
        project_start,
        jnp.zeros(w_out.shape, jnp.float32),
        pair_start,
        down_start,
        jnp.zeros(gain_attn.shape, jnp.float32),
        jnp.zeros(gain_ffn.shape, jnp.float32),
    )
    sums, (outputs, input_grads) = lax.scan(micro_step, start, (tokens, out_grad, path, positions))
    grad_project, grad_out, grad_pair, grad_down, grad_gain_attn, grad_gain_ffn = sums
    grad_project, grad_out, grad_pair, grad_down = (
        lax.psum(grad_project.astype(jnp.bfloat16), "dp").astype(jnp.float32),
        lax.psum(grad_out.astype(jnp.bfloat16), "dp").astype(jnp.float32),
        lax.psum(grad_pair.astype(jnp.bfloat16), "dp").astype(jnp.float32),
        lax.psum(grad_down.astype(jnp.bfloat16), "dp").astype(jnp.float32),
    )
    grad_gain_attn, grad_gain_ffn = lax.psum((grad_gain_attn, grad_gain_ffn), ("dp", "row"))
    query_part = grad_project[:, :query_width]
    key_part_grad = grad_project[:, query_width : query_width + key_width]
    value_part_grad = grad_project[:, query_width + key_width :]
    return (
        outputs,
        input_grads,
        query_part,
        key_part_grad,
        value_part_grad,
        grad_out,
        grad_pair[:, :hidden_width],
        grad_pair[:, hidden_width:],
        grad_down,
        grad_gain_attn,
        grad_gain_ffn,
    )


CORE_SWAP = [(0, 1), (1, 0), (2, 3), (3, 2)]
X_SWAP = [(0, 2), (2, 0), (1, 3), (3, 1)]
COL_SWAP = [(0, 1), (1, 0)]
CROSS_SWAP = [(2 * d + j, 2 * (d ^ 1) + 1 - j) for d in range(4) for j in range(2)]
ROW_SECOND = [(0, 2), (1, 3), (2, 0), (3, 1)]
ROW_SWAP = [(0, 1), (1, 0), (2, 3), (3, 2)]
LOG2E = 1.4426950408889634
TRUNK = 1024
LEAF_BEGIN = TRUNK + 4 * 128
SHARE_OF_COST = 8
VMEM_LIMIT = 58 * 1024 * 1024
NT = (((1,), (1,)), ((), ()))
TN = (((0,), (0,)), ((), ()))
NN = (((1,), (0,)), ((), ()))


def swap_core(a):
    return lax.ppermute(a, "dp", CORE_SWAP)


def swap_x(a):
    return lax.ppermute(a, "dp", X_SWAP)


def swap_col(a):
    return lax.ppermute(a, "col", COL_SWAP)


def shift(a, pairs):
    return lax.ppermute(a, "row", pairs)


def after(value, *deps):
    return lax.optimization_barrier((value, *deps))[0]


def cost(flops, moved):
    return pl.CostEstimate(
        flops=flops // SHARE_OF_COST, bytes_accessed=moved // SHARE_OF_COST, transcendentals=0
    )


def mxu(a, b, dims):
    return lax.dot_general(a, b, dims, preferred_element_type=jnp.float32)


def low(a):
    return a.astype(jnp.bfloat16)


def wide(a):
    return a.astype(jnp.float32)


def rows_call(fn, block, row_ins, full_ins, outs, flops, name, scratch=()):
    rows = row_ins[0].shape[0]
    in_specs = [pl.BlockSpec((block, a.shape[1]), lambda i: (i, 0)) for a in row_ins]
    for a in full_ins:
        in_specs.append(
            pl.BlockSpec(
                a.shape, lambda i, nd=a.ndim: (0,) * nd, pipeline_mode=pl.Buffered(1)
            )
        )
    moved = sum(a.size * a.dtype.itemsize for a in (*row_ins, *full_ins))
    moved += sum(rows * w * jnp.dtype(dt).itemsize for w, dt in outs)
    results = pl.pallas_call(
        fn,
        grid=(rows // block,),
        in_specs=in_specs,
        out_specs=[pl.BlockSpec((block, w), lambda i: (i, 0)) for w, _ in outs],
        out_shape=[jax.ShapeDtypeStruct((rows, w), dt) for w, dt in outs],
        scratch_shapes=list(scratch),
        compiler_params=pltpu.CompilerParams(vmem_limit_bytes=VMEM_LIMIT),
        cost_estimate=cost(flops, moved),
        name=name,
    )(*row_ins, *full_ins)
    return list(results)


def turn(u, cosine, sine_signed):
    return u * cosine + pltpu.roll(u, HEAD // 2, 1) * sine_signed


def turn_back(u, cosine, sine_signed):
    return u * cosine - pltpu.roll(u, HEAD // 2, 1) * sine_signed


def project_kernel(
    x0, x1, x2, x3, cos_ref, sin_ref, gain_ref, own_ref, far_ref, xn_ref, qkv_ref, r_ref
):
    pieces = [wide(r[...]) for r in (x0, x1, x2, x3)]
    width = pieces[0].shape[1]
    total = sum(jnp.sum(p * p, axis=1, keepdims=True) for p in pieces)
    ratio = lax.rsqrt(total / (4 * width) + EPSILON)
    r_ref[...] = ratio
    for i, p in enumerate(pieces):
        cols = slice(i * width, (i + 1) * width)
        xn_ref[:, cols] = low(p * ratio * gain_ref[:, cols])
    near = xn_ref[:, : 2 * width]
    far = xn_ref[:, 2 * width :]
    cosine = cos_ref[...]
    sine = sin_ref[...]
    span = own_ref.shape[2]
    heads = span // HEAD
    for g in range(own_ref.shape[0]):
        acc = mxu(near, own_ref[g], NN) + mxu(far, far_ref[g], NN)
        for h in range(heads):
            u = acc[:, h * HEAD : (h + 1) * HEAD]
            if h < heads - 1:
                u = turn(u, cosine, sine)
            at = g * span + h * HEAD
            qkv_ref[:, at : at + HEAD] = low(u)


def segments_of(kind, trunk, leaf_begin, block):
    if kind == "branch":
        return [(0, trunk, None), (None, block, "own")]
    if kind == "leaf":
        return [(0, trunk, None), (trunk, leaf_begin - trunk, "parent"), (None, 2 * block, "own")]
    return [(0, kind, "causal")]


def attention_blocks(qb, block, trunk, leaf_begin, run):
    half = trunk // 2

    @pl.when(qb < half // block)
    def _():
        run(half, 0)

    @pl.when((qb >= half // block) & (qb < trunk // block))
    def _():
        run(trunk, 0)

    @pl.when((qb >= trunk // block) & (qb < leaf_begin // block))
    def _():
        run("branch", pl.multiple_of(qb * block, block))

    @pl.when(qb >= leaf_begin // block)
    def _():
        run("leaf", pl.multiple_of(qb * block - block, block))


def key_rows(start, window, length):
    if start is None:
        return pl.ds(window, length)
    return pl.ds(start, length)


def score_segment(s, start, window, length, mask, qb, block, lab_ref, own_row, parent_row):
    if mask is None:
        return s
    rows = s.shape[0]
    cols = s.shape[1]
    if mask == "parent":
        return jnp.where(lab_ref[key_rows(start, window, length), :] == parent_row, s, -jnp.inf)
    base = window if start is None else start
    key_at = base + lax.broadcasted_iota(jnp.int32, (rows, 1), 0)
    lane = lax.broadcasted_iota(jnp.int32, (1, cols), 1)
    query_at = qb * block + jnp.where(lane >= block, lane - block, lane)
    seen = key_at <= query_at
    if mask == "own":
        seen = seen & (lab_ref[key_rows(start, window, length), :] == own_row)
    return jnp.where(seen, s, -jnp.inf)


def attend_kernel(trunk, leaf_begin, block, q_ref, k_ref, v_ref, lab_ref, row_ref, o_ref, lse_ref, vt_ref):
    qb = pl.program_id(1)
    factor = LOG2E / math.sqrt(HEAD)

    @pl.when(qb == 0)
    def _():
        vt_ref[...] = v_ref[...].T

    queries = jnp.concatenate([q_ref[:, :HEAD], q_ref[:, HEAD:]], axis=0)
    own = row_ref[0:1, :]
    parent = row_ref[1:2, :]
    own_row = jnp.concatenate([own, own], axis=1)
    parent_row = jnp.concatenate([parent, parent], axis=1)

    def run(kind, window):
        scores = []
        segs = segments_of(kind, trunk, leaf_begin, block)
        for start, length, mask in segs:
            s = mxu(k_ref[key_rows(start, window, length), :], queries, NT)
            s = score_segment(
                s, start, window, length, mask, qb, block, lab_ref, own_row, parent_row
            )
            scores.append(s)
        top = scores[0].max(axis=0, keepdims=True)
        for s in scores[1:]:
            top = jnp.maximum(top, s.max(axis=0, keepdims=True))
        total = jnp.zeros_like(top)
        mixed = jnp.zeros((HEAD, 2 * block), jnp.float32)
        shift = top * factor
        for (start, length, mask), s in zip(segs, scores):
            p = jnp.exp2(s * factor - shift)
            total = total + p.sum(axis=0, keepdims=True)
            mixed = mixed + mxu(vt_ref[:, key_rows(start, window, length)], low(p), NN)
        lse_ref[...] = shift + jnp.log2(total)
        mixed = mixed / total
        o_ref[:, :HEAD] = low(mixed[:, :block].T)
        o_ref[:, HEAD:] = low(mixed[:, block:].T)

    attention_blocks(qb, block, trunk, leaf_begin, run)


def attend_back_kernel(
    trunk, leaf_begin, block, blocks, q_ref, k_ref, v_ref, o_ref, do_ref, lab_ref, row_ref, lse_ref,
    cos_ref, sin_ref, out_ref, kt_ref, dk_ref, dv_ref,
):
    qb = pl.program_id(1)
    scale = 1.0 / math.sqrt(HEAD)
    factor = LOG2E * scale

    @pl.when(qb == 0)
    def _():
        kt_ref[...] = k_ref[...].T
        dk_ref[...] = jnp.zeros_like(dk_ref)
        dv_ref[...] = jnp.zeros_like(dv_ref)

    queries = jnp.concatenate([q_ref[:, :HEAD], q_ref[:, HEAD:]], axis=0)
    grads = jnp.concatenate([do_ref[:, :HEAD], do_ref[:, HEAD:]], axis=0)
    outs = jnp.concatenate([o_ref[:, :HEAD], o_ref[:, HEAD:]], axis=0)
    inner = (wide(grads) * wide(outs)).T.sum(axis=0, keepdims=True)
    lse = lse_ref[...]
    own = row_ref[0:1, :]
    parent = row_ref[1:2, :]
    own_row = jnp.concatenate([own, own], axis=1)
    parent_row = jnp.concatenate([parent, parent], axis=1)
    q_rows = pl.ds(pl.multiple_of(qb * block, block), block)

    def run(kind, window):
        dq = jnp.zeros((HEAD, 2 * block), jnp.float32)
        for start, length, mask in segments_of(kind, trunk, leaf_begin, block):
            keys = key_rows(start, window, length)
            s = mxu(k_ref[keys, :], queries, NT)
            s = score_segment(
                s, start, window, length, mask, qb, block, lab_ref, own_row, parent_row
            )
            p = jnp.exp2(s * factor - lse)
            dp = mxu(v_ref[keys, :], grads, NT)
            ds = low(p * (dp - inner))
            dv_ref[keys, :] += mxu(low(p), grads, NN)
            dk_ref[keys, :] += mxu(ds, queries, NN)
            dq = dq + mxu(kt_ref[:, keys], ds, NN)
        dq = dq * scale
        cosine = cos_ref[q_rows, :]
        sine = sin_ref[q_rows, :]
        for h in range(2):
            part = dq[:, h * block : (h + 1) * block].T
            out_ref[q_rows, h * HEAD : (h + 1) * HEAD] = low(turn_back(part, cosine, sine))

    attention_blocks(qb, block, trunk, leaf_begin, run)

    @pl.when(qb == blocks - 1)
    def _():
        dk = dk_ref[...] * scale
        out_ref[:, 2 * HEAD : 3 * HEAD] = low(turn_back(dk, cos_ref[...], sin_ref[...]))
        out_ref[:, 3 * HEAD :] = low(dv_ref[...])


def attention_specs(rows, block, groups):
    q_spec = pl.BlockSpec((block, 2 * HEAD), lambda g, i: (i, 2 * g))
    k_spec = pl.BlockSpec((rows, HEAD), lambda g, i: (0, 4 * g + 2))
    v_spec = pl.BlockSpec((rows, HEAD), lambda g, i: (0, 4 * g + 3))
    lab_spec = pl.BlockSpec((rows, 1), lambda g, i: (0, 0))
    row_spec = pl.BlockSpec((8, block), lambda g, i: (0, i))
    o_spec = pl.BlockSpec((block, 2 * HEAD), lambda g, i: (i, g))
    lse_spec = pl.BlockSpec((None, None, 1, 2 * block), lambda g, i: (g, i, 0, 0))
    return q_spec, k_spec, v_spec, lab_spec, row_spec, o_spec, lse_spec


def attend(qkv, label_col, label_rows, trunk, leaf_begin, block):
    rows = qkv.shape[0]
    groups = qkv.shape[1] // (4 * HEAD)
    blocks = rows // block
    q_spec, k_spec, v_spec, lab_spec, row_spec, o_spec, lse_spec = attention_specs(rows, block, groups)
    pairs = groups * 2 * rows * rows // 2
    return pl.pallas_call(
        functools.partial(attend_kernel, trunk, leaf_begin, block),
        grid=(groups, blocks),
        in_specs=[q_spec, k_spec, v_spec, lab_spec, row_spec],
        out_specs=[o_spec, lse_spec],
        out_shape=[
            jax.ShapeDtypeStruct((rows, groups * 2 * HEAD), jnp.bfloat16),
            jax.ShapeDtypeStruct((groups, blocks, 1, 2 * block), jnp.float32),
        ],
        scratch_shapes=[pltpu.VMEM((HEAD, rows), jnp.bfloat16)],
        compiler_params=pltpu.CompilerParams(vmem_limit_bytes=VMEM_LIMIT),
        cost_estimate=cost(4 * 4 * pairs * HEAD, 20 * rows * HEAD * 2),
        name="attend",
    )(qkv, qkv, qkv, label_col, label_rows)


def attend_back(qkv, attn, attn_grad, label_col, label_rows, lse, cosine, sine, trunk, leaf_begin, block):
    rows = qkv.shape[0]
    groups = qkv.shape[1] // (4 * HEAD)
    blocks = rows // block
    q_spec, k_spec, v_spec, lab_spec, row_spec, o_spec, lse_spec = attention_specs(rows, block, groups)
    table = pl.BlockSpec((rows, HEAD), lambda g, i: (0, 0))
    pairs = groups * 2 * rows * rows // 2
    return pl.pallas_call(
        functools.partial(attend_back_kernel, trunk, leaf_begin, block, blocks),
        grid=(groups, blocks),
        in_specs=[q_spec, k_spec, v_spec, o_spec, o_spec, lab_spec, row_spec, lse_spec, table, table],
        out_specs=pl.BlockSpec((rows, 4 * HEAD), lambda g, i: (0, g)),
        out_shape=jax.ShapeDtypeStruct((rows, groups * 4 * HEAD), jnp.bfloat16),
        scratch_shapes=[
            pltpu.VMEM((HEAD, rows), jnp.bfloat16),
            pltpu.VMEM((rows, HEAD), jnp.float32),
            pltpu.VMEM((rows, HEAD), jnp.float32),
        ],
        compiler_params=pltpu.CompilerParams(vmem_limit_bytes=VMEM_LIMIT),
        cost_estimate=cost(10 * 4 * pairs * HEAD, 40 * rows * HEAD * 2),
        name="attend_back",
    )(qkv, qkv, qkv, attn, attn_grad, label_col, label_rows, lse, cosine, sine)


def quarters_out(acc, out_refs):
    width = out_refs[0].shape[1]
    for i, ref in enumerate(out_refs):
        ref[...] = low(acc[:, i * width : (i + 1) * width])


def mix_kernel(a_ref, near_ref, far_ref, *out_refs):
    groups = near_ref.shape[0]
    span = near_ref.shape[2]
    for i, out_ref in enumerate(out_refs):
        w_ref = (near_ref, far_ref)[i // 2]
        acc = sum(
            mxu(a_ref[:, g * span : (g + 1) * span], w_ref[g, i % 2], NN) for g in range(groups)
        )
        out_ref[...] = low(acc)


def sum_out_kernel(count, *refs):
    a_refs = refs[:count]
    w_refs, out_refs = refs[count:-4], refs[-4:]
    acc = None
    left = list(a_refs)
    at = 0
    for w in w_refs:
        depth = w.shape[0]
        part = mxu(left[0][:, at : at + depth], w[...], NN)
        acc = part if acc is None else acc + part
        at += depth
        if at == left[0].shape[1]:
            left.pop(0)
            at = 0
    quarters_out(acc, out_refs)


def project_back_kernel(d_ref, near_ref, far_ref, *out_refs):
    groups = near_ref.shape[0]
    span = near_ref.shape[2]
    for i, w_ref in enumerate((near_ref, far_ref)):
        acc = sum(mxu(d_ref[:, g * span : (g + 1) * span], w_ref[g], NT) for g in range(groups))
        quarters_out(acc, out_refs[2 * i : 2 * i + 2])


def attn_grad_kernel(h0, h1, h2, h3, near_ref, far_ref, out_ref):
    groups = near_ref.shape[0]
    span = near_ref.shape[2]
    for g in range(groups):
        acc = sum(
            mxu(h[...], (near_ref, far_ref)[i // 2][g, i % 2], NT)
            for i, h in enumerate((h0, h1, h2, h3))
        )
        out_ref[:, g * span : (g + 1) * span] = low(acc)


def gate_up_kernel(*refs):
    x_refs, w_refs, out_refs = refs[:4], refs[4:10], refs[10:14]
    xs_ref = refs[14]
    width = x_refs[0].shape[1]
    for i, x in enumerate(x_refs):
        xs_ref[:, i * width : (i + 1) * width] = x[...]
    normed = xs_ref[...]
    outs = list(out_refs)
    at = 0
    for w_ref in w_refs:
        for start in range(0, w_ref.shape[0], 512):
            size = min(512, w_ref.shape[0] - start)
            product = mxu(normed, w_ref[start : start + size, :], NT)
            outs[0][:, at : at + size] = low(product)
            at += size
        if at == outs[0].shape[1]:
            outs.pop(0)
            at = 0


def hidden_kernel(*refs):
    g_refs, gate_refs, up_refs, w_refs = refs[:4], refs[4:6], refs[6:8], refs[8:11]
    out_refs = refs[11:17]
    gs_ref = refs[17]
    width = g_refs[0].shape[1]
    for i, g in enumerate(g_refs):
        gs_ref[:, i * width : (i + 1) * width] = g[...]
    grads = gs_ref[...]
    unit = 256
    places = [(0, w_refs[0], i, i) for i in range(0, w_refs[0].shape[0], unit)]
    places += [(1, w_refs[1], i, i) for i in range(0, w_refs[1].shape[0], unit)]
    first = w_refs[1].shape[0]
    places += [(1, w_refs[2], i, first + i) for i in range(0, w_refs[2].shape[0], unit)]
    for side, w_ref, row, at in places:
        dgate_ref, dup_ref, hid_ref = out_refs[3 * side : 3 * side + 3]
        cols = slice(at, at + unit)
        gate = wide(gate_refs[side][:, cols])
        upper = wide(up_refs[side][:, cols])
        hidden_grad = mxu(grads, w_ref[row : row + unit, :], NT)
        sigma = jax.nn.sigmoid(gate)
        silu_value = gate * sigma
        hid_ref[:, cols] = low(silu_value * upper)
        dgate_ref[:, cols] = low(hidden_grad * upper * sigma * (1.0 + gate * (1.0 - sigma)))
        dup_ref[:, cols] = low(hidden_grad * silu_value)


def pass_kernel(where_ref, in_ref, out_ref):
    out_ref[...] = in_ref[...]


def next_blocks(gathered, z, planes):
    rows, width = gathered.shape
    unit = rows // planes
    return pl.pallas_call(
        pass_kernel,
        grid_spec=pltpu.PrefetchScalarGridSpec(
            num_scalar_prefetch=1,
            grid=(planes - 1,),
            in_specs=[pl.BlockSpec((unit, width), lambda i, w: (lax.rem(w[0] + 1 + i, planes), 0))],
            out_specs=pl.BlockSpec((unit, width), lambda i, w: (i, 0)),
        ),
        out_shape=jax.ShapeDtypeStruct((rows - unit, width), gathered.dtype),
        compiler_params=pltpu.CompilerParams(vmem_limit_bytes=VMEM_LIMIT),
        cost_estimate=cost(0, 4 * rows * width),
        name="next_blocks",
    )(z.reshape(1), gathered)


def turned_grad_kernel(count, where_ref, *refs):
    weight_grad_kernel(count, 0, *refs)


def turned_grad(a, bs, z, planes, name):
    rows, m = a.shape
    n = sum(b.shape[1] for b in bs)
    unit = m // planes
    in_specs = [
        pl.BlockSpec((rows, unit), lambda i, w: (0, lax.rem(i + planes - w[0], planes)))
    ]
    for b in bs:
        in_specs.append(
            pl.BlockSpec(b.shape, lambda i, w: (0, 0), pipeline_mode=pl.Buffered(1))
        )
    return pl.pallas_call(
        functools.partial(turned_grad_kernel, len(bs)),
        grid_spec=pltpu.PrefetchScalarGridSpec(
            num_scalar_prefetch=1,
            grid=(planes,),
            in_specs=in_specs,
            out_specs=pl.BlockSpec((unit, n), lambda i, w: (i, 0)),
        ),
        out_shape=jax.ShapeDtypeStruct((m, n), jnp.bfloat16),
        compiler_params=pltpu.CompilerParams(vmem_limit_bytes=VMEM_LIMIT),
        cost_estimate=cost(2 * rows * m * n, 2 * (rows * m + rows * n + m * n)),
        name=name,
    )(z.reshape(1), a, *bs)


def ffn_home_kernel(turned, where_ref, *refs):
    part_refs, out_ref = refs[:4], refs[4]
    step = pl.program_id(0)
    at_col, at_core, at_x = step // 4, lax.rem(step // 2, 2), lax.rem(step, 2)
    other_col = jnp.where(at_col == where_ref[0], 0, 1)
    want = 2 * jnp.where(at_x == where_ref[1], 0, 1) + jnp.where(at_core == where_ref[2], 0, 1)
    quarter = part_refs[0].shape[2] // 2
    for j in range(4):

        @pl.when(want == j)
        def _(part=part_refs[j]):
            for h in range(2):
                start = at_core * quarter if h == 0 else (1 - at_core) * quarter
                place = pl.ds(pl.multiple_of(start, quarter), quarter)
                values = wide(part[other_col, :, h * quarter : (h + 1) * quarter])
                if turned:
                    out_ref[place, :] = values.T
                else:
                    out_ref[:, place] = values


def ffn_home(where, parts, at, unit, turned, name):
    half = parts[0].shape[2]
    whole = pl.BlockSpec((2, unit, half), lambda i, w: (0, at, 0), pipeline_mode=pl.Buffered(1))
    if turned:
        spec, shape = pl.BlockSpec((half, unit), lambda i, w: (0, i)), (half, 8 * unit)
    else:
        spec, shape = pl.BlockSpec((unit, half), lambda i, w: (i, 0)), (8 * unit, half)
    return pl.pallas_call(
        functools.partial(ffn_home_kernel, turned),
        grid_spec=pltpu.PrefetchScalarGridSpec(
            num_scalar_prefetch=1, grid=(8,), in_specs=[whole] * 4, out_specs=spec
        ),
        out_shape=jax.ShapeDtypeStruct(shape, jnp.float32),
        compiler_params=pltpu.CompilerParams(vmem_limit_bytes=VMEM_LIMIT),
        cost_estimate=cost(0, 8 * unit * half * 6),
        name=name,
    )(where, *parts)


def weight_grad_kernel(count, split, *refs):
    a_ref = refs[0]
    b_refs = refs[1 : 1 + count]
    o_refs = refs[1 + count :]
    left = a_ref[...].T
    for i, b in enumerate(b_refs):
        width = b.shape[1]
        acc = low(mxu(left, b[...], NN))
        if split:
            for j in range(split):
                o_refs[0][j] = acc[:, j * width // split : (j + 1) * width // split]
        elif len(o_refs) == 1:
            o_refs[0][:, i * width : (i + 1) * width] = acc
        else:
            o_refs[i][...] = acc


def weight_grad(a, bs, block, name, joined=True, split=0):
    rows, m = a.shape
    n = sum(b.shape[1] for b in bs)
    in_specs = [pl.BlockSpec((rows, block), lambda i: (0, i))]
    for b in bs:
        in_specs.append(
            pl.BlockSpec(b.shape, lambda i: (0, 0), pipeline_mode=pl.Buffered(1))
        )
    if split:
        out_specs = [pl.BlockSpec((split, block, n // split), lambda i: (0, i, 0))]
        shapes = [(split, m, n // split)]
    else:
        widths = [n] if joined else [b.shape[1] for b in bs]
        out_specs = [pl.BlockSpec((block, w), lambda i: (i, 0)) for w in widths]
        shapes = [(m, w) for w in widths]
    outs = pl.pallas_call(
        functools.partial(weight_grad_kernel, len(bs), split),
        grid=(m // block,),
        in_specs=in_specs,
        out_specs=out_specs,
        out_shape=[jax.ShapeDtypeStruct(shape, jnp.bfloat16) for shape in shapes],
        compiler_params=pltpu.CompilerParams(vmem_limit_bytes=VMEM_LIMIT),
        cost_estimate=cost(2 * rows * m * n, 2 * (rows * m + rows * n + m * n)),
        name=name,
    )(a, *bs)
    return outs if len(outs) > 1 else outs[0]


def take(a, index, axis):
    return lax.dynamic_index_in_dim(a, index, axis, keepdims=False)


def in_order(index, mine, other, axis=0):
    first = jnp.where(index == 0, mine, other)
    second = jnp.where(index == 0, other, mine)
    return jnp.stack([first, second], axis=axis)


def spread(a):
    b = swap_col(a)
    return [a, b, swap_core(a), swap_core(b)]


def collect_core(parts):
    own, own_other, send, send_other = parts
    outgoing = low(wide(own_other) + wide(swap_core(send_other)))
    return own, swap_core(send), outgoing


def collect_col(own, got, outgoing):
    return wide(own) + wide(got) + wide(swap_col(outgoing))


def small_sum(v):
    cross = lax.ppermute(v, ("dp", "col"), CROSS_SWAP)
    return (v + swap_core(v)) + (swap_col(v) + cross)


def tree_body(
    tokens,
    out_grad,
    path,
    positions,
    w_query,
    w_key,
    w_value,
    w_out,
    w_gate,
    w_up,
    w_down,
    gain_attn,
    gain_ffn,
):
    dp = lax.axis_index("dp")
    x = dp // 2
    c = lax.rem(dp, 2)
    z = lax.axis_index("row")
    y = lax.axis_index("col")
    micro, local_rows, half = tokens.shape
    quarter = half // 2
    rows = path.shape[1]
    planes = lax.axis_size("row")
    features = 2 * half
    block = 256

    def to_trees(a):
        mine = lax.dynamic_slice_in_dim(a, c * quarter, quarter, 2)
        other = swap_core(lax.dynamic_slice_in_dim(a, (1 - c) * quarter, quarter, 2))
        return in_order(c, mine, other).reshape(planes * local_rows, quarter)

    def of_core(trees):
        trees = trees.reshape(2, micro, local_rows, quarter)
        return take(trees, c, 0), take(trees, 1 - c, 0)

    def by_feature(mine, other):
        return in_order(c, mine, swap_core(other), 2).reshape(micro, local_rows, half)

    groups = w_key.shape[1] // HEAD
    share = quarter // 2
    unit = w_gate.shape[1] // 8

    def project_piece(g):
        at = c * quarter + x * share
        return jnp.concatenate(
            [
                lax.dynamic_slice(w_query, (at, g * 2 * HEAD), (share, 2 * HEAD)),
                lax.dynamic_slice(w_key, (at, g * HEAD), (share, HEAD)),
                lax.dynamic_slice(w_value, (at, g * HEAD), (share, HEAD)),
            ],
            axis=1,
        )

    def mix_piece(g):
        return lax.dynamic_slice(w_out, ((g * 2 + x) * HEAD, c * quarter), (HEAD, quarter))

    def by_core(a):
        return jnp.where(c == 0, a, jnp.concatenate([a[:, quarter:], a[:, :quarter]], axis=1))

    def four(kept, got):
        return jnp.concatenate(
            [kept[:, :quarter], got[:, :quarter], kept[:, quarter:], got[:, quarter:]], axis=1
        )

    project_sent = project_piece(1 - y)
    project_mine = jnp.stack([project_piece(y), swap_col(project_sent)])
    trees = to_trees(tokens)
    block_in = lax.all_to_all(trees, "row", 0, 0, tiled=True)
    def hidden_piece(j, xh):
        at = ((2 * j + c) * 2 + xh) * unit
        return [
            by_core(lax.dynamic_slice_in_dim(w_gate, at, unit, 1).T),
            by_core(lax.dynamic_slice_in_dim(w_up, at, unit, 1).T),
            by_core(lax.dynamic_slice_in_dim(w_down, at, unit, 0)),
        ]

    sent = jnp.concatenate([*hidden_piece(1 - y, x), jnp.tile(mix_piece(1 - y), (1, 2))])
    got = swap_col(after(sent, project_sent))
    project_all = lax.all_gather(project_mine, "row", axis=0)

    marks = jnp.concatenate([path, positions[:, :, None]], axis=2)
    marks = jnp.transpose(marks, (2, 0, 1))
    marks = in_order(c, marks, swap_core(marks), 1).reshape(4, 2 * micro, rows)
    marks = take(marks, z, 1)
    cosine, sine = rope_tables(marks[3])
    sign = jnp.where(jnp.arange(HEAD) < HEAD // 2, -1.0, 1.0).astype(jnp.float32)
    sine = sine * sign[None, :]
    label_col = marks[0][:, None]
    label_rows = jnp.pad(marks, ((0, 4), (0, 0)))

    hidden_mine = [
        four(kept, got[i * unit : (i + 1) * unit])
        for i, kept in enumerate(hidden_piece(y, x))
    ]
    mix_mine = jnp.stack([mix_piece(y), got[3 * unit :, :quarter]])
    near_sent = jnp.concatenate(hidden_piece(1 - y, 1 - x))
    near_got = swap_col(after(near_sent, mix_mine))
    hidden_near = [
        four(kept, near_got[i * unit : (i + 1) * unit])
        for i, kept in enumerate(hidden_piece(y, 1 - x))
    ]

    def gain_order(gain):
        kept = gain.reshape(2, quarter)
        both = jnp.stack([kept, swap_col(kept)], axis=1)
        both = jnp.where(c == 0, both, both[::-1])
        return both.reshape(1, features)

    gain_attn_all = gain_order(gain_attn)
    gain_attn_own = gain_attn_all[:, :quarter]
    gain_ffn_own = lax.dynamic_slice_in_dim(gain_ffn, c * quarter, quarter, 0)[None, :]

    (
        project_all, block_in, mix_mine, gate_piece, up_piece, down_piece,
        gate_near, up_near, down_near, cosine, sine, label_col, label_rows, gain_attn_all,
    ) = lax.optimization_barrier(
        (
            project_all, block_in, mix_mine, *hidden_mine, *hidden_near,
            cosine, sine, label_col, label_rows, gain_attn_all,
        )
    )

    pieces = spread(block_in)
    mix_all = lax.all_gather(mix_mine, "row", axis=0)
    gate_mine = lax.all_gather(gate_piece, "row", axis=0, tiled=True)
    up_mine = lax.all_gather(after(up_piece, mix_all), "row", axis=0, tiled=True)
    down_mine = lax.all_gather(after(down_piece, gate_mine), "row", axis=0, tiled=True)
    gate_next, up_next, down_next = (
        next_blocks(u, z, planes) for u in (gate_mine, up_mine, down_mine)
    )
    gate_far, up_far, down_far = (swap_x(u) for u in (gate_next, up_next, down_next))

    def of_core_pairs(mine, other):
        both = in_order(x, mine, other, 2)
        pairs = both.reshape((2, planes // 2) + both.shape[1:])
        return take(pairs, c, 0), swap_core(take(pairs, 1 - c, 0))

    near, far = of_core_pairs(project_all, swap_x(project_all))
    w_near = near.reshape(groups, half, 4 * HEAD)
    w_far = far.reshape(groups, half, 4 * HEAD)

    normed_attn, qkv, ratio_attn = rows_call(
        project_kernel,
        block,
        [*pieces, cosine, sine],
        [gain_attn_all, w_near, w_far],
        [(features, jnp.bfloat16), (groups * 4 * HEAD, jnp.bfloat16), (1, jnp.float32)],
        2 * rows * features * groups * 4 * HEAD,
        "project",
    )
    near, far = of_core_pairs(mix_all, after(swap_x(mix_all), qkv))
    attn, lse = attend(after(qkv, near), label_col, label_rows, TRUNK, LEAF_BEGIN, block)
    mix_shape = (groups, 2, 2 * HEAD, quarter)
    m_near, m_far = near.reshape(mix_shape), after(far, attn).reshape(mix_shape)
    parts = rows_call(
        mix_kernel,
        2 * block,
        [attn],
        [m_near, m_far],
        [(quarter, jnp.bfloat16)] * 4,
        2 * rows * features * groups * 2 * HEAD,
        "mix",
    )
    cotangent = lax.all_to_all(to_trees(out_grad), "row", 0, 0, tiled=True)
    parts[1] = after(parts[1], cotangent, gate_next)
    own, got, outgoing = collect_core(parts)
    middle = wide(block_in) + collect_col(own, got, outgoing)
    square = small_sum(jnp.sum(middle * middle, axis=1))
    ratio_ffn = lax.rsqrt(square / features + EPSILON)[:, None]
    normed_ffn = middle * ratio_ffn
    ffn_near = after(low(normed_ffn * gain_ffn_own), up_next, gate_far)
    ffn_across = swap_col(ffn_near)
    ffn_pieces = [ffn_near, ffn_across, swap_core(ffn_near), swap_core(ffn_across)]
    grad_near, grad_across = cotangent, swap_col(after(cotangent, ffn_pieces[1]))
    gate_m, up_m, gate_o, up_o = rows_call(
        gate_up_kernel,
        block,
        ffn_pieces,
        [gate_mine, up_mine, gate_near, gate_far, up_near, up_far],
        [(planes * unit, jnp.bfloat16)] * 4,
        2 * rows * features * 4 * planes * unit,
        "gate_up",
        [pltpu.VMEM((block, features), jnp.bfloat16)],
    )
    grad_pieces = [
        grad_near,
        grad_across,
        swap_core(after(grad_near, ffn_pieces[3])),
        swap_core(after(grad_across, gate_m)),
    ]
    dgate_m, dup_m, hid_m, dgate_o, dup_o, hid_o = rows_call(
        hidden_kernel,
        block,
        [*grad_pieces, gate_m, gate_o, up_m, up_o],
        [down_mine, down_near, down_far],
        [(planes * unit, jnp.bfloat16)] * 6,
        2 * rows * features * 2 * planes * unit,
        "hidden",
        [pltpu.VMEM((block, features), jnp.bfloat16)],
    )

    def unit_grad(a, pieces_of, name, before):
        return weight_grad(after(a, before), pieces_of, 2 * block, name)

    def to_row(total):
        return lax.psum_scatter(total, "row", scatter_dimension=0, tiled=True)

    down_other = turned_grad(hid_o, grad_pieces, z, planes, "down_grad_other")
    parts = rows_call(
        functools.partial(sum_out_kernel, 4),
        2 * block,
        [after(dgate_m, down_other), dup_m, dgate_o, dup_o],
        [gate_mine, up_mine, gate_near, gate_far, up_near, up_far],
        [(quarter, jnp.bfloat16)] * 4,
        2 * rows * features * 4 * planes * unit,
        "pair_back",
    )
    gate_other = turned_grad(after(dgate_o, parts[0]), ffn_pieces, z, planes, "gate_grad_other")
    down_own = unit_grad(hid_m, grad_pieces, "down_grad_mine", gate_other)
    parts[1] = after(parts[1], down_own)
    own, got, outgoing = collect_core(parts)
    down_total = low(wide(after(down_own, outgoing)) + wide(swap_x(down_other)))
    down_sum = to_row(down_total)
    up_other = turned_grad(after(dup_o, down_total), ffn_pieces, z, planes, "up_grad_other")
    gate_own = unit_grad(dgate_m, ffn_pieces, "gate_grad_mine", up_other)
    normed_ffn_grad = collect_col(after(own, gate_own), got, outgoing)

    def norm_back(grad, ratio, normed, gain):
        scaled = grad * gain
        inner = small_sum(jnp.sum(scaled * normed, axis=1))[:, None] / features
        return ratio * (scaled - normed * inner), jnp.sum(grad * normed, axis=0)

    middle_back, gain_ffn_part = norm_back(normed_ffn_grad, ratio_ffn, normed_ffn, gain_ffn_own)
    middle_grad = wide(cotangent) + middle_back
    middle_low = low(middle_grad)
    up_own = unit_grad(dup_m, ffn_pieces, "up_grad_mine", middle_low)
    gate_total = low(wide(after(gate_own, up_own)) + wide(swap_x(gate_other)))
    gate_sum = to_row(gate_total)
    where = jnp.stack([y, x, c]).astype(jnp.int32)

    def unit_halves(total):
        kept = jnp.concatenate([total[:, :quarter], total[:, half : half + quarter]], axis=1)
        sent = jnp.concatenate([total[:, quarter:half], total[:, half + quarter :]], axis=1)
        return kept, sent

    def unit_parts(kept, sent, first, second):
        both = jnp.stack([kept, after(swap_col(sent), first)])
        over = after(swap_x(both), second)
        return [both, swap_core(both), over, swap_core(over)]

    out_parts = rows_call(
        functools.partial(sum_out_kernel, 2),
        2 * block,
        [after(hid_m, gate_total), hid_o],
        [down_mine, down_near, down_far],
        [(quarter, jnp.bfloat16)] * 4,
        2 * rows * features * 2 * planes * unit,
        "down",
    )
    middle_across = after(swap_col(middle_low), out_parts[0])
    middle_pieces = [middle_low, middle_across, swap_core(middle_low), swap_core(middle_across)]
    attn_grad = rows_call(
        attn_grad_kernel,
        2 * block,
        middle_pieces,
        [m_near, m_far],
        [(groups * 2 * HEAD, jnp.bfloat16)],
        2 * rows * features * groups * 2 * HEAD,
        "attn_grad",
    )[0]
    out_parts[1] = after(out_parts[1], attn_grad)
    out_own, out_got, out_outgoing = collect_core(out_parts)
    qkv_grad = attend_back(
        qkv, attn, after(attn_grad, out_outgoing), label_col, label_rows, lse, cosine, sine,
        TRUNK, LEAF_BEGIN, block,
    )
    output = low(after(middle, qkv_grad) + collect_col(out_own, out_got, out_outgoing))
    up_total = low(wide(after(up_own, output)) + wide(swap_x(up_other)))
    up_sum = to_row(up_total)
    parts = rows_call(
        project_back_kernel,
        2 * block,
        [after(qkv_grad, up_total)],
        [w_near, w_far],
        [(quarter, jnp.bfloat16)] * 4,
        2 * rows * features * groups * 4 * HEAD,
        "project_back",
    )
    output_tree = lax.all_to_all(output, "row", 0, 0, tiled=True)
    own, got, outgoing = collect_core(parts)
    project_grad = weight_grad(
        normed_attn, [after(qkv_grad, outgoing)], 2 * block, "project_grad", split=groups
    )
    mix_grads = weight_grad(
        attn,
        [after(middle_pieces[0], project_grad), *middle_pieces[1:]],
        groups * 2 * HEAD,
        "mix_grad",
        joined=False,
    )

    project_parts = project_grad.reshape(groups, 2, 2, 2, share, 4 * HEAD)
    mix_parts = jnp.stack([m.reshape(groups, 2, HEAD, quarter) for m in mix_grads], axis=1)
    mix_parts = mix_parts.reshape(groups, 2, 2, 2, HEAD, quarter)

    def of_x(index):
        return jnp.concatenate([take(project_parts, index, 3), take(mix_parts, index, 3)], axis=3)

    attn_sent = of_x(1 - x)
    attn_kept = of_x(after(x, attn_sent))
    normed_attn_grad = collect_col(after(own, attn_kept), got, outgoing)
    normed_attn_own = wide(block_in) * ratio_attn
    input_back, gain_attn_part = norm_back(
        normed_attn_grad, ratio_attn, normed_attn_own, gain_attn_own
    )
    input_low = low(middle_grad + input_back)
    input_tree = lax.all_to_all(input_low, "row", 0, 0, tiled=True)
    home_kept, home_sent = unit_halves(
        jnp.concatenate([after(down_sum, input_low), gate_sum])
    )
    output, output_sent = of_core(after(output_tree, home_sent))
    attn_total = low(wide(after(attn_kept, output_sent)) + wide(swap_x(attn_sent)))
    by_plane = in_order(c, attn_total[:, 0], swap_core(attn_total[:, 1]))
    by_plane = by_plane.reshape((planes,) + by_plane.shape[2:])
    attn_sum = lax.psum_scatter(by_plane, "row", scatter_dimension=0, tiled=False)
    output = by_feature(after(output, by_plane), output_sent)
    up_kept, up_sent = unit_halves(after(up_sum, output))
    home_parts = unit_parts(home_kept, home_sent, attn_total, up_sent)
    down_out = ffn_home(where, home_parts, 0, unit, False, "down_home")
    gate_out = ffn_home(where, home_parts, 1, unit, True, "gate_home")
    up_parts = unit_parts(up_kept, up_sent, home_parts[0], gate_out)
    up_out = ffn_home(where, up_parts, 0, unit, True, "up_home")
    input_grad = by_feature(*of_core(after(input_tree, up_out)))

    home = in_order(y, attn_sum[0], swap_col(attn_sum[1]))
    home = in_order(x, home, swap_x(home))
    home = in_order(c, home, swap_core(home))
    mix_home = home[:, :, :, share:]
    out_out = wide(jnp.transpose(mix_home, (2, 1, 3, 0, 4)).reshape(groups * 2 * HEAD, half))
    project_home = jnp.transpose(home[:, :, :, :share], (0, 1, 3, 2, 4))
    project_home = project_home.reshape(half, groups, 4 * HEAD)
    query_out = wide(project_home[:, :, : 2 * HEAD].reshape(half, groups * 2 * HEAD))
    key_out = wide(project_home[:, :, 2 * HEAD : 3 * HEAD].reshape(half, groups * HEAD))
    value_out = wide(project_home[:, :, 3 * HEAD :].reshape(half, groups * HEAD))

    gains = jnp.stack([gain_attn_part, gain_ffn_part])
    gains = gains + shift(gains, ROW_SECOND)
    gains = gains + shift(gains, ROW_SWAP)
    gains = gains + swap_x(gains)
    gains = in_order(c, gains, swap_core(gains), 1)
    gain_attn_out = gains[0].reshape(half)
    gain_ffn_out = gains[1].reshape(half)
    return (
        output,
        input_grad,
        query_out,
        key_out,
        value_out,
        out_out,
        gate_out,
        up_out,
        down_out,
        gain_attn_out,
        gain_ffn_out,
    )


def solution(mesh):
    in_specs = (
        P(None, ("dp", "row"), "col"),
        P(None, ("dp", "row"), "col"),
        P(None, "dp", None),
        P(None, "dp"),
        P("col", "row"),
        P("col", "row"),
        P("col", "row"),
        P("row", "col"),
        P("col", "row"),
        P("col", "row"),
        P("row", "col"),
        P("col"),
        P("col"),
    )
    out_specs = (
        P(None, ("dp", "row"), "col"),
        P(None, ("dp", "row"), "col"),
        P("col", "row"),
        P("col", "row"),
        P("col", "row"),
        P("row", "col"),
        P("col", "row"),
        P("col", "row"),
        P("row", "col"),
        P("col"),
        P("col"),
    )
    sizes = dict(mesh.shape)
    fits = sizes == {"dp": 4, "row": 4, "col": 2}
    chosen = tree_body if fits else body
    return jax.shard_map(chosen, mesh=mesh, in_specs=in_specs, out_specs=out_specs, check_vma=False)
```

```python
import functools
import math

import jax
import jax.numpy as jnp
from jax import lax
from jax.experimental import pallas as pl
from jax.experimental.pallas import tpu as pltpu
from jax.sharding import PartitionSpec as P

D = 2048
HEADS = 16
KV_HEADS = 8
HEAD = 128


EPSILON = 1e-05
THETA = 1000000.0


def contract_rows(left, right):
    return lax.dot_general(
        left, right, (((0,), (0,)), ((), ())), preferred_element_type=jnp.float32
    )


def contract_cols(left, right):
    return lax.dot_general(
        left, right, (((1,), (1,)), ((), ())), preferred_element_type=jnp.float32
    )


def rows_gather(values):
    return lax.all_gather(values, "row", axis=0, tiled=True)


def cols_gather(values):
    return lax.all_gather(values, "col", axis=0, tiled=True)


def cols_reduce(part_fn, rows):
    return lax.psum_scatter(
        part_fn(jnp.int32(0), rows * lax.axis_size("col")), "col", scatter_dimension=0, tiled=True
    )


def rows_reduce(part_fn, rows):
    return lax.psum_scatter(
        part_fn(jnp.int32(0), rows * lax.axis_size("row")).astype(jnp.bfloat16),
        "row",
        scatter_dimension=0,
        tiled=True,
    ).astype(jnp.float32)


def feature_sums(values):
    return lax.psum(jnp.sum(values, axis=1), "col")


def sliced_product(whole, weight, transpose):

    def part_fn(start, count):
        if transpose:
            return contract_cols(whole, weight)
        return jnp.dot(whole, weight, preferred_element_type=jnp.float32)

    return part_fn


def rope_tables(positions):
    half = HEAD // 2
    frequency = jnp.power(THETA, -2.0 * jnp.arange(half, dtype=jnp.float32) / HEAD)
    angles = positions.astype(jnp.float32)[:, None] * frequency[None, :]
    angles = jnp.concatenate([angles, angles], axis=1)
    return (jnp.cos(angles), jnp.sin(angles))


def rotate(values, cosine, sine):
    half = values.shape[-1] // 2
    turned = jnp.concatenate([-values[..., half:], values[..., :half]], axis=-1)
    return values * cosine[:, None, :] + turned * sine[:, None, :]


def rotate_back(grads, cosine, sine):
    half = grads.shape[-1] // 2
    scaled = grads * sine[:, None, :]
    turned = jnp.concatenate([scaled[..., half:], -scaled[..., :half]], axis=-1)
    return grads * cosine[:, None, :] + turned


def norm_forward(values, gain):
    ratio = lax.rsqrt(feature_sums(values * values) / D + EPSILON)[:, None]
    normed = values * ratio
    return (ratio, normed, (normed * gain).astype(jnp.bfloat16))


def norm_backward(grad, ratio, normed, gain):
    scaled = grad * gain
    inner = feature_sums(scaled * normed)[:, None] / D
    return (ratio * (scaled - normed * inner), jnp.sum(grad * normed, axis=0))


def body(
    tokens,
    out_grad,
    path,
    positions,
    w_query,
    w_key,
    w_value,
    w_out,
    w_gate,
    w_up,
    w_down,
    gain_attn,
    gain_ffn,
):
    query_width = w_query.shape[1]
    key_width = w_key.shape[1]
    hidden_width = w_gate.shape[1]
    local_heads = key_width // HEAD
    group = HEADS // KV_HEADS
    scale = 1.0 / math.sqrt(HEAD)
    block_rows = path.shape[1]
    local_rows = tokens.shape[1]
    query_rows = block_rows // lax.axis_size("col")
    first = lax.axis_index("col") * query_rows
    w_project = jnp.concatenate([w_query, w_key, w_value], axis=1)
    w_pair = jnp.concatenate([w_gate, w_up], axis=1)
    project_start = jnp.zeros(w_project.shape, jnp.float32)
    pair_start = jnp.zeros(w_pair.shape, jnp.float32)
    down_start = jnp.zeros(w_down.shape, jnp.float32)

    def micro_step(carry, batch):
        grad_project, grad_out, grad_pair, grad_down, grad_gain_attn, grad_gain_ffn = carry
        block, cotangent, block_path, block_place = batch
        inputs = block.astype(jnp.float32)
        cosine, sine = rope_tables(lax.dynamic_slice_in_dim(block_place, first, query_rows, 0))
        query_path = lax.dynamic_slice_in_dim(block_path, first, query_rows, 0)
        key_labels = block_path[:, 0]
        query_place = first + jnp.arange(query_rows, dtype=jnp.int32)
        key_place = jnp.arange(block_rows, dtype=jnp.int32)
        same_path = (
            (key_labels[None, :] == query_path[:, 0:1])
            | (key_labels[None, :] == query_path[:, 1:2])
            | (key_labels[None, :] == query_path[:, 2:3])
        )
        visible = same_path & (key_place[None, :] <= query_place[:, None])
        ratio_attn, normed_attn, input_attn = norm_forward(inputs, gain_attn)
        gathered_attn = rows_gather(input_attn)
        projected = cols_reduce(sliced_product(gathered_attn, w_project, False), query_rows)
        query = rotate(
            projected[:, :query_width].reshape(query_rows, -1, HEAD), cosine, sine
        ).astype(jnp.bfloat16)
        keys = rotate(
            projected[:, query_width : query_width + key_width].reshape(query_rows, -1, HEAD),
            cosine,
            sine,
        ).astype(jnp.bfloat16)
        values = projected[:, query_width + key_width :].astype(jnp.bfloat16)
        keys_all, values_all = (
            lax.all_gather(keys.reshape(query_rows, key_width), "col", axis=0, tiled=True),
            lax.all_gather(values, "col", axis=0, tiled=True),
        )
        query_groups = query.reshape(query_rows, local_heads, group, HEAD)
        key_heads = keys_all.reshape(block_rows, local_heads, HEAD)
        value_heads = values_all.reshape(block_rows, local_heads, HEAD)
        scores = (
            jnp.einsum(
                "ikgd,jkd->kgij", query_groups, key_heads, preferred_element_type=jnp.float32
            )
            * scale
        )
        scores = jnp.where(visible[None, None], scores, -jnp.inf)
        weights = jax.nn.softmax(scores, axis=-1)
        weights_low = weights.astype(jnp.bfloat16)
        mixed = jnp.einsum(
            "kgij,jkd->ikgd", weights_low, value_heads, preferred_element_type=jnp.float32
        )
        attn_low = mixed.reshape(query_rows, query_width).astype(jnp.bfloat16)
        attn_all = cols_gather(attn_low)
        branch_attn = rows_reduce(sliced_product(attn_all, w_out, False), local_rows)
        middle = inputs + branch_attn
        ratio_ffn, normed_ffn, input_ffn = norm_forward(middle, gain_ffn)
        gathered_ffn = rows_gather(input_ffn)
        pair = cols_reduce(sliced_product(gathered_ffn, w_pair, False), query_rows)
        gate = pair[:, :hidden_width]
        upper = pair[:, hidden_width:]
        sigma = jax.nn.sigmoid(gate)
        silu_value = gate * sigma
        hidden = (silu_value * upper).astype(jnp.bfloat16)
        hidden_all = cols_gather(hidden)
        branch_ffn = rows_reduce(sliced_product(hidden_all, w_down, False), local_rows)
        output = (middle + branch_ffn).astype(jnp.bfloat16)
        cotangent_all = rows_gather(cotangent)
        hidden_grad = cols_reduce(sliced_product(cotangent_all, w_down, True), query_rows)
        grad_down = grad_down + contract_rows(hidden_all, cotangent_all)
        gate_grad = hidden_grad * upper * sigma * (1.0 + gate * (1.0 - sigma))
        upper_grad = hidden_grad * silu_value
        pair_grad = jnp.concatenate([gate_grad, upper_grad], axis=1).astype(jnp.bfloat16)
        pair_all = cols_gather(pair_grad)
        normed_ffn_grad = rows_reduce(sliced_product(pair_all, w_pair, True), local_rows)
        grad_pair = grad_pair + contract_rows(gathered_ffn, pair_all)
        middle_back, gain_ffn_step = norm_backward(normed_ffn_grad, ratio_ffn, normed_ffn, gain_ffn)
        middle_grad = cotangent.astype(jnp.float32) + middle_back
        middle_low = middle_grad.astype(jnp.bfloat16)
        middle_all = rows_gather(middle_low)
        attn_grad = cols_reduce(sliced_product(middle_all, w_out, True), query_rows).astype(
            jnp.bfloat16
        )
        grad_out = grad_out + contract_rows(attn_all, middle_all)
        attn_heads = attn_grad.reshape(query_rows, local_heads, group, HEAD)
        weight_grad = jnp.einsum(
            "ikgd,jkd->kgij", attn_heads, value_heads, preferred_element_type=jnp.float32
        )
        score_grad = (
            weights * (weight_grad - jnp.sum(weights * weight_grad, axis=-1, keepdims=True))
        ).astype(jnp.bfloat16)
        query_grad = (
            jnp.einsum("kgij,jkd->ikgd", score_grad, key_heads, preferred_element_type=jnp.float32)
            * scale
        )
        key_part = (
            jnp.einsum(
                "kgij,ikgd->jkd", score_grad, query_groups, preferred_element_type=jnp.float32
            )
            * scale
        )
        value_part = jnp.einsum(
            "kgij,ikgd->jkd", weights_low, attn_heads, preferred_element_type=jnp.float32
        )
        key_grad, value_grad = (
            lax.psum_scatter(
                key_part.reshape(block_rows, key_width).astype(jnp.bfloat16),
                "col",
                scatter_dimension=0,
                tiled=True,
            ).astype(jnp.float32),
            lax.psum_scatter(
                value_part.reshape(block_rows, key_width).astype(jnp.bfloat16),
                "col",
                scatter_dimension=0,
                tiled=True,
            ).astype(jnp.float32),
        )
        query_back = rotate_back(query_grad.reshape(query_rows, -1, HEAD), cosine, sine).reshape(
            query_rows, query_width
        )
        key_back = rotate_back(key_grad.reshape(query_rows, -1, HEAD), cosine, sine).reshape(
            query_rows, key_width
        )
        projected_grad = jnp.concatenate([query_back, key_back, value_grad], axis=1).astype(
            jnp.bfloat16
        )
        projected_all = cols_gather(projected_grad)
        normed_attn_grad = rows_reduce(sliced_product(projected_all, w_project, True), local_rows)
        grad_project = grad_project + contract_rows(gathered_attn, projected_all)
        input_back, gain_attn_step = norm_backward(
            normed_attn_grad, ratio_attn, normed_attn, gain_attn
        )
        input_grad = (middle_grad + input_back).astype(jnp.bfloat16)
        carry = (
            grad_project,
            grad_out,
            grad_pair,
            grad_down,
            grad_gain_attn + gain_attn_step,
            grad_gain_ffn + gain_ffn_step,
        )
        return (carry, (output, input_grad))

    start = (
        project_start,
        jnp.zeros(w_out.shape, jnp.float32),
        pair_start,
        down_start,
        jnp.zeros(gain_attn.shape, jnp.float32),
        jnp.zeros(gain_ffn.shape, jnp.float32),
    )
    sums, (outputs, input_grads) = lax.scan(micro_step, start, (tokens, out_grad, path, positions))
    grad_project, grad_out, grad_pair, grad_down, grad_gain_attn, grad_gain_ffn = sums
    grad_project, grad_out, grad_pair, grad_down = (
        lax.psum(grad_project.astype(jnp.bfloat16), "dp").astype(jnp.float32),
        lax.psum(grad_out.astype(jnp.bfloat16), "dp").astype(jnp.float32),
        lax.psum(grad_pair.astype(jnp.bfloat16), "dp").astype(jnp.float32),
        lax.psum(grad_down.astype(jnp.bfloat16), "dp").astype(jnp.float32),
    )
    grad_gain_attn, grad_gain_ffn = lax.psum((grad_gain_attn, grad_gain_ffn), ("dp", "row"))
    query_part = grad_project[:, :query_width]
    key_part_grad = grad_project[:, query_width : query_width + key_width]
    value_part_grad = grad_project[:, query_width + key_width :]
    return (
        outputs,
        input_grads,
        query_part,
        key_part_grad,
        value_part_grad,
        grad_out,
        grad_pair[:, :hidden_width],
        grad_pair[:, hidden_width:],
        grad_down,
        grad_gain_attn,
        grad_gain_ffn,
    )


CORE_SWAP = [(0, 1), (1, 0), (2, 3), (3, 2)]
X_SWAP = [(0, 2), (2, 0), (1, 3), (3, 1)]
COL_SWAP = [(0, 1), (1, 0)]
CROSS_SWAP = [(2 * d + j, 2 * (d ^ 1) + 1 - j) for d in range(4) for j in range(2)]
ROW_SECOND = [(0, 2), (1, 3), (2, 0), (3, 1)]
ROW_SWAP = [(0, 1), (1, 0), (2, 3), (3, 2)]
LOG2E = 1.4426950408889634
TRUNK = 1024
LEAF_BEGIN = TRUNK + 4 * 128
SHARE_OF_COST = 8
VMEM_LIMIT = 58 * 1024 * 1024
NT = (((1,), (1,)), ((), ()))
TN = (((0,), (0,)), ((), ()))
NN = (((1,), (0,)), ((), ()))


def swap_core(a):
    return lax.ppermute(a, "dp", CORE_SWAP)


def swap_x(a):
    return lax.ppermute(a, "dp", X_SWAP)


def swap_col(a):
    return lax.ppermute(a, "col", COL_SWAP)


def shift(a, pairs):
    return lax.ppermute(a, "row", pairs)


def after(value, *deps):
    return lax.optimization_barrier((value, *deps))[0]


def cost(flops, moved):
    return pl.CostEstimate(
        flops=flops // SHARE_OF_COST, bytes_accessed=moved // SHARE_OF_COST, transcendentals=0
    )


def mxu(a, b, dims):
    return lax.dot_general(a, b, dims, preferred_element_type=jnp.float32)


def low(a):
    return a.astype(jnp.bfloat16)


def wide(a):
    return a.astype(jnp.float32)


def rows_call(fn, block, row_ins, full_ins, outs, flops, name, scratch=()):
    rows = row_ins[0].shape[0]
    in_specs = [pl.BlockSpec((block, a.shape[1]), lambda i: (i, 0)) for a in row_ins]
    for a in full_ins:
        in_specs.append(
            pl.BlockSpec(
                a.shape, lambda i, nd=a.ndim: (0,) * nd, pipeline_mode=pl.Buffered(1)
            )
        )
    moved = sum(a.size * a.dtype.itemsize for a in (*row_ins, *full_ins))
    moved += sum(rows * w * jnp.dtype(dt).itemsize for w, dt in outs)
    results = pl.pallas_call(
        fn,
        grid=(rows // block,),
        in_specs=in_specs,
        out_specs=[pl.BlockSpec((block, w), lambda i: (i, 0)) for w, _ in outs],
        out_shape=[jax.ShapeDtypeStruct((rows, w), dt) for w, dt in outs],
        scratch_shapes=list(scratch),
        compiler_params=pltpu.CompilerParams(vmem_limit_bytes=VMEM_LIMIT),
        cost_estimate=cost(flops, moved),
        name=name,
    )(*row_ins, *full_ins)
    return list(results)


def turn(u, cosine, sine_signed):
    return u * cosine + pltpu.roll(u, HEAD // 2, 1) * sine_signed


def turn_back(u, cosine, sine_signed):
    return u * cosine - pltpu.roll(u, HEAD // 2, 1) * sine_signed


def project_kernel(
    x0, x1, x2, x3, cos_ref, sin_ref, gain_ref, own_ref, far_ref, xn_ref, qkv_ref, r_ref
):
    pieces = [wide(r[...]) for r in (x0, x1, x2, x3)]
    width = pieces[0].shape[1]
    total = sum(jnp.sum(p * p, axis=1, keepdims=True) for p in pieces)
    ratio = lax.rsqrt(total / (4 * width) + EPSILON)
    r_ref[...] = ratio
    for i, p in enumerate(pieces):
        cols = slice(i * width, (i + 1) * width)
        xn_ref[:, cols] = low(p * ratio * gain_ref[:, cols])
    near = xn_ref[:, : 2 * width]
    far = xn_ref[:, 2 * width :]
    cosine = cos_ref[...]
    sine = sin_ref[...]
    span = own_ref.shape[2]
    heads = span // HEAD
    for g in range(own_ref.shape[0]):
        acc = mxu(near, own_ref[g], NN) + mxu(far, far_ref[g], NN)
        for h in range(heads):
            u = acc[:, h * HEAD : (h + 1) * HEAD]
            if h < heads - 1:
                u = turn(u, cosine, sine)
            at = g * span + h * HEAD
            qkv_ref[:, at : at + HEAD] = low(u)


def segments_of(kind, trunk, leaf_begin, block):
    if kind == "branch":
        return [(0, trunk, None), (None, block, "own")]
    if kind == "leaf":
        return [(0, trunk, None), (trunk, leaf_begin - trunk, "parent"), (None, 2 * block, "own")]
    return [(0, kind, "causal")]


def attention_blocks(qb, block, trunk, leaf_begin, run):
    half = trunk // 2

    @pl.when(qb < half // block)
    def _():
        run(half, 0)

    @pl.when((qb >= half // block) & (qb < trunk // block))
    def _():
        run(trunk, 0)

    @pl.when((qb >= trunk // block) & (qb < leaf_begin // block))
    def _():
        run("branch", pl.multiple_of(qb * block, block))

    @pl.when(qb >= leaf_begin // block)
    def _():
        run("leaf", pl.multiple_of(qb * block - block, block))


def key_rows(start, window, length):
    if start is None:
        return pl.ds(window, length)
    return pl.ds(start, length)


def score_segment(s, start, window, length, mask, qb, block, lab_ref, own_row, parent_row):
    if mask is None:
        return s
    rows = s.shape[0]
    cols = s.shape[1]
    if mask == "parent":
        return jnp.where(lab_ref[key_rows(start, window, length), :] == parent_row, s, -jnp.inf)
    base = window if start is None else start
    key_at = base + lax.broadcasted_iota(jnp.int32, (rows, 1), 0)
    lane = lax.broadcasted_iota(jnp.int32, (1, cols), 1)
    query_at = qb * block + jnp.where(lane >= block, lane - block, lane)
    seen = key_at <= query_at
    if mask == "own":
        seen = seen & (lab_ref[key_rows(start, window, length), :] == own_row)
    return jnp.where(seen, s, -jnp.inf)


def attend_kernel(trunk, leaf_begin, block, q_ref, k_ref, v_ref, lab_ref, row_ref, o_ref, lse_ref, vt_ref):
    qb = pl.program_id(1)
    factor = LOG2E / math.sqrt(HEAD)

    @pl.when(qb == 0)
    def _():
        vt_ref[...] = v_ref[...].T

    queries = jnp.concatenate([q_ref[:, :HEAD], q_ref[:, HEAD:]], axis=0)
    own = row_ref[0:1, :]
    parent = row_ref[1:2, :]
    own_row = jnp.concatenate([own, own], axis=1)
    parent_row = jnp.concatenate([parent, parent], axis=1)

    def run(kind, window):
        scores = []
        segs = segments_of(kind, trunk, leaf_begin, block)
        for start, length, mask in segs:
            s = mxu(k_ref[key_rows(start, window, length), :], queries, NT)
            s = score_segment(
                s, start, window, length, mask, qb, block, lab_ref, own_row, parent_row
            )
            scores.append(s)
        top = scores[0].max(axis=0, keepdims=True)
        for s in scores[1:]:
            top = jnp.maximum(top, s.max(axis=0, keepdims=True))
        total = jnp.zeros_like(top)
        mixed = jnp.zeros((HEAD, 2 * block), jnp.float32)
        shift = top * factor
        for (start, length, mask), s in zip(segs, scores):
            p = jnp.exp2(s * factor - shift)
            total = total + p.sum(axis=0, keepdims=True)
            mixed = mixed + mxu(vt_ref[:, key_rows(start, window, length)], low(p), NN)
        lse_ref[...] = shift + jnp.log2(total)
        mixed = mixed / total
        o_ref[:, :HEAD] = low(mixed[:, :block].T)
        o_ref[:, HEAD:] = low(mixed[:, block:].T)

    attention_blocks(qb, block, trunk, leaf_begin, run)


def attend_back_kernel(
    trunk, leaf_begin, block, blocks, q_ref, k_ref, v_ref, o_ref, do_ref, lab_ref, row_ref, lse_ref,
    cos_ref, sin_ref, out_ref, kt_ref, dk_ref, dv_ref,
):
    qb = pl.program_id(1)
    scale = 1.0 / math.sqrt(HEAD)
    factor = LOG2E * scale

    @pl.when(qb == 0)
    def _():
        kt_ref[...] = k_ref[...].T
        dk_ref[...] = jnp.zeros_like(dk_ref)
        dv_ref[...] = jnp.zeros_like(dv_ref)

    queries = jnp.concatenate([q_ref[:, :HEAD], q_ref[:, HEAD:]], axis=0)
    grads = jnp.concatenate([do_ref[:, :HEAD], do_ref[:, HEAD:]], axis=0)
    outs = jnp.concatenate([o_ref[:, :HEAD], o_ref[:, HEAD:]], axis=0)
    inner = (wide(grads) * wide(outs)).T.sum(axis=0, keepdims=True)
    lse = lse_ref[...]
    own = row_ref[0:1, :]
    parent = row_ref[1:2, :]
    own_row = jnp.concatenate([own, own], axis=1)
    parent_row = jnp.concatenate([parent, parent], axis=1)
    q_rows = pl.ds(pl.multiple_of(qb * block, block), block)

    def run(kind, window):
        dq = jnp.zeros((HEAD, 2 * block), jnp.float32)
        for start, length, mask in segments_of(kind, trunk, leaf_begin, block):
            keys = key_rows(start, window, length)
            s = mxu(k_ref[keys, :], queries, NT)
            s = score_segment(
                s, start, window, length, mask, qb, block, lab_ref, own_row, parent_row
            )
            p = jnp.exp2(s * factor - lse)
            dp = mxu(v_ref[keys, :], grads, NT)
            ds = low(p * (dp - inner))
            dv_ref[keys, :] += mxu(low(p), grads, NN)
            dk_ref[keys, :] += mxu(ds, queries, NN)
            dq = dq + mxu(kt_ref[:, keys], ds, NN)
        dq = dq * scale
        cosine = cos_ref[q_rows, :]
        sine = sin_ref[q_rows, :]
        for h in range(2):
            part = dq[:, h * block : (h + 1) * block].T
            out_ref[q_rows, h * HEAD : (h + 1) * HEAD] = low(turn_back(part, cosine, sine))

    attention_blocks(qb, block, trunk, leaf_begin, run)

    @pl.when(qb == blocks - 1)
    def _():
        dk = dk_ref[...] * scale
        out_ref[:, 2 * HEAD : 3 * HEAD] = low(turn_back(dk, cos_ref[...], sin_ref[...]))
        out_ref[:, 3 * HEAD :] = low(dv_ref[...])


def attention_specs(rows, block, groups):
    q_spec = pl.BlockSpec((block, 2 * HEAD), lambda g, i: (i, 2 * g))
    k_spec = pl.BlockSpec((rows, HEAD), lambda g, i: (0, 4 * g + 2))
    v_spec = pl.BlockSpec((rows, HEAD), lambda g, i: (0, 4 * g + 3))
    lab_spec = pl.BlockSpec((rows, 1), lambda g, i: (0, 0))
    row_spec = pl.BlockSpec((8, block), lambda g, i: (0, i))
    o_spec = pl.BlockSpec((block, 2 * HEAD), lambda g, i: (i, g))
    lse_spec = pl.BlockSpec((None, None, 1, 2 * block), lambda g, i: (g, i, 0, 0))
    return q_spec, k_spec, v_spec, lab_spec, row_spec, o_spec, lse_spec


def attend(qkv, label_col, label_rows, trunk, leaf_begin, block):
    rows = qkv.shape[0]
    groups = qkv.shape[1] // (4 * HEAD)
    blocks = rows // block
    q_spec, k_spec, v_spec, lab_spec, row_spec, o_spec, lse_spec = attention_specs(rows, block, groups)
    pairs = groups * 2 * rows * rows // 2
    return pl.pallas_call(
        functools.partial(attend_kernel, trunk, leaf_begin, block),
        grid=(groups, blocks),
        in_specs=[q_spec, k_spec, v_spec, lab_spec, row_spec],
        out_specs=[o_spec, lse_spec],
        out_shape=[
            jax.ShapeDtypeStruct((rows, groups * 2 * HEAD), jnp.bfloat16),
            jax.ShapeDtypeStruct((groups, blocks, 1, 2 * block), jnp.float32),
        ],
        scratch_shapes=[pltpu.VMEM((HEAD, rows), jnp.bfloat16)],
        compiler_params=pltpu.CompilerParams(vmem_limit_bytes=VMEM_LIMIT),
        cost_estimate=cost(4 * 4 * pairs * HEAD, 20 * rows * HEAD * 2),
        name="attend",
    )(qkv, qkv, qkv, label_col, label_rows)


def attend_back(qkv, attn, attn_grad, label_col, label_rows, lse, cosine, sine, trunk, leaf_begin, block):
    rows = qkv.shape[0]
    groups = qkv.shape[1] // (4 * HEAD)
    blocks = rows // block
    q_spec, k_spec, v_spec, lab_spec, row_spec, o_spec, lse_spec = attention_specs(rows, block, groups)
    table = pl.BlockSpec((rows, HEAD), lambda g, i: (0, 0))
    pairs = groups * 2 * rows * rows // 2
    return pl.pallas_call(
        functools.partial(attend_back_kernel, trunk, leaf_begin, block, blocks),
        grid=(groups, blocks),
        in_specs=[q_spec, k_spec, v_spec, o_spec, o_spec, lab_spec, row_spec, lse_spec, table, table],
        out_specs=pl.BlockSpec((rows, 4 * HEAD), lambda g, i: (0, g)),
        out_shape=jax.ShapeDtypeStruct((rows, groups * 4 * HEAD), jnp.bfloat16),
        scratch_shapes=[
            pltpu.VMEM((HEAD, rows), jnp.bfloat16),
            pltpu.VMEM((rows, HEAD), jnp.float32),
            pltpu.VMEM((rows, HEAD), jnp.float32),
        ],
        compiler_params=pltpu.CompilerParams(vmem_limit_bytes=VMEM_LIMIT),
        cost_estimate=cost(10 * 4 * pairs * HEAD, 40 * rows * HEAD * 2),
        name="attend_back",
    )(qkv, qkv, qkv, attn, attn_grad, label_col, label_rows, lse, cosine, sine)


def quarters_out(acc, out_refs):
    width = out_refs[0].shape[1]
    for i, ref in enumerate(out_refs):
        ref[...] = low(acc[:, i * width : (i + 1) * width])


def mix_kernel(a_ref, near_ref, far_ref, *out_refs):
    groups = near_ref.shape[0]
    span = near_ref.shape[2]
    for i, out_ref in enumerate(out_refs):
        w_ref = (near_ref, far_ref)[i // 2]
        acc = sum(
            mxu(a_ref[:, g * span : (g + 1) * span], w_ref[g, i % 2], NN) for g in range(groups)
        )
        out_ref[...] = low(acc)


def sum_out_kernel(count, *refs):
    a_refs = refs[:count]
    w_refs, out_refs = refs[count:-4], refs[-4:]
    acc = None
    left = list(a_refs)
    at = 0
    for w in w_refs:
        depth = w.shape[0]
        part = mxu(left[0][:, at : at + depth], w[...], NN)
        acc = part if acc is None else acc + part
        at += depth
        if at == left[0].shape[1]:
            left.pop(0)
            at = 0
    quarters_out(acc, out_refs)


def project_back_kernel(d_ref, near_ref, far_ref, *out_refs):
    groups = near_ref.shape[0]
    span = near_ref.shape[2]
    for i, w_ref in enumerate((near_ref, far_ref)):
        acc = sum(mxu(d_ref[:, g * span : (g + 1) * span], w_ref[g], NT) for g in range(groups))
        quarters_out(acc, out_refs[2 * i : 2 * i + 2])


def attn_grad_kernel(h0, h1, h2, h3, near_ref, far_ref, out_ref):
    groups = near_ref.shape[0]
    span = near_ref.shape[2]
    for g in range(groups):
        acc = sum(
            mxu(h[...], (near_ref, far_ref)[i // 2][g, i % 2], NT)
            for i, h in enumerate((h0, h1, h2, h3))
        )
        out_ref[:, g * span : (g + 1) * span] = low(acc)


def gate_up_kernel(*refs):
    x_refs, w_refs, out_refs = refs[:4], refs[4:10], refs[10:14]
    xs_ref = refs[14]
    width = x_refs[0].shape[1]
    for i, x in enumerate(x_refs):
        xs_ref[:, i * width : (i + 1) * width] = x[...]
    normed = xs_ref[...]
    outs = list(out_refs)
    at = 0
    for w_ref in w_refs:
        for start in range(0, w_ref.shape[0], 512):
            size = min(512, w_ref.shape[0] - start)
            product = mxu(normed, w_ref[start : start + size, :], NT)
            outs[0][:, at : at + size] = low(product)
            at += size
        if at == outs[0].shape[1]:
            outs.pop(0)
            at = 0


def hidden_kernel(*refs):
    g_refs, gate_refs, up_refs, w_refs = refs[:4], refs[4:6], refs[6:8], refs[8:11]
    out_refs = refs[11:17]
    gs_ref = refs[17]
    width = g_refs[0].shape[1]
    for i, g in enumerate(g_refs):
        gs_ref[:, i * width : (i + 1) * width] = g[...]
    grads = gs_ref[...]
    unit = 256
    places = [(0, w_refs[0], i, i) for i in range(0, w_refs[0].shape[0], unit)]
    places += [(1, w_refs[1], i, i) for i in range(0, w_refs[1].shape[0], unit)]
    first = w_refs[1].shape[0]
    places += [(1, w_refs[2], i, first + i) for i in range(0, w_refs[2].shape[0], unit)]
    for side, w_ref, row, at in places:
        dgate_ref, dup_ref, hid_ref = out_refs[3 * side : 3 * side + 3]
        cols = slice(at, at + unit)
        gate = wide(gate_refs[side][:, cols])
        upper = wide(up_refs[side][:, cols])
        hidden_grad = mxu(grads, w_ref[row : row + unit, :], NT)
        sigma = jax.nn.sigmoid(gate)
        silu_value = gate * sigma
        hid_ref[:, cols] = low(silu_value * upper)
        dgate_ref[:, cols] = low(hidden_grad * upper * sigma * (1.0 + gate * (1.0 - sigma)))
        dup_ref[:, cols] = low(hidden_grad * silu_value)


def pass_kernel(where_ref, in_ref, out_ref):
    out_ref[...] = in_ref[...]


def next_blocks(gathered, z, planes):
    rows, width = gathered.shape
    unit = rows // planes
    return pl.pallas_call(
        pass_kernel,
        grid_spec=pltpu.PrefetchScalarGridSpec(
            num_scalar_prefetch=1,
            grid=(planes - 1,),
            in_specs=[pl.BlockSpec((unit, width), lambda i, w: (lax.rem(w[0] + 1 + i, planes), 0))],
            out_specs=pl.BlockSpec((unit, width), lambda i, w: (i, 0)),
        ),
        out_shape=jax.ShapeDtypeStruct((rows - unit, width), gathered.dtype),
        compiler_params=pltpu.CompilerParams(vmem_limit_bytes=VMEM_LIMIT),
        cost_estimate=cost(0, 4 * rows * width),
        name="next_blocks",
    )(z.reshape(1), gathered)


def turned_grad_kernel(count, where_ref, *refs):
    weight_grad_kernel(count, 0, *refs)


def turned_grad(a, bs, z, planes, name):
    rows, m = a.shape
    n = sum(b.shape[1] for b in bs)
    unit = m // planes
    in_specs = [
        pl.BlockSpec((rows, unit), lambda i, w: (0, lax.rem(i + planes - w[0], planes)))
    ]
    for b in bs:
        in_specs.append(
            pl.BlockSpec(b.shape, lambda i, w: (0, 0), pipeline_mode=pl.Buffered(1))
        )
    return pl.pallas_call(
        functools.partial(turned_grad_kernel, len(bs)),
        grid_spec=pltpu.PrefetchScalarGridSpec(
            num_scalar_prefetch=1,
            grid=(planes,),
            in_specs=in_specs,
            out_specs=pl.BlockSpec((unit, n), lambda i, w: (i, 0)),
        ),
        out_shape=jax.ShapeDtypeStruct((m, n), jnp.bfloat16),
        compiler_params=pltpu.CompilerParams(vmem_limit_bytes=VMEM_LIMIT),
        cost_estimate=cost(2 * rows * m * n, 2 * (rows * m + rows * n + m * n)),
        name=name,
    )(z.reshape(1), a, *bs)


def ffn_home_kernel(turned, where_ref, *refs):
    part_refs, out_ref = refs[:4], refs[4]
    step = pl.program_id(0)
    at_col, at_core, at_x = step // 4, lax.rem(step // 2, 2), lax.rem(step, 2)
    other_col = jnp.where(at_col == where_ref[0], 0, 1)
    want = 2 * jnp.where(at_x == where_ref[1], 0, 1) + jnp.where(at_core == where_ref[2], 0, 1)
    quarter = part_refs[0].shape[2] // 2
    for j in range(4):

        @pl.when(want == j)
        def _(part=part_refs[j]):
            for h in range(2):
                start = at_core * quarter if h == 0 else (1 - at_core) * quarter
                place = pl.ds(pl.multiple_of(start, quarter), quarter)
                values = wide(part[other_col, :, h * quarter : (h + 1) * quarter])
                if turned:
                    out_ref[place, :] = values.T
                else:
                    out_ref[:, place] = values


def ffn_home(where, parts, at, unit, turned, name):
    half = parts[0].shape[2]
    whole = pl.BlockSpec((2, unit, half), lambda i, w: (0, at, 0), pipeline_mode=pl.Buffered(1))
    if turned:
        spec, shape = pl.BlockSpec((half, unit), lambda i, w: (0, i)), (half, 8 * unit)
    else:
        spec, shape = pl.BlockSpec((unit, half), lambda i, w: (i, 0)), (8 * unit, half)
    return pl.pallas_call(
        functools.partial(ffn_home_kernel, turned),
        grid_spec=pltpu.PrefetchScalarGridSpec(
            num_scalar_prefetch=1, grid=(8,), in_specs=[whole] * 4, out_specs=spec
        ),
        out_shape=jax.ShapeDtypeStruct(shape, jnp.float32),
        compiler_params=pltpu.CompilerParams(vmem_limit_bytes=VMEM_LIMIT),
        cost_estimate=cost(0, 8 * unit * half * 6),
        name=name,
    )(where, *parts)


def weight_grad_kernel(count, split, *refs):
    a_ref = refs[0]
    b_refs = refs[1 : 1 + count]
    o_refs = refs[1 + count :]
    left = a_ref[...].T
    for i, b in enumerate(b_refs):
        width = b.shape[1]
        acc = low(mxu(left, b[...], NN))
        if split:
            for j in range(split):
                o_refs[0][j] = acc[:, j * width // split : (j + 1) * width // split]
        elif len(o_refs) == 1:
            o_refs[0][:, i * width : (i + 1) * width] = acc
        else:
            o_refs[i][...] = acc


def weight_grad(a, bs, block, name, joined=True, split=0):
    rows, m = a.shape
    n = sum(b.shape[1] for b in bs)
    in_specs = [pl.BlockSpec((rows, block), lambda i: (0, i))]
    for b in bs:
        in_specs.append(
            pl.BlockSpec(b.shape, lambda i: (0, 0), pipeline_mode=pl.Buffered(1))
        )
    if split:
        out_specs = [pl.BlockSpec((split, block, n // split), lambda i: (0, i, 0))]
        shapes = [(split, m, n // split)]
    else:
        widths = [n] if joined else [b.shape[1] for b in bs]
        out_specs = [pl.BlockSpec((block, w), lambda i: (i, 0)) for w in widths]
        shapes = [(m, w) for w in widths]
    outs = pl.pallas_call(
        functools.partial(weight_grad_kernel, len(bs), split),
        grid=(m // block,),
        in_specs=in_specs,
        out_specs=out_specs,
        out_shape=[jax.ShapeDtypeStruct(shape, jnp.bfloat16) for shape in shapes],
        compiler_params=pltpu.CompilerParams(vmem_limit_bytes=VMEM_LIMIT),
        cost_estimate=cost(2 * rows * m * n, 2 * (rows * m + rows * n + m * n)),
        name=name,
    )(a, *bs)
    return outs if len(outs) > 1 else outs[0]


def take(a, index, axis):
    return lax.dynamic_index_in_dim(a, index, axis, keepdims=False)


def in_order(index, mine, other, axis=0):
    first = jnp.where(index == 0, mine, other)
    second = jnp.where(index == 0, other, mine)
    return jnp.stack([first, second], axis=axis)


def spread(a):
    b = swap_col(a)
    return [a, b, swap_core(a), swap_core(b)]


def collect_core(parts):
    own, own_other, send, send_other = parts
    outgoing = low(wide(own_other) + wide(swap_core(send_other)))
    return own, swap_core(send), outgoing


def collect_col(own, got, outgoing):
    return wide(own) + wide(got) + wide(swap_col(outgoing))


def small_sum(v):
    cross = lax.ppermute(v, ("dp", "col"), CROSS_SWAP)
    return (v + swap_core(v)) + (swap_col(v) + cross)


def tree_body(
    tokens,
    out_grad,
    path,
    positions,
    w_query,
    w_key,
    w_value,
    w_out,
    w_gate,
    w_up,
    w_down,
    gain_attn,
    gain_ffn,
):
    dp = lax.axis_index("dp")
    x = dp // 2
    c = lax.rem(dp, 2)
    z = lax.axis_index("row")
    y = lax.axis_index("col")
    micro, local_rows, half = tokens.shape
    quarter = half // 2
    rows = path.shape[1]
    planes = lax.axis_size("row")
    features = 2 * half
    block = 256

    def to_trees(a):
        mine = lax.dynamic_slice_in_dim(a, c * quarter, quarter, 2)
        other = swap_core(lax.dynamic_slice_in_dim(a, (1 - c) * quarter, quarter, 2))
        return in_order(c, mine, other).reshape(planes * local_rows, quarter)

    def of_core(trees):
        trees = trees.reshape(2, micro, local_rows, quarter)
        return take(trees, c, 0), take(trees, 1 - c, 0)

    def by_feature(mine, other):
        return in_order(c, mine, swap_core(other), 2).reshape(micro, local_rows, half)

    groups = w_key.shape[1] // HEAD
    share = quarter // 2
    unit = w_gate.shape[1] // 8

    def project_piece(g):
        at = c * quarter + x * share
        return jnp.concatenate(
            [
                lax.dynamic_slice(w_query, (at, g * 2 * HEAD), (share, 2 * HEAD)),
                lax.dynamic_slice(w_key, (at, g * HEAD), (share, HEAD)),
                lax.dynamic_slice(w_value, (at, g * HEAD), (share, HEAD)),
            ],
            axis=1,
        )

    def mix_piece(g):
        return lax.dynamic_slice(w_out, ((g * 2 + x) * HEAD, c * quarter), (HEAD, quarter))

    def by_core(a):
        return jnp.where(c == 0, a, jnp.concatenate([a[:, quarter:], a[:, :quarter]], axis=1))

    def four(kept, got):
        return jnp.concatenate(
            [kept[:, :quarter], got[:, :quarter], kept[:, quarter:], got[:, quarter:]], axis=1
        )

    project_sent = project_piece(1 - y)
    project_mine = jnp.stack([project_piece(y), swap_col(project_sent)])
    trees = to_trees(tokens)
    block_in = lax.all_to_all(trees, "row", 0, 0, tiled=True)
    def hidden_piece(j, xh):
        at = ((2 * j + c) * 2 + xh) * unit
        return [
            by_core(lax.dynamic_slice_in_dim(w_gate, at, unit, 1).T),
            by_core(lax.dynamic_slice_in_dim(w_up, at, unit, 1).T),
            by_core(lax.dynamic_slice_in_dim(w_down, at, unit, 0)),
        ]

    sent = jnp.concatenate([*hidden_piece(1 - y, x), jnp.tile(mix_piece(1 - y), (1, 2))])
    got = swap_col(after(sent, project_sent))
    project_all = lax.all_gather(project_mine, "row", axis=0)

    marks = jnp.concatenate([path, positions[:, :, None]], axis=2)
    marks = jnp.transpose(marks, (2, 0, 1))
    marks = in_order(c, marks, swap_core(marks), 1).reshape(4, 2 * micro, rows)
    marks = take(marks, z, 1)
    cosine, sine = rope_tables(marks[3])
    sign = jnp.where(jnp.arange(HEAD) < HEAD // 2, -1.0, 1.0).astype(jnp.float32)
    sine = sine * sign[None, :]
    label_col = marks[0][:, None]
    label_rows = jnp.pad(marks, ((0, 4), (0, 0)))

    hidden_mine = [
        four(kept, got[i * unit : (i + 1) * unit])
        for i, kept in enumerate(hidden_piece(y, x))
    ]
    mix_mine = jnp.stack([mix_piece(y), got[3 * unit :, :quarter]])
    near_sent = jnp.concatenate(hidden_piece(1 - y, 1 - x))
    near_got = swap_col(after(near_sent, mix_mine))
    hidden_near = [
        four(kept, near_got[i * unit : (i + 1) * unit])
        for i, kept in enumerate(hidden_piece(y, 1 - x))
    ]

    def gain_order(gain):
        kept = gain.reshape(2, quarter)
        both = jnp.stack([kept, swap_col(kept)], axis=1)
        both = jnp.where(c == 0, both, both[::-1])
        return both.reshape(1, features)

    gain_attn_all = gain_order(gain_attn)
    gain_attn_own = gain_attn_all[:, :quarter]
    gain_ffn_own = lax.dynamic_slice_in_dim(gain_ffn, c * quarter, quarter, 0)[None, :]

    (
        project_all, block_in, mix_mine, gate_piece, up_piece, down_piece,
        gate_near, up_near, down_near, cosine, sine, label_col, label_rows, gain_attn_all,
    ) = lax.optimization_barrier(
        (
            project_all, block_in, mix_mine, *hidden_mine, *hidden_near,
            cosine, sine, label_col, label_rows, gain_attn_all,
        )
    )

    pieces = spread(block_in)
    mix_all = lax.all_gather(mix_mine, "row", axis=0)
    gate_mine = lax.all_gather(gate_piece, "row", axis=0, tiled=True)
    up_mine = lax.all_gather(after(up_piece, mix_all), "row", axis=0, tiled=True)
    down_mine = lax.all_gather(after(down_piece, gate_mine), "row", axis=0, tiled=True)
    gate_next, up_next, down_next = (
        next_blocks(u, z, planes) for u in (gate_mine, up_mine, down_mine)
    )
    gate_far, up_far, down_far = (swap_x(u) for u in (gate_next, up_next, down_next))

    def of_core_pairs(mine, other):
        both = in_order(x, mine, other, 2)
        pairs = both.reshape((2, planes // 2) + both.shape[1:])
        return take(pairs, c, 0), swap_core(take(pairs, 1 - c, 0))

    near, far = of_core_pairs(project_all, swap_x(project_all))
    w_near = near.reshape(groups, half, 4 * HEAD)
    w_far = far.reshape(groups, half, 4 * HEAD)

    normed_attn, qkv, ratio_attn = rows_call(
        project_kernel,
        block,
        [*pieces, cosine, sine],
        [gain_attn_all, w_near, w_far],
        [(features, jnp.bfloat16), (groups * 4 * HEAD, jnp.bfloat16), (1, jnp.float32)],
        2 * rows * features * groups * 4 * HEAD,
        "project",
    )
    near, far = of_core_pairs(mix_all, after(swap_x(mix_all), qkv))
    attn, lse = attend(after(qkv, near), label_col, label_rows, TRUNK, LEAF_BEGIN, block)
    mix_shape = (groups, 2, 2 * HEAD, quarter)
    m_near, m_far = near.reshape(mix_shape), after(far, attn).reshape(mix_shape)
    parts = rows_call(
        mix_kernel,
        2 * block,
        [attn],
        [m_near, m_far],
        [(quarter, jnp.bfloat16)] * 4,
        2 * rows * features * groups * 2 * HEAD,
        "mix",
    )
    cotangent = lax.all_to_all(to_trees(out_grad), "row", 0, 0, tiled=True)
    parts[1] = after(parts[1], cotangent, gate_next)
    own, got, outgoing = collect_core(parts)
    middle = wide(block_in) + collect_col(own, got, outgoing)
    square = small_sum(jnp.sum(middle * middle, axis=1))
    ratio_ffn = lax.rsqrt(square / features + EPSILON)[:, None]
    normed_ffn = middle * ratio_ffn
    ffn_near = after(low(normed_ffn * gain_ffn_own), up_next, gate_far)
    ffn_across = swap_col(ffn_near)
    ffn_pieces = [ffn_near, ffn_across, swap_core(ffn_near), swap_core(ffn_across)]
    grad_near, grad_across = cotangent, swap_col(after(cotangent, ffn_pieces[1]))
    gate_m, up_m, gate_o, up_o = rows_call(
        gate_up_kernel,
        block,
        ffn_pieces,
        [gate_mine, up_mine, gate_near, gate_far, up_near, up_far],
        [(planes * unit, jnp.bfloat16)] * 4,
        2 * rows * features * 4 * planes * unit,
        "gate_up",
        [pltpu.VMEM((block, features), jnp.bfloat16)],
    )
    grad_pieces = [
        grad_near,
        grad_across,
        swap_core(after(grad_near, ffn_pieces[3])),
        swap_core(after(grad_across, gate_m)),
    ]
    dgate_m, dup_m, hid_m, dgate_o, dup_o, hid_o = rows_call(
        hidden_kernel,
        block,
        [*grad_pieces, gate_m, gate_o, up_m, up_o],
        [down_mine, down_near, down_far],
        [(planes * unit, jnp.bfloat16)] * 6,
        2 * rows * features * 2 * planes * unit,
        "hidden",
        [pltpu.VMEM((block, features), jnp.bfloat16)],
    )

    def unit_grad(a, pieces_of, name, before):
        return weight_grad(after(a, before), pieces_of, 2 * block, name)

    def to_row(total):
        return lax.psum_scatter(total, "row", scatter_dimension=0, tiled=True)

    down_other = turned_grad(hid_o, grad_pieces, z, planes, "down_grad_other")
    parts = rows_call(
        functools.partial(sum_out_kernel, 4),
        2 * block,
        [after(dgate_m, down_other), dup_m, dgate_o, dup_o],
        [gate_mine, up_mine, gate_near, gate_far, up_near, up_far],
        [(quarter, jnp.bfloat16)] * 4,
        2 * rows * features * 4 * planes * unit,
        "pair_back",
    )
    gate_other = turned_grad(after(dgate_o, parts[0]), ffn_pieces, z, planes, "gate_grad_other")
    down_own = unit_grad(hid_m, grad_pieces, "down_grad_mine", gate_other)
    parts[1] = after(parts[1], down_own)
    own, got, outgoing = collect_core(parts)
    down_total = low(wide(after(down_own, outgoing)) + wide(swap_x(down_other)))
    down_sum = to_row(down_total)
    up_other = turned_grad(after(dup_o, down_total), ffn_pieces, z, planes, "up_grad_other")
    gate_own = unit_grad(dgate_m, ffn_pieces, "gate_grad_mine", up_other)
    normed_ffn_grad = collect_col(after(own, gate_own), got, outgoing)

    def norm_back(grad, ratio, normed, gain):
        scaled = grad * gain
        inner = small_sum(jnp.sum(scaled * normed, axis=1))[:, None] / features
        return ratio * (scaled - normed * inner), jnp.sum(grad * normed, axis=0)

    middle_back, gain_ffn_part = norm_back(normed_ffn_grad, ratio_ffn, normed_ffn, gain_ffn_own)
    middle_grad = wide(cotangent) + middle_back
    middle_low = low(middle_grad)
    up_own = unit_grad(dup_m, ffn_pieces, "up_grad_mine", middle_low)
    gate_total = low(wide(after(gate_own, up_own)) + wide(swap_x(gate_other)))
    gate_sum = to_row(gate_total)
    where = jnp.stack([y, x, c]).astype(jnp.int32)

    def unit_halves(total):
        kept = jnp.concatenate([total[:, :quarter], total[:, half : half + quarter]], axis=1)
        sent = jnp.concatenate([total[:, quarter:half], total[:, half + quarter :]], axis=1)
        return kept, sent

    def unit_parts(kept, sent, first, second):
        both = jnp.stack([kept, after(swap_col(sent), first)])
        over = after(swap_x(both), second)
        return [both, swap_core(both), over, swap_core(over)]

    out_parts = rows_call(
        functools.partial(sum_out_kernel, 2),
        2 * block,
        [after(hid_m, gate_total), hid_o],
        [down_mine, down_near, down_far],
        [(quarter, jnp.bfloat16)] * 4,
        2 * rows * features * 2 * planes * unit,
        "down",
    )
    middle_across = after(swap_col(middle_low), out_parts[0])
    middle_pieces = [middle_low, middle_across, swap_core(middle_low), swap_core(middle_across)]
    attn_grad = rows_call(
        attn_grad_kernel,
        2 * block,
        middle_pieces,
        [m_near, m_far],
        [(groups * 2 * HEAD, jnp.bfloat16)],
        2 * rows * features * groups * 2 * HEAD,
        "attn_grad",
    )[0]
    out_parts[1] = after(out_parts[1], attn_grad)
    out_own, out_got, out_outgoing = collect_core(out_parts)
    qkv_grad = attend_back(
        qkv, attn, after(attn_grad, out_outgoing), label_col, label_rows, lse, cosine, sine,
        TRUNK, LEAF_BEGIN, block,
    )
    output = low(after(middle, qkv_grad) + collect_col(out_own, out_got, out_outgoing))
    up_total = low(wide(after(up_own, output)) + wide(swap_x(up_other)))
    up_sum = to_row(up_total)
    parts = rows_call(
        project_back_kernel,
        2 * block,
        [after(qkv_grad, up_total)],
        [w_near, w_far],
        [(quarter, jnp.bfloat16)] * 4,
        2 * rows * features * groups * 4 * HEAD,
        "project_back",
    )
    output_tree = lax.all_to_all(output, "row", 0, 0, tiled=True)
    own, got, outgoing = collect_core(parts)
    project_grad = weight_grad(
        normed_attn, [after(qkv_grad, outgoing)], 2 * block, "project_grad", split=groups
    )
    mix_grads = weight_grad(
        attn,
        [after(middle_pieces[0], project_grad), *middle_pieces[1:]],
        groups * 2 * HEAD,
        "mix_grad",
        joined=False,
    )

    project_parts = project_grad.reshape(groups, 2, 2, 2, share, 4 * HEAD)
    mix_parts = jnp.stack([m.reshape(groups, 2, HEAD, quarter) for m in mix_grads], axis=1)
    mix_parts = mix_parts.reshape(groups, 2, 2, 2, HEAD, quarter)

    def of_x(index):
        return jnp.concatenate([take(project_parts, index, 3), take(mix_parts, index, 3)], axis=3)

    attn_sent = of_x(1 - x)
    attn_kept = of_x(after(x, attn_sent))
    normed_attn_grad = collect_col(after(own, attn_kept), got, outgoing)
    normed_attn_own = wide(block_in) * ratio_attn
    input_back, gain_attn_part = norm_back(
        normed_attn_grad, ratio_attn, normed_attn_own, gain_attn_own
    )
    input_low = low(middle_grad + input_back)
    input_tree = lax.all_to_all(input_low, "row", 0, 0, tiled=True)
    home_kept, home_sent = unit_halves(
        jnp.concatenate([after(down_sum, input_low), gate_sum])
    )
    output, output_sent = of_core(after(output_tree, home_sent))
    home_both = jnp.stack([home_kept, after(swap_col(home_sent), output_sent)])
    home_over = swap_x(home_both)
    attn_total = low(wide(after(attn_kept, home_both)) + wide(swap_x(attn_sent)))
    by_plane = in_order(c, attn_total[:, 0], swap_core(attn_total[:, 1]))
    by_plane = by_plane.reshape((planes,) + by_plane.shape[2:])
    attn_sum = lax.psum_scatter(by_plane, "row", scatter_dimension=0, tiled=False)
    output = by_feature(after(output, by_plane), output_sent)
    up_kept, up_sent = unit_halves(after(up_sum, output))
    home_over = after(home_over, up_sent)
    home_parts = [home_both, swap_core(home_both), home_over, swap_core(home_over)]
    down_out = ffn_home(where, home_parts, 0, unit, False, "down_home")
    gate_out = ffn_home(where, home_parts, 1, unit, True, "gate_home")
    attn_sum = after(attn_sum, down_out, gate_out)
    home = in_order(y, attn_sum[0], swap_col(attn_sum[1]))
    up_parts = unit_parts(up_kept, up_sent, gate_out, home)
    up_out = ffn_home(where, up_parts, 0, unit, True, "up_home")
    home = in_order(x, home, after(swap_x(home), up_out))
    input_grad = by_feature(*of_core(after(input_tree, up_out)))
    home = in_order(c, home, swap_core(home))
    mix_home = home[:, :, :, share:]
    out_out = wide(jnp.transpose(mix_home, (2, 1, 3, 0, 4)).reshape(groups * 2 * HEAD, half))
    project_home = jnp.transpose(home[:, :, :, :share], (0, 1, 3, 2, 4))
    project_home = project_home.reshape(half, groups, 4 * HEAD)
    query_out = wide(project_home[:, :, : 2 * HEAD].reshape(half, groups * 2 * HEAD))
    key_out = wide(project_home[:, :, 2 * HEAD : 3 * HEAD].reshape(half, groups * HEAD))
    value_out = wide(project_home[:, :, 3 * HEAD :].reshape(half, groups * HEAD))

    gains = jnp.stack([gain_attn_part, gain_ffn_part])
    gains = gains + shift(gains, ROW_SECOND)
    gains = gains + shift(gains, ROW_SWAP)
    gains = gains + swap_x(gains)
    gains = in_order(c, gains, swap_core(gains), 1)
    gain_attn_out = gains[0].reshape(half)
    gain_ffn_out = gains[1].reshape(half)
    return (
        output,
        input_grad,
        query_out,
        key_out,
        value_out,
        out_out,
        gate_out,
        up_out,
        down_out,
        gain_attn_out,
        gain_ffn_out,
    )


def solution(mesh):
    in_specs = (
        P(None, ("dp", "row"), "col"),
        P(None, ("dp", "row"), "col"),
        P(None, "dp", None),
        P(None, "dp"),
        P("col", "row"),
        P("col", "row"),
        P("col", "row"),
        P("row", "col"),
        P("col", "row"),
        P("col", "row"),
        P("row", "col"),
        P("col"),
        P("col"),
    )
    out_specs = (
        P(None, ("dp", "row"), "col"),
        P(None, ("dp", "row"), "col"),
        P("col", "row"),
        P("col", "row"),
        P("col", "row"),
        P("row", "col"),
        P("col", "row"),
        P("col", "row"),
        P("row", "col"),
        P("col"),
        P("col"),
    )
    sizes = dict(mesh.shape)
    fits = sizes == {"dp": 4, "row": 4, "col": 2}
    chosen = tree_body if fits else body
    return jax.shard_map(chosen, mesh=mesh, in_specs=in_specs, out_specs=out_specs, check_vma=False)
```

```python
import functools
import math

import jax
import jax.numpy as jnp
from jax import lax
from jax.experimental import pallas as pl
from jax.experimental.pallas import tpu as pltpu
from jax.sharding import PartitionSpec as P

D = 2048
HEADS = 16
KV_HEADS = 8
HEAD = 128


EPSILON = 1e-05
THETA = 1000000.0


def contract_rows(left, right):
    return lax.dot_general(
        left, right, (((0,), (0,)), ((), ())), preferred_element_type=jnp.float32
    )


def contract_cols(left, right):
    return lax.dot_general(
        left, right, (((1,), (1,)), ((), ())), preferred_element_type=jnp.float32
    )


def rows_gather(values):
    return lax.all_gather(values, "row", axis=0, tiled=True)


def cols_gather(values):
    return lax.all_gather(values, "col", axis=0, tiled=True)


def cols_reduce(part_fn, rows):
    return lax.psum_scatter(
        part_fn(jnp.int32(0), rows * lax.axis_size("col")), "col", scatter_dimension=0, tiled=True
    )


def rows_reduce(part_fn, rows):
    return lax.psum_scatter(
        part_fn(jnp.int32(0), rows * lax.axis_size("row")).astype(jnp.bfloat16),
        "row",
        scatter_dimension=0,
        tiled=True,
    ).astype(jnp.float32)


def feature_sums(values):
    return lax.psum(jnp.sum(values, axis=1), "col")


def sliced_product(whole, weight, transpose):

    def part_fn(start, count):
        if transpose:
            return contract_cols(whole, weight)
        return jnp.dot(whole, weight, preferred_element_type=jnp.float32)

    return part_fn


def rope_tables(positions):
    half = HEAD // 2
    frequency = jnp.power(THETA, -2.0 * jnp.arange(half, dtype=jnp.float32) / HEAD)
    angles = positions.astype(jnp.float32)[:, None] * frequency[None, :]
    angles = jnp.concatenate([angles, angles], axis=1)
    return (jnp.cos(angles), jnp.sin(angles))


def rotate(values, cosine, sine):
    half = values.shape[-1] // 2
    turned = jnp.concatenate([-values[..., half:], values[..., :half]], axis=-1)
    return values * cosine[:, None, :] + turned * sine[:, None, :]


def rotate_back(grads, cosine, sine):
    half = grads.shape[-1] // 2
    scaled = grads * sine[:, None, :]
    turned = jnp.concatenate([scaled[..., half:], -scaled[..., :half]], axis=-1)
    return grads * cosine[:, None, :] + turned


def norm_forward(values, gain):
    ratio = lax.rsqrt(feature_sums(values * values) / D + EPSILON)[:, None]
    normed = values * ratio
    return (ratio, normed, (normed * gain).astype(jnp.bfloat16))


def norm_backward(grad, ratio, normed, gain):
    scaled = grad * gain
    inner = feature_sums(scaled * normed)[:, None] / D
    return (ratio * (scaled - normed * inner), jnp.sum(grad * normed, axis=0))


def body(
    tokens,
    out_grad,
    path,
    positions,
    w_query,
    w_key,
    w_value,
    w_out,
    w_gate,
    w_up,
    w_down,
    gain_attn,
    gain_ffn,
):
    query_width = w_query.shape[1]
    key_width = w_key.shape[1]
    hidden_width = w_gate.shape[1]
    local_heads = key_width // HEAD
    group = HEADS // KV_HEADS
    scale = 1.0 / math.sqrt(HEAD)
    block_rows = path.shape[1]
    local_rows = tokens.shape[1]
    query_rows = block_rows // lax.axis_size("col")
    first = lax.axis_index("col") * query_rows
    w_project = jnp.concatenate([w_query, w_key, w_value], axis=1)
    w_pair = jnp.concatenate([w_gate, w_up], axis=1)
    project_start = jnp.zeros(w_project.shape, jnp.float32)
    pair_start = jnp.zeros(w_pair.shape, jnp.float32)
    down_start = jnp.zeros(w_down.shape, jnp.float32)

    def micro_step(carry, batch):
        grad_project, grad_out, grad_pair, grad_down, grad_gain_attn, grad_gain_ffn = carry
        block, cotangent, block_path, block_place = batch
        inputs = block.astype(jnp.float32)
        cosine, sine = rope_tables(lax.dynamic_slice_in_dim(block_place, first, query_rows, 0))
        query_path = lax.dynamic_slice_in_dim(block_path, first, query_rows, 0)
        key_labels = block_path[:, 0]
        query_place = first + jnp.arange(query_rows, dtype=jnp.int32)
        key_place = jnp.arange(block_rows, dtype=jnp.int32)
        same_path = (
            (key_labels[None, :] == query_path[:, 0:1])
            | (key_labels[None, :] == query_path[:, 1:2])
            | (key_labels[None, :] == query_path[:, 2:3])
        )
        visible = same_path & (key_place[None, :] <= query_place[:, None])
        ratio_attn, normed_attn, input_attn = norm_forward(inputs, gain_attn)
        gathered_attn = rows_gather(input_attn)
        projected = cols_reduce(sliced_product(gathered_attn, w_project, False), query_rows)
        query = rotate(
            projected[:, :query_width].reshape(query_rows, -1, HEAD), cosine, sine
        ).astype(jnp.bfloat16)
        keys = rotate(
            projected[:, query_width : query_width + key_width].reshape(query_rows, -1, HEAD),
            cosine,
            sine,
        ).astype(jnp.bfloat16)
        values = projected[:, query_width + key_width :].astype(jnp.bfloat16)
        keys_all, values_all = (
            lax.all_gather(keys.reshape(query_rows, key_width), "col", axis=0, tiled=True),
            lax.all_gather(values, "col", axis=0, tiled=True),
        )
        query_groups = query.reshape(query_rows, local_heads, group, HEAD)
        key_heads = keys_all.reshape(block_rows, local_heads, HEAD)
        value_heads = values_all.reshape(block_rows, local_heads, HEAD)
        scores = (
            jnp.einsum(
                "ikgd,jkd->kgij", query_groups, key_heads, preferred_element_type=jnp.float32
            )
            * scale
        )
        scores = jnp.where(visible[None, None], scores, -jnp.inf)
        weights = jax.nn.softmax(scores, axis=-1)
        weights_low = weights.astype(jnp.bfloat16)
        mixed = jnp.einsum(
            "kgij,jkd->ikgd", weights_low, value_heads, preferred_element_type=jnp.float32
        )
        attn_low = mixed.reshape(query_rows, query_width).astype(jnp.bfloat16)
        attn_all = cols_gather(attn_low)
        branch_attn = rows_reduce(sliced_product(attn_all, w_out, False), local_rows)
        middle = inputs + branch_attn
        ratio_ffn, normed_ffn, input_ffn = norm_forward(middle, gain_ffn)
        gathered_ffn = rows_gather(input_ffn)
        pair = cols_reduce(sliced_product(gathered_ffn, w_pair, False), query_rows)
        gate = pair[:, :hidden_width]
        upper = pair[:, hidden_width:]
        sigma = jax.nn.sigmoid(gate)
        silu_value = gate * sigma
        hidden = (silu_value * upper).astype(jnp.bfloat16)
        hidden_all = cols_gather(hidden)
        branch_ffn = rows_reduce(sliced_product(hidden_all, w_down, False), local_rows)
        output = (middle + branch_ffn).astype(jnp.bfloat16)
        cotangent_all = rows_gather(cotangent)
        hidden_grad = cols_reduce(sliced_product(cotangent_all, w_down, True), query_rows)
        grad_down = grad_down + contract_rows(hidden_all, cotangent_all)
        gate_grad = hidden_grad * upper * sigma * (1.0 + gate * (1.0 - sigma))
        upper_grad = hidden_grad * silu_value
        pair_grad = jnp.concatenate([gate_grad, upper_grad], axis=1).astype(jnp.bfloat16)
        pair_all = cols_gather(pair_grad)
        normed_ffn_grad = rows_reduce(sliced_product(pair_all, w_pair, True), local_rows)
        grad_pair = grad_pair + contract_rows(gathered_ffn, pair_all)
        middle_back, gain_ffn_step = norm_backward(normed_ffn_grad, ratio_ffn, normed_ffn, gain_ffn)
        middle_grad = cotangent.astype(jnp.float32) + middle_back
        middle_low = middle_grad.astype(jnp.bfloat16)
        middle_all = rows_gather(middle_low)
        attn_grad = cols_reduce(sliced_product(middle_all, w_out, True), query_rows).astype(
            jnp.bfloat16
        )
        grad_out = grad_out + contract_rows(attn_all, middle_all)
        attn_heads = attn_grad.reshape(query_rows, local_heads, group, HEAD)
        weight_grad = jnp.einsum(
            "ikgd,jkd->kgij", attn_heads, value_heads, preferred_element_type=jnp.float32
        )
        score_grad = (
            weights * (weight_grad - jnp.sum(weights * weight_grad, axis=-1, keepdims=True))
        ).astype(jnp.bfloat16)
        query_grad = (
            jnp.einsum("kgij,jkd->ikgd", score_grad, key_heads, preferred_element_type=jnp.float32)
            * scale
        )
        key_part = (
            jnp.einsum(
                "kgij,ikgd->jkd", score_grad, query_groups, preferred_element_type=jnp.float32
            )
            * scale
        )
        value_part = jnp.einsum(
            "kgij,ikgd->jkd", weights_low, attn_heads, preferred_element_type=jnp.float32
        )
        key_grad, value_grad = (
            lax.psum_scatter(
                key_part.reshape(block_rows, key_width).astype(jnp.bfloat16),
                "col",
                scatter_dimension=0,
                tiled=True,
            ).astype(jnp.float32),
            lax.psum_scatter(
                value_part.reshape(block_rows, key_width).astype(jnp.bfloat16),
                "col",
                scatter_dimension=0,
                tiled=True,
            ).astype(jnp.float32),
        )
        query_back = rotate_back(query_grad.reshape(query_rows, -1, HEAD), cosine, sine).reshape(
            query_rows, query_width
        )
        key_back = rotate_back(key_grad.reshape(query_rows, -1, HEAD), cosine, sine).reshape(
            query_rows, key_width
        )
        projected_grad = jnp.concatenate([query_back, key_back, value_grad], axis=1).astype(
            jnp.bfloat16
        )
        projected_all = cols_gather(projected_grad)
        normed_attn_grad = rows_reduce(sliced_product(projected_all, w_project, True), local_rows)
        grad_project = grad_project + contract_rows(gathered_attn, projected_all)
        input_back, gain_attn_step = norm_backward(
            normed_attn_grad, ratio_attn, normed_attn, gain_attn
        )
        input_grad = (middle_grad + input_back).astype(jnp.bfloat16)
        carry = (
            grad_project,
            grad_out,
            grad_pair,
            grad_down,
            grad_gain_attn + gain_attn_step,
            grad_gain_ffn + gain_ffn_step,
        )
        return (carry, (output, input_grad))

    start = (
        project_start,
        jnp.zeros(w_out.shape, jnp.float32),
        pair_start,
        down_start,
        jnp.zeros(gain_attn.shape, jnp.float32),
        jnp.zeros(gain_ffn.shape, jnp.float32),
    )
    sums, (outputs, input_grads) = lax.scan(micro_step, start, (tokens, out_grad, path, positions))
    grad_project, grad_out, grad_pair, grad_down, grad_gain_attn, grad_gain_ffn = sums
    grad_project, grad_out, grad_pair, grad_down = (
        lax.psum(grad_project.astype(jnp.bfloat16), "dp").astype(jnp.float32),
        lax.psum(grad_out.astype(jnp.bfloat16), "dp").astype(jnp.float32),
        lax.psum(grad_pair.astype(jnp.bfloat16), "dp").astype(jnp.float32),
        lax.psum(grad_down.astype(jnp.bfloat16), "dp").astype(jnp.float32),
    )
    grad_gain_attn, grad_gain_ffn = lax.psum((grad_gain_attn, grad_gain_ffn), ("dp", "row"))
    query_part = grad_project[:, :query_width]
    key_part_grad = grad_project[:, query_width : query_width + key_width]
    value_part_grad = grad_project[:, query_width + key_width :]
    return (
        outputs,
        input_grads,
        query_part,
        key_part_grad,
        value_part_grad,
        grad_out,
        grad_pair[:, :hidden_width],
        grad_pair[:, hidden_width:],
        grad_down,
        grad_gain_attn,
        grad_gain_ffn,
    )


CORE_SWAP = [(0, 1), (1, 0), (2, 3), (3, 2)]
X_SWAP = [(0, 2), (2, 0), (1, 3), (3, 1)]
COL_SWAP = [(0, 1), (1, 0)]
CROSS_SWAP = [(2 * d + j, 2 * (d ^ 1) + 1 - j) for d in range(4) for j in range(2)]
ROW_SECOND = [(0, 2), (1, 3), (2, 0), (3, 1)]
ROW_SWAP = [(0, 1), (1, 0), (2, 3), (3, 2)]
LOG2E = 1.4426950408889634
TRUNK = 1024
LEAF_BEGIN = TRUNK + 4 * 128
SHARE_OF_COST = 8
VMEM_LIMIT = 58 * 1024 * 1024
NT = (((1,), (1,)), ((), ()))
TN = (((0,), (0,)), ((), ()))
NN = (((1,), (0,)), ((), ()))


def swap_core(a):
    return lax.ppermute(a, "dp", CORE_SWAP)


def swap_x(a):
    return lax.ppermute(a, "dp", X_SWAP)


def swap_col(a):
    return lax.ppermute(a, "col", COL_SWAP)


def shift(a, pairs):
    return lax.ppermute(a, "row", pairs)


def after(value, *deps):
    return lax.optimization_barrier((value, *deps))[0]


def cost(flops, moved):
    return pl.CostEstimate(
        flops=flops // SHARE_OF_COST, bytes_accessed=moved // SHARE_OF_COST, transcendentals=0
    )


def mxu(a, b, dims):
    return lax.dot_general(a, b, dims, preferred_element_type=jnp.float32)


def low(a):
    return a.astype(jnp.bfloat16)


def wide(a):
    return a.astype(jnp.float32)


def rows_call(fn, block, row_ins, full_ins, outs, flops, name, scratch=()):
    rows = row_ins[0].shape[0]
    in_specs = [pl.BlockSpec((block, a.shape[1]), lambda i: (i, 0)) for a in row_ins]
    for a in full_ins:
        in_specs.append(
            pl.BlockSpec(
                a.shape, lambda i, nd=a.ndim: (0,) * nd, pipeline_mode=pl.Buffered(1)
            )
        )
    moved = sum(a.size * a.dtype.itemsize for a in (*row_ins, *full_ins))
    moved += sum(rows * w * jnp.dtype(dt).itemsize for w, dt in outs)
    results = pl.pallas_call(
        fn,
        grid=(rows // block,),
        in_specs=in_specs,
        out_specs=[pl.BlockSpec((block, w), lambda i: (i, 0)) for w, _ in outs],
        out_shape=[jax.ShapeDtypeStruct((rows, w), dt) for w, dt in outs],
        scratch_shapes=list(scratch),
        compiler_params=pltpu.CompilerParams(vmem_limit_bytes=VMEM_LIMIT),
        cost_estimate=cost(flops, moved),
        name=name,
    )(*row_ins, *full_ins)
    return list(results)


def turn(u, cosine, sine_signed):
    return u * cosine + pltpu.roll(u, HEAD // 2, 1) * sine_signed


def turn_back(u, cosine, sine_signed):
    return u * cosine - pltpu.roll(u, HEAD // 2, 1) * sine_signed


def project_kernel(
    x0, x1, x2, x3, cos_ref, sin_ref, gain_ref, own_ref, far_ref, xn_ref, qkv_ref, r_ref
):
    pieces = [wide(r[...]) for r in (x0, x1, x2, x3)]
    width = pieces[0].shape[1]
    total = sum(jnp.sum(p * p, axis=1, keepdims=True) for p in pieces)
    ratio = lax.rsqrt(total / (4 * width) + EPSILON)
    r_ref[...] = ratio
    for i, p in enumerate(pieces):
        cols = slice(i * width, (i + 1) * width)
        xn_ref[:, cols] = low(p * ratio * gain_ref[:, cols])
    near = xn_ref[:, : 2 * width]
    far = xn_ref[:, 2 * width :]
    cosine = cos_ref[...]
    sine = sin_ref[...]
    span = own_ref.shape[2]
    heads = span // HEAD
    for g in range(own_ref.shape[0]):
        acc = mxu(near, own_ref[g], NN) + mxu(far, far_ref[g], NN)
        for h in range(heads):
            u = acc[:, h * HEAD : (h + 1) * HEAD]
            if h < heads - 1:
                u = turn(u, cosine, sine)
            at = g * span + h * HEAD
            qkv_ref[:, at : at + HEAD] = low(u)


def segments_of(kind, trunk, leaf_begin, block):
    if kind == "branch":
        return [(0, trunk, None), (None, block, "own")]
    if kind == "leaf":
        return [(0, trunk, None), (trunk, leaf_begin - trunk, "parent"), (None, 2 * block, "own")]
    return [(0, kind, "causal")]


def attention_blocks(qb, block, trunk, leaf_begin, run):
    half = trunk // 2

    @pl.when(qb < half // block)
    def _():
        run(half, 0)

    @pl.when((qb >= half // block) & (qb < trunk // block))
    def _():
        run(trunk, 0)

    @pl.when((qb >= trunk // block) & (qb < leaf_begin // block))
    def _():
        run("branch", pl.multiple_of(qb * block, block))

    @pl.when(qb >= leaf_begin // block)
    def _():
        run("leaf", pl.multiple_of(qb * block - block, block))


def key_rows(start, window, length):
    if start is None:
        return pl.ds(window, length)
    return pl.ds(start, length)


def score_segment(s, start, window, length, mask, qb, block, lab_ref, own_row, parent_row):
    if mask is None:
        return s
    rows = s.shape[0]
    cols = s.shape[1]
    if mask == "parent":
        return jnp.where(lab_ref[key_rows(start, window, length), :] == parent_row, s, -jnp.inf)
    base = window if start is None else start
    key_at = base + lax.broadcasted_iota(jnp.int32, (rows, 1), 0)
    lane = lax.broadcasted_iota(jnp.int32, (1, cols), 1)
    query_at = qb * block + jnp.where(lane >= block, lane - block, lane)
    seen = key_at <= query_at
    if mask == "own":
        seen = seen & (lab_ref[key_rows(start, window, length), :] == own_row)
    return jnp.where(seen, s, -jnp.inf)


def attend_kernel(trunk, leaf_begin, block, q_ref, k_ref, v_ref, lab_ref, row_ref, o_ref, lse_ref, vt_ref):
    qb = pl.program_id(1)
    factor = LOG2E / math.sqrt(HEAD)

    @pl.when(qb == 0)
    def _():
        vt_ref[...] = v_ref[...].T

    queries = jnp.concatenate([q_ref[:, :HEAD], q_ref[:, HEAD:]], axis=0)
    own = row_ref[0:1, :]
    parent = row_ref[1:2, :]
    own_row = jnp.concatenate([own, own], axis=1)
    parent_row = jnp.concatenate([parent, parent], axis=1)

    def run(kind, window):
        scores = []
        segs = segments_of(kind, trunk, leaf_begin, block)
        for start, length, mask in segs:
            s = mxu(k_ref[key_rows(start, window, length), :], queries, NT)
            s = score_segment(
                s, start, window, length, mask, qb, block, lab_ref, own_row, parent_row
            )
            scores.append(s)
        top = scores[0].max(axis=0, keepdims=True)
        for s in scores[1:]:
            top = jnp.maximum(top, s.max(axis=0, keepdims=True))
        total = jnp.zeros_like(top)
        mixed = jnp.zeros((HEAD, 2 * block), jnp.float32)
        shift = top * factor
        for (start, length, mask), s in zip(segs, scores):
            p = jnp.exp2(s * factor - shift)
            total = total + p.sum(axis=0, keepdims=True)
            mixed = mixed + mxu(vt_ref[:, key_rows(start, window, length)], low(p), NN)
        lse_ref[...] = shift + jnp.log2(total)
        mixed = mixed / total
        o_ref[:, :HEAD] = low(mixed[:, :block].T)
        o_ref[:, HEAD:] = low(mixed[:, block:].T)

    attention_blocks(qb, block, trunk, leaf_begin, run)


def attend_back_kernel(
    trunk, leaf_begin, block, blocks, q_ref, k_ref, v_ref, o_ref, do_ref, lab_ref, row_ref, lse_ref,
    cos_ref, sin_ref, out_ref, kt_ref, dk_ref, dv_ref,
):
    qb = pl.program_id(1)
    scale = 1.0 / math.sqrt(HEAD)
    factor = LOG2E * scale

    @pl.when(qb == 0)
    def _():
        kt_ref[...] = k_ref[...].T
        dk_ref[...] = jnp.zeros_like(dk_ref)
        dv_ref[...] = jnp.zeros_like(dv_ref)

    queries = jnp.concatenate([q_ref[:, :HEAD], q_ref[:, HEAD:]], axis=0)
    grads = jnp.concatenate([do_ref[:, :HEAD], do_ref[:, HEAD:]], axis=0)
    outs = jnp.concatenate([o_ref[:, :HEAD], o_ref[:, HEAD:]], axis=0)
    inner = (wide(grads) * wide(outs)).T.sum(axis=0, keepdims=True)
    lse = lse_ref[...]
    own = row_ref[0:1, :]
    parent = row_ref[1:2, :]
    own_row = jnp.concatenate([own, own], axis=1)
    parent_row = jnp.concatenate([parent, parent], axis=1)
    q_rows = pl.ds(pl.multiple_of(qb * block, block), block)

    def run(kind, window):
        dq = jnp.zeros((HEAD, 2 * block), jnp.float32)
        for start, length, mask in segments_of(kind, trunk, leaf_begin, block):
            keys = key_rows(start, window, length)
            s = mxu(k_ref[keys, :], queries, NT)
            s = score_segment(
                s, start, window, length, mask, qb, block, lab_ref, own_row, parent_row
            )
            p = jnp.exp2(s * factor - lse)
            dp = mxu(v_ref[keys, :], grads, NT)
            ds = low(p * (dp - inner))
            dv_ref[keys, :] += mxu(low(p), grads, NN)
            dk_ref[keys, :] += mxu(ds, queries, NN)
            dq = dq + mxu(kt_ref[:, keys], ds, NN)
        dq = dq * scale
        cosine = cos_ref[q_rows, :]
        sine = sin_ref[q_rows, :]
        for h in range(2):
            part = dq[:, h * block : (h + 1) * block].T
            out_ref[q_rows, h * HEAD : (h + 1) * HEAD] = low(turn_back(part, cosine, sine))

    attention_blocks(qb, block, trunk, leaf_begin, run)

    @pl.when(qb == blocks - 1)
    def _():
        dk = dk_ref[...] * scale
        out_ref[:, 2 * HEAD : 3 * HEAD] = low(turn_back(dk, cos_ref[...], sin_ref[...]))
        out_ref[:, 3 * HEAD :] = low(dv_ref[...])


def attention_specs(rows, block, groups):
    q_spec = pl.BlockSpec((block, 2 * HEAD), lambda g, i: (i, 2 * g))
    k_spec = pl.BlockSpec((rows, HEAD), lambda g, i: (0, 4 * g + 2))
    v_spec = pl.BlockSpec((rows, HEAD), lambda g, i: (0, 4 * g + 3))
    lab_spec = pl.BlockSpec((rows, 1), lambda g, i: (0, 0))
    row_spec = pl.BlockSpec((8, block), lambda g, i: (0, i))
    o_spec = pl.BlockSpec((block, 2 * HEAD), lambda g, i: (i, g))
    lse_spec = pl.BlockSpec((None, None, 1, 2 * block), lambda g, i: (g, i, 0, 0))
    return q_spec, k_spec, v_spec, lab_spec, row_spec, o_spec, lse_spec


def attend(qkv, label_col, label_rows, trunk, leaf_begin, block):
    rows = qkv.shape[0]
    groups = qkv.shape[1] // (4 * HEAD)
    blocks = rows // block
    q_spec, k_spec, v_spec, lab_spec, row_spec, o_spec, lse_spec = attention_specs(rows, block, groups)
    pairs = groups * 2 * rows * rows // 2
    return pl.pallas_call(
        functools.partial(attend_kernel, trunk, leaf_begin, block),
        grid=(groups, blocks),
        in_specs=[q_spec, k_spec, v_spec, lab_spec, row_spec],
        out_specs=[o_spec, lse_spec],
        out_shape=[
            jax.ShapeDtypeStruct((rows, groups * 2 * HEAD), jnp.bfloat16),
            jax.ShapeDtypeStruct((groups, blocks, 1, 2 * block), jnp.float32),
        ],
        scratch_shapes=[pltpu.VMEM((HEAD, rows), jnp.bfloat16)],
        compiler_params=pltpu.CompilerParams(vmem_limit_bytes=VMEM_LIMIT),
        cost_estimate=cost(4 * 4 * pairs * HEAD, 20 * rows * HEAD * 2),
        name="attend",
    )(qkv, qkv, qkv, label_col, label_rows)


def attend_back(qkv, attn, attn_grad, label_col, label_rows, lse, cosine, sine, trunk, leaf_begin, block):
    rows = qkv.shape[0]
    groups = qkv.shape[1] // (4 * HEAD)
    blocks = rows // block
    q_spec, k_spec, v_spec, lab_spec, row_spec, o_spec, lse_spec = attention_specs(rows, block, groups)
    table = pl.BlockSpec((rows, HEAD), lambda g, i: (0, 0))
    pairs = groups * 2 * rows * rows // 2
    return pl.pallas_call(
        functools.partial(attend_back_kernel, trunk, leaf_begin, block, blocks),
        grid=(groups, blocks),
        in_specs=[q_spec, k_spec, v_spec, o_spec, o_spec, lab_spec, row_spec, lse_spec, table, table],
        out_specs=pl.BlockSpec((rows, 4 * HEAD), lambda g, i: (0, g)),
        out_shape=jax.ShapeDtypeStruct((rows, groups * 4 * HEAD), jnp.bfloat16),
        scratch_shapes=[
            pltpu.VMEM((HEAD, rows), jnp.bfloat16),
            pltpu.VMEM((rows, HEAD), jnp.float32),
            pltpu.VMEM((rows, HEAD), jnp.float32),
        ],
        compiler_params=pltpu.CompilerParams(vmem_limit_bytes=VMEM_LIMIT),
        cost_estimate=cost(10 * 4 * pairs * HEAD, 40 * rows * HEAD * 2),
        name="attend_back",
    )(qkv, qkv, qkv, attn, attn_grad, label_col, label_rows, lse, cosine, sine)


def quarters_out(acc, out_refs):
    width = out_refs[0].shape[1]
    for i, ref in enumerate(out_refs):
        ref[...] = low(acc[:, i * width : (i + 1) * width])


def mix_kernel(a_ref, near_ref, far_ref, *out_refs):
    groups = near_ref.shape[0]
    span = near_ref.shape[2]
    for i, out_ref in enumerate(out_refs):
        w_ref = (near_ref, far_ref)[i // 2]
        acc = sum(
            mxu(a_ref[:, g * span : (g + 1) * span], w_ref[g, i % 2], NN) for g in range(groups)
        )
        out_ref[...] = low(acc)


def sum_out_kernel(count, *refs):
    a_refs = refs[:count]
    w_refs, out_refs = refs[count:-4], refs[-4:]
    acc = None
    left = list(a_refs)
    at = 0
    for w in w_refs:
        depth = w.shape[0]
        part = mxu(left[0][:, at : at + depth], w[...], NN)
        acc = part if acc is None else acc + part
        at += depth
        if at == left[0].shape[1]:
            left.pop(0)
            at = 0
    quarters_out(acc, out_refs)


def project_back_kernel(d_ref, near_ref, far_ref, *out_refs):
    groups = near_ref.shape[0]
    span = near_ref.shape[2]
    for i, w_ref in enumerate((near_ref, far_ref)):
        acc = sum(mxu(d_ref[:, g * span : (g + 1) * span], w_ref[g], NT) for g in range(groups))
        quarters_out(acc, out_refs[2 * i : 2 * i + 2])


def attn_grad_kernel(h0, h1, h2, h3, near_ref, far_ref, out_ref):
    groups = near_ref.shape[0]
    span = near_ref.shape[2]
    for g in range(groups):
        acc = sum(
            mxu(h[...], (near_ref, far_ref)[i // 2][g, i % 2], NT)
            for i, h in enumerate((h0, h1, h2, h3))
        )
        out_ref[:, g * span : (g + 1) * span] = low(acc)


def gate_up_kernel(*refs):
    x_refs, w_refs, out_refs = refs[:4], refs[4:10], refs[10:14]
    xs_ref = refs[14]
    width = x_refs[0].shape[1]
    for i, x in enumerate(x_refs):
        xs_ref[:, i * width : (i + 1) * width] = x[...]
    normed = xs_ref[...]
    outs = list(out_refs)
    at = 0
    for w_ref in w_refs:
        for start in range(0, w_ref.shape[0], 512):
            size = min(512, w_ref.shape[0] - start)
            product = mxu(normed, w_ref[start : start + size, :], NT)
            outs[0][:, at : at + size] = low(product)
            at += size
        if at == outs[0].shape[1]:
            outs.pop(0)
            at = 0


def hidden_kernel(*refs):
    g_refs, gate_refs, up_refs, w_refs = refs[:4], refs[4:6], refs[6:8], refs[8:11]
    out_refs = refs[11:17]
    gs_ref = refs[17]
    width = g_refs[0].shape[1]
    for i, g in enumerate(g_refs):
        gs_ref[:, i * width : (i + 1) * width] = g[...]
    grads = gs_ref[...]
    unit = 256
    places = [(0, w_refs[0], i, i) for i in range(0, w_refs[0].shape[0], unit)]
    places += [(1, w_refs[1], i, i) for i in range(0, w_refs[1].shape[0], unit)]
    first = w_refs[1].shape[0]
    places += [(1, w_refs[2], i, first + i) for i in range(0, w_refs[2].shape[0], unit)]
    for side, w_ref, row, at in places:
        dgate_ref, dup_ref, hid_ref = out_refs[3 * side : 3 * side + 3]
        cols = slice(at, at + unit)
        gate = wide(gate_refs[side][:, cols])
        upper = wide(up_refs[side][:, cols])
        hidden_grad = mxu(grads, w_ref[row : row + unit, :], NT)
        sigma = jax.nn.sigmoid(gate)
        silu_value = gate * sigma
        hid_ref[:, cols] = low(silu_value * upper)
        dgate_ref[:, cols] = low(hidden_grad * upper * sigma * (1.0 + gate * (1.0 - sigma)))
        dup_ref[:, cols] = low(hidden_grad * silu_value)


def pass_kernel(where_ref, in_ref, out_ref):
    out_ref[...] = in_ref[...]


def next_blocks(gathered, z, planes):
    rows, width = gathered.shape
    unit = rows // planes
    return pl.pallas_call(
        pass_kernel,
        grid_spec=pltpu.PrefetchScalarGridSpec(
            num_scalar_prefetch=1,
            grid=(planes - 1,),
            in_specs=[pl.BlockSpec((unit, width), lambda i, w: (lax.rem(w[0] + 1 + i, planes), 0))],
            out_specs=pl.BlockSpec((unit, width), lambda i, w: (i, 0)),
        ),
        out_shape=jax.ShapeDtypeStruct((rows - unit, width), gathered.dtype),
        compiler_params=pltpu.CompilerParams(vmem_limit_bytes=VMEM_LIMIT),
        cost_estimate=cost(0, 4 * rows * width),
        name="next_blocks",
    )(z.reshape(1), gathered)


def turned_grad_kernel(count, where_ref, *refs):
    weight_grad_kernel(count, 0, *refs)


def turned_grad(a, bs, z, planes, name):
    rows, m = a.shape
    n = sum(b.shape[1] for b in bs)
    unit = m // planes
    in_specs = [
        pl.BlockSpec((rows, unit), lambda i, w: (0, lax.rem(i + planes - w[0], planes)))
    ]
    for b in bs:
        in_specs.append(
            pl.BlockSpec(b.shape, lambda i, w: (0, 0), pipeline_mode=pl.Buffered(1))
        )
    return pl.pallas_call(
        functools.partial(turned_grad_kernel, len(bs)),
        grid_spec=pltpu.PrefetchScalarGridSpec(
            num_scalar_prefetch=1,
            grid=(planes,),
            in_specs=in_specs,
            out_specs=pl.BlockSpec((unit, n), lambda i, w: (i, 0)),
        ),
        out_shape=jax.ShapeDtypeStruct((m, n), jnp.bfloat16),
        compiler_params=pltpu.CompilerParams(vmem_limit_bytes=VMEM_LIMIT),
        cost_estimate=cost(2 * rows * m * n, 2 * (rows * m + rows * n + m * n)),
        name=name,
    )(z.reshape(1), a, *bs)


def ffn_home_kernel(turned, where_ref, *refs):
    part_refs, out_ref = refs[:4], refs[4]
    step = pl.program_id(0)
    at_col, at_core, at_x = step // 4, lax.rem(step // 2, 2), lax.rem(step, 2)
    other_col = jnp.where(at_col == where_ref[0], 0, 1)
    want = 2 * jnp.where(at_x == where_ref[1], 0, 1) + jnp.where(at_core == where_ref[2], 0, 1)
    quarter = part_refs[0].shape[2] // 2
    for j in range(4):

        @pl.when(want == j)
        def _(part=part_refs[j]):
            for h in range(2):
                start = at_core * quarter if h == 0 else (1 - at_core) * quarter
                place = pl.ds(pl.multiple_of(start, quarter), quarter)
                values = wide(part[other_col, :, h * quarter : (h + 1) * quarter])
                if turned:
                    out_ref[place, :] = values.T
                else:
                    out_ref[:, place] = values


def ffn_home(where, parts, at, unit, turned, name):
    half = parts[0].shape[2]
    whole = pl.BlockSpec((2, unit, half), lambda i, w: (0, at, 0), pipeline_mode=pl.Buffered(1))
    if turned:
        spec, shape = pl.BlockSpec((half, unit), lambda i, w: (0, i)), (half, 8 * unit)
    else:
        spec, shape = pl.BlockSpec((unit, half), lambda i, w: (i, 0)), (8 * unit, half)
    return pl.pallas_call(
        functools.partial(ffn_home_kernel, turned),
        grid_spec=pltpu.PrefetchScalarGridSpec(
            num_scalar_prefetch=1, grid=(8,), in_specs=[whole] * 4, out_specs=spec
        ),
        out_shape=jax.ShapeDtypeStruct(shape, jnp.float32),
        compiler_params=pltpu.CompilerParams(vmem_limit_bytes=VMEM_LIMIT),
        cost_estimate=cost(0, 8 * unit * half * 6),
        name=name,
    )(where, *parts)


def weight_grad_kernel(count, split, *refs):
    a_ref = refs[0]
    b_refs = refs[1 : 1 + count]
    o_refs = refs[1 + count :]
    left = a_ref[...].T
    for i, b in enumerate(b_refs):
        width = b.shape[1]
        acc = low(mxu(left, b[...], NN))
        if split:
            for j in range(split):
                o_refs[0][j] = acc[:, j * width // split : (j + 1) * width // split]
        elif len(o_refs) == 1:
            o_refs[0][:, i * width : (i + 1) * width] = acc
        else:
            o_refs[i][...] = acc


def weight_grad(a, bs, block, name, joined=True, split=0):
    rows, m = a.shape
    n = sum(b.shape[1] for b in bs)
    in_specs = [pl.BlockSpec((rows, block), lambda i: (0, i))]
    for b in bs:
        in_specs.append(
            pl.BlockSpec(b.shape, lambda i: (0, 0), pipeline_mode=pl.Buffered(1))
        )
    if split:
        out_specs = [pl.BlockSpec((split, block, n // split), lambda i: (0, i, 0))]
        shapes = [(split, m, n // split)]
    else:
        widths = [n] if joined else [b.shape[1] for b in bs]
        out_specs = [pl.BlockSpec((block, w), lambda i: (i, 0)) for w in widths]
        shapes = [(m, w) for w in widths]
    outs = pl.pallas_call(
        functools.partial(weight_grad_kernel, len(bs), split),
        grid=(m // block,),
        in_specs=in_specs,
        out_specs=out_specs,
        out_shape=[jax.ShapeDtypeStruct(shape, jnp.bfloat16) for shape in shapes],
        compiler_params=pltpu.CompilerParams(vmem_limit_bytes=VMEM_LIMIT),
        cost_estimate=cost(2 * rows * m * n, 2 * (rows * m + rows * n + m * n)),
        name=name,
    )(a, *bs)
    return outs if len(outs) > 1 else outs[0]


def take(a, index, axis):
    return lax.dynamic_index_in_dim(a, index, axis, keepdims=False)


def in_order(index, mine, other, axis=0):
    first = jnp.where(index == 0, mine, other)
    second = jnp.where(index == 0, other, mine)
    return jnp.stack([first, second], axis=axis)


def spread(a):
    b = swap_col(a)
    return [a, b, swap_core(a), swap_core(b)]


def collect_core(parts):
    own, own_other, send, send_other = parts
    outgoing = low(wide(own_other) + wide(swap_core(send_other)))
    return own, swap_core(send), outgoing


def collect_col(own, got, outgoing):
    return wide(own) + wide(got) + wide(swap_col(outgoing))


def small_sum(v):
    cross = lax.ppermute(v, ("dp", "col"), CROSS_SWAP)
    return (v + swap_core(v)) + (swap_col(v) + cross)


def tree_body(
    tokens,
    out_grad,
    path,
    positions,
    w_query,
    w_key,
    w_value,
    w_out,
    w_gate,
    w_up,
    w_down,
    gain_attn,
    gain_ffn,
):
    dp = lax.axis_index("dp")
    x = dp // 2
    c = lax.rem(dp, 2)
    z = lax.axis_index("row")
    y = lax.axis_index("col")
    micro, local_rows, half = tokens.shape
    quarter = half // 2
    rows = path.shape[1]
    planes = lax.axis_size("row")
    features = 2 * half
    block = 256

    def to_trees(a):
        mine = lax.dynamic_slice_in_dim(a, c * quarter, quarter, 2)
        other = swap_core(lax.dynamic_slice_in_dim(a, (1 - c) * quarter, quarter, 2))
        return in_order(c, mine, other).reshape(planes * local_rows, quarter)

    def of_core(trees):
        trees = trees.reshape(2, micro, local_rows, quarter)
        return take(trees, c, 0), take(trees, 1 - c, 0)

    def by_feature(mine, other):
        return in_order(c, mine, swap_core(other), 2).reshape(micro, local_rows, half)

    groups = w_key.shape[1] // HEAD
    share = quarter // 2
    unit = w_gate.shape[1] // 8

    def project_piece(g):
        at = c * quarter + x * share
        return jnp.concatenate(
            [
                lax.dynamic_slice(w_query, (at, g * 2 * HEAD), (share, 2 * HEAD)),
                lax.dynamic_slice(w_key, (at, g * HEAD), (share, HEAD)),
                lax.dynamic_slice(w_value, (at, g * HEAD), (share, HEAD)),
            ],
            axis=1,
        )

    def mix_piece(g):
        return lax.dynamic_slice(w_out, ((g * 2 + x) * HEAD, c * quarter), (HEAD, quarter))

    def by_core(a):
        return jnp.where(c == 0, a, jnp.concatenate([a[:, quarter:], a[:, :quarter]], axis=1))

    def four(kept, got):
        return jnp.concatenate(
            [kept[:, :quarter], got[:, :quarter], kept[:, quarter:], got[:, quarter:]], axis=1
        )

    project_sent = project_piece(1 - y)
    project_mine = jnp.stack([project_piece(y), swap_col(project_sent)])
    trees = to_trees(tokens)
    block_in = lax.all_to_all(trees, "row", 0, 0, tiled=True)
    def hidden_piece(j, xh):
        at = ((2 * j + c) * 2 + xh) * unit
        return [
            by_core(lax.dynamic_slice_in_dim(w_gate, at, unit, 1).T),
            by_core(lax.dynamic_slice_in_dim(w_up, at, unit, 1).T),
            by_core(lax.dynamic_slice_in_dim(w_down, at, unit, 0)),
        ]

    sent = jnp.concatenate([*hidden_piece(1 - y, x), jnp.tile(mix_piece(1 - y), (1, 2))])
    got = swap_col(after(sent, project_sent))
    project_all = lax.all_gather(project_mine, "row", axis=0)

    marks = jnp.concatenate([path, positions[:, :, None]], axis=2)
    marks = jnp.transpose(marks, (2, 0, 1))
    marks = in_order(c, marks, swap_core(marks), 1).reshape(4, 2 * micro, rows)
    marks = take(marks, z, 1)
    cosine, sine = rope_tables(marks[3])
    sign = jnp.where(jnp.arange(HEAD) < HEAD // 2, -1.0, 1.0).astype(jnp.float32)
    sine = sine * sign[None, :]
    label_col = marks[0][:, None]
    label_rows = jnp.pad(marks, ((0, 4), (0, 0)))

    hidden_mine = [
        four(kept, got[i * unit : (i + 1) * unit])
        for i, kept in enumerate(hidden_piece(y, x))
    ]
    mix_mine = jnp.stack([mix_piece(y), got[3 * unit :, :quarter]])
    near_sent = jnp.concatenate(hidden_piece(1 - y, 1 - x))
    near_got = swap_col(after(near_sent, mix_mine))
    hidden_near = [
        four(kept, near_got[i * unit : (i + 1) * unit])
        for i, kept in enumerate(hidden_piece(y, 1 - x))
    ]

    def gain_order(gain):
        kept = gain.reshape(2, quarter)
        both = jnp.stack([kept, swap_col(kept)], axis=1)
        both = jnp.where(c == 0, both, both[::-1])
        return both.reshape(1, features)

    gain_attn_all = gain_order(gain_attn)
    gain_attn_own = gain_attn_all[:, :quarter]
    gain_ffn_own = lax.dynamic_slice_in_dim(gain_ffn, c * quarter, quarter, 0)[None, :]

    (
        project_all, block_in, mix_mine, gate_piece, up_piece, down_piece,
        gate_near, up_near, down_near, cosine, sine, label_col, label_rows, gain_attn_all,
    ) = lax.optimization_barrier(
        (
            project_all, block_in, mix_mine, *hidden_mine, *hidden_near,
            cosine, sine, label_col, label_rows, gain_attn_all,
        )
    )

    pieces = spread(block_in)
    mix_all = lax.all_gather(mix_mine, "row", axis=0)
    gate_mine = lax.all_gather(gate_piece, "row", axis=0, tiled=True)
    up_mine = lax.all_gather(after(up_piece, mix_all), "row", axis=0, tiled=True)
    down_mine = lax.all_gather(after(down_piece, gate_mine), "row", axis=0, tiled=True)
    gate_next, up_next, down_next = (
        next_blocks(u, z, planes) for u in (gate_mine, up_mine, down_mine)
    )
    gate_far, up_far, down_far = (swap_x(u) for u in (gate_next, up_next, down_next))

    def of_core_pairs(mine, other):
        both = in_order(x, mine, other, 2)
        pairs = both.reshape((2, planes // 2) + both.shape[1:])
        return take(pairs, c, 0), swap_core(take(pairs, 1 - c, 0))

    near, far = of_core_pairs(project_all, swap_x(project_all))
    w_near = near.reshape(groups, half, 4 * HEAD)
    w_far = far.reshape(groups, half, 4 * HEAD)

    normed_attn, qkv, ratio_attn = rows_call(
        project_kernel,
        block,
        [*pieces, cosine, sine],
        [gain_attn_all, w_near, w_far],
        [(features, jnp.bfloat16), (groups * 4 * HEAD, jnp.bfloat16), (1, jnp.float32)],
        2 * rows * features * groups * 4 * HEAD,
        "project",
    )
    near, far = of_core_pairs(mix_all, after(swap_x(mix_all), qkv))
    attn, lse = attend(after(qkv, near), label_col, label_rows, TRUNK, LEAF_BEGIN, block)
    mix_shape = (groups, 2, 2 * HEAD, quarter)
    m_near, m_far = near.reshape(mix_shape), after(far, attn).reshape(mix_shape)
    parts = rows_call(
        mix_kernel,
        2 * block,
        [attn],
        [m_near, m_far],
        [(quarter, jnp.bfloat16)] * 4,
        2 * rows * features * groups * 2 * HEAD,
        "mix",
    )
    cotangent = lax.all_to_all(to_trees(out_grad), "row", 0, 0, tiled=True)
    parts[1] = after(parts[1], cotangent, gate_next)
    own, got, outgoing = collect_core(parts)
    middle = wide(block_in) + collect_col(own, got, outgoing)
    square = small_sum(jnp.sum(middle * middle, axis=1))
    ratio_ffn = lax.rsqrt(square / features + EPSILON)[:, None]
    normed_ffn = middle * ratio_ffn
    ffn_near = after(low(normed_ffn * gain_ffn_own), up_next, gate_far)
    ffn_across = swap_col(ffn_near)
    ffn_pieces = [ffn_near, ffn_across, swap_core(ffn_near), swap_core(ffn_across)]
    grad_near, grad_across = cotangent, swap_col(after(cotangent, ffn_pieces[1]))
    gate_m, up_m, gate_o, up_o = rows_call(
        gate_up_kernel,
        block,
        ffn_pieces,
        [gate_mine, up_mine, gate_near, gate_far, up_near, up_far],
        [(planes * unit, jnp.bfloat16)] * 4,
        2 * rows * features * 4 * planes * unit,
        "gate_up",
        [pltpu.VMEM((block, features), jnp.bfloat16)],
    )
    grad_pieces = [
        grad_near,
        grad_across,
        swap_core(after(grad_near, ffn_pieces[3])),
        swap_core(after(grad_across, gate_m)),
    ]
    dgate_m, dup_m, hid_m, dgate_o, dup_o, hid_o = rows_call(
        hidden_kernel,
        block,
        [*grad_pieces, gate_m, gate_o, up_m, up_o],
        [down_mine, down_near, down_far],
        [(planes * unit, jnp.bfloat16)] * 6,
        2 * rows * features * 2 * planes * unit,
        "hidden",
        [pltpu.VMEM((block, features), jnp.bfloat16)],
    )

    def unit_grad(a, pieces_of, name, before):
        return weight_grad(after(a, before), pieces_of, 2 * block, name)

    def to_row(total):
        return lax.psum_scatter(total, "row", scatter_dimension=0, tiled=True)

    down_other = turned_grad(hid_o, grad_pieces, z, planes, "down_grad_other")
    parts = rows_call(
        functools.partial(sum_out_kernel, 4),
        2 * block,
        [after(dgate_m, down_other), dup_m, dgate_o, dup_o],
        [gate_mine, up_mine, gate_near, gate_far, up_near, up_far],
        [(quarter, jnp.bfloat16)] * 4,
        2 * rows * features * 4 * planes * unit,
        "pair_back",
    )
    gate_other = turned_grad(after(dgate_o, parts[0]), ffn_pieces, z, planes, "gate_grad_other")
    down_own = unit_grad(hid_m, grad_pieces, "down_grad_mine", gate_other)
    parts[1] = after(parts[1], down_own)
    own, got, outgoing = collect_core(parts)
    up_other = turned_grad(after(dup_o, outgoing), ffn_pieces, z, planes, "up_grad_other")
    gate_own = unit_grad(dgate_m, ffn_pieces, "gate_grad_mine", up_other)
    down_total = low(wide(after(down_own, gate_own)) + wide(swap_x(down_other)))
    down_sum = to_row(down_total)
    normed_ffn_grad = collect_col(after(own, down_total), got, outgoing)

    def norm_back(grad, ratio, normed, gain):
        scaled = grad * gain
        inner = small_sum(jnp.sum(scaled * normed, axis=1))[:, None] / features
        return ratio * (scaled - normed * inner), jnp.sum(grad * normed, axis=0)

    middle_back, gain_ffn_part = norm_back(normed_ffn_grad, ratio_ffn, normed_ffn, gain_ffn_own)
    middle_grad = wide(cotangent) + middle_back
    middle_low = low(middle_grad)
    up_own = unit_grad(dup_m, ffn_pieces, "up_grad_mine", middle_low)
    where = jnp.stack([y, x, c]).astype(jnp.int32)

    def unit_halves(total):
        kept = jnp.concatenate([total[:, :quarter], total[:, half : half + quarter]], axis=1)
        sent = jnp.concatenate([total[:, quarter:half], total[:, half + quarter :]], axis=1)
        return kept, sent

    def unit_parts(kept, sent, first, second):
        both = jnp.stack([kept, after(swap_col(sent), first)])
        over = after(swap_x(both), second)
        return [both, swap_core(both), over, swap_core(over)]

    out_parts = rows_call(
        functools.partial(sum_out_kernel, 2),
        2 * block,
        [after(hid_m, up_own), hid_o],
        [down_mine, down_near, down_far],
        [(quarter, jnp.bfloat16)] * 4,
        2 * rows * features * 2 * planes * unit,
        "down",
    )
    middle_across = after(swap_col(middle_low), out_parts[0])
    middle_pieces = [middle_low, middle_across, swap_core(middle_low), swap_core(middle_across)]
    attn_grad = rows_call(
        attn_grad_kernel,
        2 * block,
        middle_pieces,
        [m_near, m_far],
        [(groups * 2 * HEAD, jnp.bfloat16)],
        2 * rows * features * groups * 2 * HEAD,
        "attn_grad",
    )[0]
    gate_total = low(wide(after(gate_own, attn_grad)) + wide(swap_x(gate_other)))
    gate_sum = to_row(gate_total)
    out_parts[1] = after(out_parts[1], gate_total)
    out_own, out_got, out_outgoing = collect_core(out_parts)
    qkv_grad = attend_back(
        qkv, attn, after(attn_grad, out_outgoing), label_col, label_rows, lse, cosine, sine,
        TRUNK, LEAF_BEGIN, block,
    )
    output = low(after(middle, qkv_grad) + collect_col(out_own, out_got, out_outgoing))
    up_total = low(wide(after(up_own, output)) + wide(swap_x(up_other)))
    up_sum = to_row(up_total)
    parts = rows_call(
        project_back_kernel,
        2 * block,
        [after(qkv_grad, up_total)],
        [w_near, w_far],
        [(quarter, jnp.bfloat16)] * 4,
        2 * rows * features * groups * 4 * HEAD,
        "project_back",
    )
    output_tree = lax.all_to_all(output, "row", 0, 0, tiled=True)
    own, got, outgoing = collect_core(parts)
    project_grad = weight_grad(
        normed_attn, [after(qkv_grad, outgoing)], 2 * block, "project_grad", split=groups
    )
    mix_grads = weight_grad(
        attn,
        [after(middle_pieces[0], project_grad), *middle_pieces[1:]],
        groups * 2 * HEAD,
        "mix_grad",
        joined=False,
    )

    project_parts = project_grad.reshape(groups, 2, 2, 2, share, 4 * HEAD)
    mix_parts = jnp.stack([m.reshape(groups, 2, HEAD, quarter) for m in mix_grads], axis=1)
    mix_parts = mix_parts.reshape(groups, 2, 2, 2, HEAD, quarter)

    def of_x(index):
        return jnp.concatenate([take(project_parts, index, 3), take(mix_parts, index, 3)], axis=3)

    attn_sent = of_x(1 - x)
    attn_kept = of_x(after(x, attn_sent))
    normed_attn_grad = collect_col(after(own, attn_kept), got, outgoing)
    normed_attn_own = wide(block_in) * ratio_attn
    input_back, gain_attn_part = norm_back(
        normed_attn_grad, ratio_attn, normed_attn_own, gain_attn_own
    )
    input_low = low(middle_grad + input_back)
    input_tree = lax.all_to_all(input_low, "row", 0, 0, tiled=True)
    home_kept, home_sent = unit_halves(
        jnp.concatenate([after(down_sum, input_low), gate_sum])
    )
    output, output_sent = of_core(after(output_tree, home_sent))
    home_both = jnp.stack([home_kept, after(swap_col(home_sent), output_sent)])
    home_over = swap_x(home_both)
    attn_total = low(wide(after(attn_kept, home_both)) + wide(swap_x(attn_sent)))
    by_plane = in_order(c, attn_total[:, 0], swap_core(attn_total[:, 1]))
    by_plane = by_plane.reshape((planes,) + by_plane.shape[2:])
    attn_sum = lax.psum_scatter(by_plane, "row", scatter_dimension=0, tiled=False)
    output = by_feature(after(output, by_plane), output_sent)
    up_kept, up_sent = unit_halves(after(up_sum, output))
    home_over = after(home_over, up_sent)
    home_parts = [home_both, swap_core(home_both), home_over, swap_core(home_over)]
    down_out = ffn_home(where, home_parts, 0, unit, False, "down_home")
    gate_out = ffn_home(where, home_parts, 1, unit, True, "gate_home")
    attn_sum = after(attn_sum, down_out, gate_out)
    home = in_order(y, attn_sum[0], swap_col(attn_sum[1]))
    up_parts = unit_parts(up_kept, up_sent, gate_out, home)
    up_out = ffn_home(where, up_parts, 0, unit, True, "up_home")
    home = in_order(x, home, after(swap_x(home), up_out))
    input_grad = by_feature(*of_core(after(input_tree, up_out)))
    home = in_order(c, home, swap_core(home))
    mix_home = home[:, :, :, share:]
    out_out = wide(jnp.transpose(mix_home, (2, 1, 3, 0, 4)).reshape(groups * 2 * HEAD, half))
    project_home = jnp.transpose(home[:, :, :, :share], (0, 1, 3, 2, 4))
    project_home = project_home.reshape(half, groups, 4 * HEAD)
    query_out = wide(project_home[:, :, : 2 * HEAD].reshape(half, groups * 2 * HEAD))
    key_out = wide(project_home[:, :, 2 * HEAD : 3 * HEAD].reshape(half, groups * HEAD))
    value_out = wide(project_home[:, :, 3 * HEAD :].reshape(half, groups * HEAD))

    gains = jnp.stack([gain_attn_part, gain_ffn_part])
    gains = gains + shift(gains, ROW_SECOND)
    gains = gains + shift(gains, ROW_SWAP)
    gains = gains + swap_x(gains)
    gains = in_order(c, gains, swap_core(gains), 1)
    gain_attn_out = gains[0].reshape(half)
    gain_ffn_out = gains[1].reshape(half)
    return (
        output,
        input_grad,
        query_out,
        key_out,
        value_out,
        out_out,
        gate_out,
        up_out,
        down_out,
        gain_attn_out,
        gain_ffn_out,
    )


def solution(mesh):
    in_specs = (
        P(None, ("dp", "row"), "col"),
        P(None, ("dp", "row"), "col"),
        P(None, "dp", None),
        P(None, "dp"),
        P("col", "row"),
        P("col", "row"),
        P("col", "row"),
        P("row", "col"),
        P("col", "row"),
        P("col", "row"),
        P("row", "col"),
        P("col"),
        P("col"),
    )
    out_specs = (
        P(None, ("dp", "row"), "col"),
        P(None, ("dp", "row"), "col"),
        P("col", "row"),
        P("col", "row"),
        P("col", "row"),
        P("row", "col"),
        P("col", "row"),
        P("col", "row"),
        P("row", "col"),
        P("col"),
        P("col"),
    )
    sizes = dict(mesh.shape)
    fits = sizes == {"dp": 4, "row": 4, "col": 2}
    chosen = tree_body if fits else body
    return jax.shard_map(chosen, mesh=mesh, in_specs=in_specs, out_specs=out_specs, check_vma=False)
```

```python
import functools
import math

import jax
import jax.numpy as jnp
from jax import lax
from jax.experimental import pallas as pl
from jax.experimental.pallas import tpu as pltpu
from jax.sharding import PartitionSpec as P

D = 2048
HEADS = 16
KV_HEADS = 8
HEAD = 128


EPSILON = 1e-05
THETA = 1000000.0


def contract_rows(left, right):
    return lax.dot_general(
        left, right, (((0,), (0,)), ((), ())), preferred_element_type=jnp.float32
    )


def contract_cols(left, right):
    return lax.dot_general(
        left, right, (((1,), (1,)), ((), ())), preferred_element_type=jnp.float32
    )


def rows_gather(values):
    return lax.all_gather(values, "row", axis=0, tiled=True)


def cols_gather(values):
    return lax.all_gather(values, "col", axis=0, tiled=True)


def cols_reduce(part_fn, rows):
    return lax.psum_scatter(
        part_fn(jnp.int32(0), rows * lax.axis_size("col")), "col", scatter_dimension=0, tiled=True
    )


def rows_reduce(part_fn, rows):
    return lax.psum_scatter(
        part_fn(jnp.int32(0), rows * lax.axis_size("row")).astype(jnp.bfloat16),
        "row",
        scatter_dimension=0,
        tiled=True,
    ).astype(jnp.float32)


def feature_sums(values):
    return lax.psum(jnp.sum(values, axis=1), "col")


def sliced_product(whole, weight, transpose):

    def part_fn(start, count):
        if transpose:
            return contract_cols(whole, weight)
        return jnp.dot(whole, weight, preferred_element_type=jnp.float32)

    return part_fn


def rope_tables(positions):
    half = HEAD // 2
    frequency = jnp.power(THETA, -2.0 * jnp.arange(half, dtype=jnp.float32) / HEAD)
    angles = positions.astype(jnp.float32)[:, None] * frequency[None, :]
    angles = jnp.concatenate([angles, angles], axis=1)
    return (jnp.cos(angles), jnp.sin(angles))


def rotate(values, cosine, sine):
    half = values.shape[-1] // 2
    turned = jnp.concatenate([-values[..., half:], values[..., :half]], axis=-1)
    return values * cosine[:, None, :] + turned * sine[:, None, :]


def rotate_back(grads, cosine, sine):
    half = grads.shape[-1] // 2
    scaled = grads * sine[:, None, :]
    turned = jnp.concatenate([scaled[..., half:], -scaled[..., :half]], axis=-1)
    return grads * cosine[:, None, :] + turned


def norm_forward(values, gain):
    ratio = lax.rsqrt(feature_sums(values * values) / D + EPSILON)[:, None]
    normed = values * ratio
    return (ratio, normed, (normed * gain).astype(jnp.bfloat16))


def norm_backward(grad, ratio, normed, gain):
    scaled = grad * gain
    inner = feature_sums(scaled * normed)[:, None] / D
    return (ratio * (scaled - normed * inner), jnp.sum(grad * normed, axis=0))


def body(
    tokens,
    out_grad,
    path,
    positions,
    w_query,
    w_key,
    w_value,
    w_out,
    w_gate,
    w_up,
    w_down,
    gain_attn,
    gain_ffn,
):
    query_width = w_query.shape[1]
    key_width = w_key.shape[1]
    hidden_width = w_gate.shape[1]
    local_heads = key_width // HEAD
    group = HEADS // KV_HEADS
    scale = 1.0 / math.sqrt(HEAD)
    block_rows = path.shape[1]
    local_rows = tokens.shape[1]
    query_rows = block_rows // lax.axis_size("col")
    first = lax.axis_index("col") * query_rows
    w_project = jnp.concatenate([w_query, w_key, w_value], axis=1)
    w_pair = jnp.concatenate([w_gate, w_up], axis=1)
    project_start = jnp.zeros(w_project.shape, jnp.float32)
    pair_start = jnp.zeros(w_pair.shape, jnp.float32)
    down_start = jnp.zeros(w_down.shape, jnp.float32)

    def micro_step(carry, batch):
        grad_project, grad_out, grad_pair, grad_down, grad_gain_attn, grad_gain_ffn = carry
        block, cotangent, block_path, block_place = batch
        inputs = block.astype(jnp.float32)
        cosine, sine = rope_tables(lax.dynamic_slice_in_dim(block_place, first, query_rows, 0))
        query_path = lax.dynamic_slice_in_dim(block_path, first, query_rows, 0)
        key_labels = block_path[:, 0]
        query_place = first + jnp.arange(query_rows, dtype=jnp.int32)
        key_place = jnp.arange(block_rows, dtype=jnp.int32)
        same_path = (
            (key_labels[None, :] == query_path[:, 0:1])
            | (key_labels[None, :] == query_path[:, 1:2])
            | (key_labels[None, :] == query_path[:, 2:3])
        )
        visible = same_path & (key_place[None, :] <= query_place[:, None])
        ratio_attn, normed_attn, input_attn = norm_forward(inputs, gain_attn)
        gathered_attn = rows_gather(input_attn)
        projected = cols_reduce(sliced_product(gathered_attn, w_project, False), query_rows)
        query = rotate(
            projected[:, :query_width].reshape(query_rows, -1, HEAD), cosine, sine
        ).astype(jnp.bfloat16)
        keys = rotate(
            projected[:, query_width : query_width + key_width].reshape(query_rows, -1, HEAD),
            cosine,
            sine,
        ).astype(jnp.bfloat16)
        values = projected[:, query_width + key_width :].astype(jnp.bfloat16)
        keys_all, values_all = (
            lax.all_gather(keys.reshape(query_rows, key_width), "col", axis=0, tiled=True),
            lax.all_gather(values, "col", axis=0, tiled=True),
        )
        query_groups = query.reshape(query_rows, local_heads, group, HEAD)
        key_heads = keys_all.reshape(block_rows, local_heads, HEAD)
        value_heads = values_all.reshape(block_rows, local_heads, HEAD)
        scores = (
            jnp.einsum(
                "ikgd,jkd->kgij", query_groups, key_heads, preferred_element_type=jnp.float32
            )
            * scale
        )
        scores = jnp.where(visible[None, None], scores, -jnp.inf)
        weights = jax.nn.softmax(scores, axis=-1)
        weights_low = weights.astype(jnp.bfloat16)
        mixed = jnp.einsum(
            "kgij,jkd->ikgd", weights_low, value_heads, preferred_element_type=jnp.float32
        )
        attn_low = mixed.reshape(query_rows, query_width).astype(jnp.bfloat16)
        attn_all = cols_gather(attn_low)
        branch_attn = rows_reduce(sliced_product(attn_all, w_out, False), local_rows)
        middle = inputs + branch_attn
        ratio_ffn, normed_ffn, input_ffn = norm_forward(middle, gain_ffn)
        gathered_ffn = rows_gather(input_ffn)
        pair = cols_reduce(sliced_product(gathered_ffn, w_pair, False), query_rows)
        gate = pair[:, :hidden_width]
        upper = pair[:, hidden_width:]
        sigma = jax.nn.sigmoid(gate)
        silu_value = gate * sigma
        hidden = (silu_value * upper).astype(jnp.bfloat16)
        hidden_all = cols_gather(hidden)
        branch_ffn = rows_reduce(sliced_product(hidden_all, w_down, False), local_rows)
        output = (middle + branch_ffn).astype(jnp.bfloat16)
        cotangent_all = rows_gather(cotangent)
        hidden_grad = cols_reduce(sliced_product(cotangent_all, w_down, True), query_rows)
        grad_down = grad_down + contract_rows(hidden_all, cotangent_all)
        gate_grad = hidden_grad * upper * sigma * (1.0 + gate * (1.0 - sigma))
        upper_grad = hidden_grad * silu_value
        pair_grad = jnp.concatenate([gate_grad, upper_grad], axis=1).astype(jnp.bfloat16)
        pair_all = cols_gather(pair_grad)
        normed_ffn_grad = rows_reduce(sliced_product(pair_all, w_pair, True), local_rows)
        grad_pair = grad_pair + contract_rows(gathered_ffn, pair_all)
        middle_back, gain_ffn_step = norm_backward(normed_ffn_grad, ratio_ffn, normed_ffn, gain_ffn)
        middle_grad = cotangent.astype(jnp.float32) + middle_back
        middle_low = middle_grad.astype(jnp.bfloat16)
        middle_all = rows_gather(middle_low)
        attn_grad = cols_reduce(sliced_product(middle_all, w_out, True), query_rows).astype(
            jnp.bfloat16
        )
        grad_out = grad_out + contract_rows(attn_all, middle_all)
        attn_heads = attn_grad.reshape(query_rows, local_heads, group, HEAD)
        weight_grad = jnp.einsum(
            "ikgd,jkd->kgij", attn_heads, value_heads, preferred_element_type=jnp.float32
        )
        score_grad = (
            weights * (weight_grad - jnp.sum(weights * weight_grad, axis=-1, keepdims=True))
        ).astype(jnp.bfloat16)
        query_grad = (
            jnp.einsum("kgij,jkd->ikgd", score_grad, key_heads, preferred_element_type=jnp.float32)
            * scale
        )
        key_part = (
            jnp.einsum(
                "kgij,ikgd->jkd", score_grad, query_groups, preferred_element_type=jnp.float32
            )
            * scale
        )
        value_part = jnp.einsum(
            "kgij,ikgd->jkd", weights_low, attn_heads, preferred_element_type=jnp.float32
        )
        key_grad, value_grad = (
            lax.psum_scatter(
                key_part.reshape(block_rows, key_width).astype(jnp.bfloat16),
                "col",
                scatter_dimension=0,
                tiled=True,
            ).astype(jnp.float32),
            lax.psum_scatter(
                value_part.reshape(block_rows, key_width).astype(jnp.bfloat16),
                "col",
                scatter_dimension=0,
                tiled=True,
            ).astype(jnp.float32),
        )
        query_back = rotate_back(query_grad.reshape(query_rows, -1, HEAD), cosine, sine).reshape(
            query_rows, query_width
        )
        key_back = rotate_back(key_grad.reshape(query_rows, -1, HEAD), cosine, sine).reshape(
            query_rows, key_width
        )
        projected_grad = jnp.concatenate([query_back, key_back, value_grad], axis=1).astype(
            jnp.bfloat16
        )
        projected_all = cols_gather(projected_grad)
        normed_attn_grad = rows_reduce(sliced_product(projected_all, w_project, True), local_rows)
        grad_project = grad_project + contract_rows(gathered_attn, projected_all)
        input_back, gain_attn_step = norm_backward(
            normed_attn_grad, ratio_attn, normed_attn, gain_attn
        )
        input_grad = (middle_grad + input_back).astype(jnp.bfloat16)
        carry = (
            grad_project,
            grad_out,
            grad_pair,
            grad_down,
            grad_gain_attn + gain_attn_step,
            grad_gain_ffn + gain_ffn_step,
        )
        return (carry, (output, input_grad))

    start = (
        project_start,
        jnp.zeros(w_out.shape, jnp.float32),
        pair_start,
        down_start,
        jnp.zeros(gain_attn.shape, jnp.float32),
        jnp.zeros(gain_ffn.shape, jnp.float32),
    )
    sums, (outputs, input_grads) = lax.scan(micro_step, start, (tokens, out_grad, path, positions))
    grad_project, grad_out, grad_pair, grad_down, grad_gain_attn, grad_gain_ffn = sums
    grad_project, grad_out, grad_pair, grad_down = (
        lax.psum(grad_project.astype(jnp.bfloat16), "dp").astype(jnp.float32),
        lax.psum(grad_out.astype(jnp.bfloat16), "dp").astype(jnp.float32),
        lax.psum(grad_pair.astype(jnp.bfloat16), "dp").astype(jnp.float32),
        lax.psum(grad_down.astype(jnp.bfloat16), "dp").astype(jnp.float32),
    )
    grad_gain_attn, grad_gain_ffn = lax.psum((grad_gain_attn, grad_gain_ffn), ("dp", "row"))
    query_part = grad_project[:, :query_width]
    key_part_grad = grad_project[:, query_width : query_width + key_width]
    value_part_grad = grad_project[:, query_width + key_width :]
    return (
        outputs,
        input_grads,
        query_part,
        key_part_grad,
        value_part_grad,
        grad_out,
        grad_pair[:, :hidden_width],
        grad_pair[:, hidden_width:],
        grad_down,
        grad_gain_attn,
        grad_gain_ffn,
    )


CORE_SWAP = [(0, 1), (1, 0), (2, 3), (3, 2)]
X_SWAP = [(0, 2), (2, 0), (1, 3), (3, 1)]
COL_SWAP = [(0, 1), (1, 0)]
CROSS_SWAP = [(2 * d + j, 2 * (d ^ 1) + 1 - j) for d in range(4) for j in range(2)]
ROW_SECOND = [(0, 2), (1, 3), (2, 0), (3, 1)]
ROW_SWAP = [(0, 1), (1, 0), (2, 3), (3, 2)]
LOG2E = 1.4426950408889634
TRUNK = 1024
LEAF_BEGIN = TRUNK + 4 * 128
SHARE_OF_COST = 8
VMEM_LIMIT = 58 * 1024 * 1024
NT = (((1,), (1,)), ((), ()))
TN = (((0,), (0,)), ((), ()))
NN = (((1,), (0,)), ((), ()))


def swap_core(a):
    return lax.ppermute(a, "dp", CORE_SWAP)


def swap_x(a):
    return lax.ppermute(a, "dp", X_SWAP)


def swap_col(a):
    return lax.ppermute(a, "col", COL_SWAP)


def shift(a, pairs):
    return lax.ppermute(a, "row", pairs)


def after(value, *deps):
    return lax.optimization_barrier((value, *deps))[0]


def cost(flops, moved):
    return pl.CostEstimate(
        flops=flops // SHARE_OF_COST, bytes_accessed=moved // SHARE_OF_COST, transcendentals=0
    )


def mxu(a, b, dims):
    return lax.dot_general(a, b, dims, preferred_element_type=jnp.float32)


def low(a):
    return a.astype(jnp.bfloat16)


def wide(a):
    return a.astype(jnp.float32)


def rows_call(fn, block, row_ins, full_ins, outs, flops, name, scratch=()):
    rows = row_ins[0].shape[0]
    in_specs = [pl.BlockSpec((block, a.shape[1]), lambda i: (i, 0)) for a in row_ins]
    for a in full_ins:
        in_specs.append(
            pl.BlockSpec(
                a.shape, lambda i, nd=a.ndim: (0,) * nd, pipeline_mode=pl.Buffered(1)
            )
        )
    moved = sum(a.size * a.dtype.itemsize for a in (*row_ins, *full_ins))
    moved += sum(rows * w * jnp.dtype(dt).itemsize for w, dt in outs)
    results = pl.pallas_call(
        fn,
        grid=(rows // block,),
        in_specs=in_specs,
        out_specs=[pl.BlockSpec((block, w), lambda i: (i, 0)) for w, _ in outs],
        out_shape=[jax.ShapeDtypeStruct((rows, w), dt) for w, dt in outs],
        scratch_shapes=list(scratch),
        compiler_params=pltpu.CompilerParams(vmem_limit_bytes=VMEM_LIMIT),
        cost_estimate=cost(flops, moved),
        name=name,
    )(*row_ins, *full_ins)
    return list(results)


def turn(u, cosine, sine_signed):
    return u * cosine + pltpu.roll(u, HEAD // 2, 1) * sine_signed


def turn_back(u, cosine, sine_signed):
    return u * cosine - pltpu.roll(u, HEAD // 2, 1) * sine_signed


def project_kernel(
    x0, x1, x2, x3, cos_ref, sin_ref, gain_ref, own_ref, far_ref, xn_ref, qkv_ref, r_ref
):
    pieces = [wide(r[...]) for r in (x0, x1, x2, x3)]
    width = pieces[0].shape[1]
    total = sum(jnp.sum(p * p, axis=1, keepdims=True) for p in pieces)
    ratio = lax.rsqrt(total / (4 * width) + EPSILON)
    r_ref[...] = ratio
    for i, p in enumerate(pieces):
        cols = slice(i * width, (i + 1) * width)
        xn_ref[:, cols] = low(p * ratio * gain_ref[:, cols])
    near = xn_ref[:, : 2 * width]
    far = xn_ref[:, 2 * width :]
    cosine = cos_ref[...]
    sine = sin_ref[...]
    span = own_ref.shape[2]
    heads = span // HEAD
    for g in range(own_ref.shape[0]):
        acc = mxu(near, own_ref[g], NN) + mxu(far, far_ref[g], NN)
        for h in range(heads):
            u = acc[:, h * HEAD : (h + 1) * HEAD]
            if h < heads - 1:
                u = turn(u, cosine, sine)
            at = g * span + h * HEAD
            qkv_ref[:, at : at + HEAD] = low(u)


def segments_of(kind, trunk, leaf_begin, block):
    if kind == "branch":
        return [(0, trunk, None), (None, block, "own")]
    if kind == "leaf":
        return [(0, trunk, None), (trunk, leaf_begin - trunk, "parent"), (None, 2 * block, "own")]
    return [(0, kind, "causal")]


def attention_blocks(qb, block, trunk, leaf_begin, run):
    half = trunk // 2

    @pl.when(qb < half // block)
    def _():
        run(half, 0)

    @pl.when((qb >= half // block) & (qb < trunk // block))
    def _():
        run(trunk, 0)

    @pl.when((qb >= trunk // block) & (qb < leaf_begin // block))
    def _():
        run("branch", pl.multiple_of(qb * block, block))

    @pl.when(qb >= leaf_begin // block)
    def _():
        run("leaf", pl.multiple_of(qb * block - block, block))


def key_rows(start, window, length):
    if start is None:
        return pl.ds(window, length)
    return pl.ds(start, length)


def score_segment(s, start, window, length, mask, qb, block, lab_ref, own_row, parent_row):
    if mask is None:
        return s
    rows = s.shape[0]
    cols = s.shape[1]
    if mask == "parent":
        return jnp.where(lab_ref[key_rows(start, window, length), :] == parent_row, s, -jnp.inf)
    base = window if start is None else start
    key_at = base + lax.broadcasted_iota(jnp.int32, (rows, 1), 0)
    lane = lax.broadcasted_iota(jnp.int32, (1, cols), 1)
    query_at = qb * block + jnp.where(lane >= block, lane - block, lane)
    seen = key_at <= query_at
    if mask == "own":
        seen = seen & (lab_ref[key_rows(start, window, length), :] == own_row)
    return jnp.where(seen, s, -jnp.inf)


def attend_kernel(trunk, leaf_begin, block, q_ref, k_ref, v_ref, lab_ref, row_ref, o_ref, lse_ref, vt_ref):
    qb = pl.program_id(1)
    factor = LOG2E / math.sqrt(HEAD)

    @pl.when(qb == 0)
    def _():
        vt_ref[...] = v_ref[...].T

    queries = jnp.concatenate([q_ref[:, :HEAD], q_ref[:, HEAD:]], axis=0)
    own = row_ref[0:1, :]
    parent = row_ref[1:2, :]
    own_row = jnp.concatenate([own, own], axis=1)
    parent_row = jnp.concatenate([parent, parent], axis=1)

    def run(kind, window):
        scores = []
        segs = segments_of(kind, trunk, leaf_begin, block)
        for start, length, mask in segs:
            s = mxu(k_ref[key_rows(start, window, length), :], queries, NT)
            s = score_segment(
                s, start, window, length, mask, qb, block, lab_ref, own_row, parent_row
            )
            scores.append(s)
        top = scores[0].max(axis=0, keepdims=True)
        for s in scores[1:]:
            top = jnp.maximum(top, s.max(axis=0, keepdims=True))
        total = jnp.zeros_like(top)
        mixed = jnp.zeros((HEAD, 2 * block), jnp.float32)
        shift = top * factor
        for (start, length, mask), s in zip(segs, scores):
            p = jnp.exp2(s * factor - shift)
            total = total + p.sum(axis=0, keepdims=True)
            mixed = mixed + mxu(vt_ref[:, key_rows(start, window, length)], low(p), NN)
        lse_ref[...] = shift + jnp.log2(total)
        mixed = mixed / total
        o_ref[:, :HEAD] = low(mixed[:, :block].T)
        o_ref[:, HEAD:] = low(mixed[:, block:].T)

    attention_blocks(qb, block, trunk, leaf_begin, run)


def attend_back_kernel(
    trunk, leaf_begin, block, blocks, q_ref, k_ref, v_ref, o_ref, do_ref, lab_ref, row_ref, lse_ref,
    cos_ref, sin_ref, out_ref, kt_ref, dk_ref, dv_ref,
):
    qb = pl.program_id(1)
    scale = 1.0 / math.sqrt(HEAD)
    factor = LOG2E * scale

    @pl.when(qb == 0)
    def _():
        kt_ref[...] = k_ref[...].T
        dk_ref[...] = jnp.zeros_like(dk_ref)
        dv_ref[...] = jnp.zeros_like(dv_ref)

    queries = jnp.concatenate([q_ref[:, :HEAD], q_ref[:, HEAD:]], axis=0)
    grads = jnp.concatenate([do_ref[:, :HEAD], do_ref[:, HEAD:]], axis=0)
    outs = jnp.concatenate([o_ref[:, :HEAD], o_ref[:, HEAD:]], axis=0)
    inner = (wide(grads) * wide(outs)).T.sum(axis=0, keepdims=True)
    lse = lse_ref[...]
    own = row_ref[0:1, :]
    parent = row_ref[1:2, :]
    own_row = jnp.concatenate([own, own], axis=1)
    parent_row = jnp.concatenate([parent, parent], axis=1)
    q_rows = pl.ds(pl.multiple_of(qb * block, block), block)

    def run(kind, window):
        dq = jnp.zeros((HEAD, 2 * block), jnp.float32)
        for start, length, mask in segments_of(kind, trunk, leaf_begin, block):
            keys = key_rows(start, window, length)
            s = mxu(k_ref[keys, :], queries, NT)
            s = score_segment(
                s, start, window, length, mask, qb, block, lab_ref, own_row, parent_row
            )
            p = jnp.exp2(s * factor - lse)
            dp = mxu(v_ref[keys, :], grads, NT)
            ds = low(p * (dp - inner))
            dv_ref[keys, :] += mxu(low(p), grads, NN)
            dk_ref[keys, :] += mxu(ds, queries, NN)
            dq = dq + mxu(kt_ref[:, keys], ds, NN)
        dq = dq * scale
        cosine = cos_ref[q_rows, :]
        sine = sin_ref[q_rows, :]
        for h in range(2):
            part = dq[:, h * block : (h + 1) * block].T
            out_ref[q_rows, h * HEAD : (h + 1) * HEAD] = low(turn_back(part, cosine, sine))

    attention_blocks(qb, block, trunk, leaf_begin, run)

    @pl.when(qb == blocks - 1)
    def _():
        dk = dk_ref[...] * scale
        out_ref[:, 2 * HEAD : 3 * HEAD] = low(turn_back(dk, cos_ref[...], sin_ref[...]))
        out_ref[:, 3 * HEAD :] = low(dv_ref[...])


def attention_specs(rows, block, groups):
    q_spec = pl.BlockSpec((block, 2 * HEAD), lambda g, i: (i, 2 * g))
    k_spec = pl.BlockSpec((rows, HEAD), lambda g, i: (0, 4 * g + 2))
    v_spec = pl.BlockSpec((rows, HEAD), lambda g, i: (0, 4 * g + 3))
    lab_spec = pl.BlockSpec((rows, 1), lambda g, i: (0, 0))
    row_spec = pl.BlockSpec((8, block), lambda g, i: (0, i))
    o_spec = pl.BlockSpec((block, 2 * HEAD), lambda g, i: (i, g))
    lse_spec = pl.BlockSpec((None, None, 1, 2 * block), lambda g, i: (g, i, 0, 0))
    return q_spec, k_spec, v_spec, lab_spec, row_spec, o_spec, lse_spec


def attend(qkv, label_col, label_rows, trunk, leaf_begin, block):
    rows = qkv.shape[0]
    groups = qkv.shape[1] // (4 * HEAD)
    blocks = rows // block
    q_spec, k_spec, v_spec, lab_spec, row_spec, o_spec, lse_spec = attention_specs(rows, block, groups)
    pairs = groups * 2 * rows * rows // 2
    return pl.pallas_call(
        functools.partial(attend_kernel, trunk, leaf_begin, block),
        grid=(groups, blocks),
        in_specs=[q_spec, k_spec, v_spec, lab_spec, row_spec],
        out_specs=[o_spec, lse_spec],
        out_shape=[
            jax.ShapeDtypeStruct((rows, groups * 2 * HEAD), jnp.bfloat16),
            jax.ShapeDtypeStruct((groups, blocks, 1, 2 * block), jnp.float32),
        ],
        scratch_shapes=[pltpu.VMEM((HEAD, rows), jnp.bfloat16)],
        compiler_params=pltpu.CompilerParams(vmem_limit_bytes=VMEM_LIMIT),
        cost_estimate=cost(4 * 4 * pairs * HEAD, 20 * rows * HEAD * 2),
        name="attend",
    )(qkv, qkv, qkv, label_col, label_rows)


def attend_back(qkv, attn, attn_grad, label_col, label_rows, lse, cosine, sine, trunk, leaf_begin, block):
    rows = qkv.shape[0]
    groups = qkv.shape[1] // (4 * HEAD)
    blocks = rows // block
    q_spec, k_spec, v_spec, lab_spec, row_spec, o_spec, lse_spec = attention_specs(rows, block, groups)
    table = pl.BlockSpec((rows, HEAD), lambda g, i: (0, 0))
    pairs = groups * 2 * rows * rows // 2
    return pl.pallas_call(
        functools.partial(attend_back_kernel, trunk, leaf_begin, block, blocks),
        grid=(groups, blocks),
        in_specs=[q_spec, k_spec, v_spec, o_spec, o_spec, lab_spec, row_spec, lse_spec, table, table],
        out_specs=pl.BlockSpec((rows, 4 * HEAD), lambda g, i: (0, g)),
        out_shape=jax.ShapeDtypeStruct((rows, groups * 4 * HEAD), jnp.bfloat16),
        scratch_shapes=[
            pltpu.VMEM((HEAD, rows), jnp.bfloat16),
            pltpu.VMEM((rows, HEAD), jnp.float32),
            pltpu.VMEM((rows, HEAD), jnp.float32),
        ],
        compiler_params=pltpu.CompilerParams(vmem_limit_bytes=VMEM_LIMIT),
        cost_estimate=cost(10 * 4 * pairs * HEAD, 40 * rows * HEAD * 2),
        name="attend_back",
    )(qkv, qkv, qkv, attn, attn_grad, label_col, label_rows, lse, cosine, sine)


def quarters_out(acc, out_refs):
    width = out_refs[0].shape[1]
    for i, ref in enumerate(out_refs):
        ref[...] = low(acc[:, i * width : (i + 1) * width])


def mix_kernel(a_ref, near_ref, far_ref, *out_refs):
    groups = near_ref.shape[0]
    span = near_ref.shape[2]
    for i, out_ref in enumerate(out_refs):
        w_ref = (near_ref, far_ref)[i // 2]
        acc = sum(
            mxu(a_ref[:, g * span : (g + 1) * span], w_ref[g, i % 2], NN) for g in range(groups)
        )
        out_ref[...] = low(acc)


def sum_out_kernel(count, *refs):
    a_refs = refs[:count]
    w_refs, out_refs = refs[count:-4], refs[-4:]
    acc = None
    left = list(a_refs)
    at = 0
    for w in w_refs:
        depth = w.shape[0]
        part = mxu(left[0][:, at : at + depth], w[...], NN)
        acc = part if acc is None else acc + part
        at += depth
        if at == left[0].shape[1]:
            left.pop(0)
            at = 0
    quarters_out(acc, out_refs)


def project_back_kernel(d_ref, near_ref, far_ref, *out_refs):
    groups = near_ref.shape[0]
    span = near_ref.shape[2]
    for i, w_ref in enumerate((near_ref, far_ref)):
        acc = sum(mxu(d_ref[:, g * span : (g + 1) * span], w_ref[g], NT) for g in range(groups))
        quarters_out(acc, out_refs[2 * i : 2 * i + 2])


def attn_grad_kernel(h0, h1, h2, h3, near_ref, far_ref, out_ref):
    groups = near_ref.shape[0]
    span = near_ref.shape[2]
    for g in range(groups):
        acc = sum(
            mxu(h[...], (near_ref, far_ref)[i // 2][g, i % 2], NT)
            for i, h in enumerate((h0, h1, h2, h3))
        )
        out_ref[:, g * span : (g + 1) * span] = low(acc)


def gate_up_kernel(*refs):
    x_refs, w_refs, out_refs = refs[:4], refs[4:10], refs[10:14]
    xs_ref = refs[14]
    width = x_refs[0].shape[1]
    for i, x in enumerate(x_refs):
        xs_ref[:, i * width : (i + 1) * width] = x[...]
    normed = xs_ref[...]
    outs = list(out_refs)
    at = 0
    for w_ref in w_refs:
        for start in range(0, w_ref.shape[0], 512):
            size = min(512, w_ref.shape[0] - start)
            product = mxu(normed, w_ref[start : start + size, :], NT)
            outs[0][:, at : at + size] = low(product)
            at += size
        if at == outs[0].shape[1]:
            outs.pop(0)
            at = 0


def hidden_kernel(*refs):
    g_refs, gate_refs, up_refs, w_refs = refs[:4], refs[4:6], refs[6:8], refs[8:11]
    out_refs = refs[11:17]
    gs_ref = refs[17]
    width = g_refs[0].shape[1]
    for i, g in enumerate(g_refs):
        gs_ref[:, i * width : (i + 1) * width] = g[...]
    grads = gs_ref[...]
    unit = 256
    places = [(0, w_refs[0], i, i) for i in range(0, w_refs[0].shape[0], unit)]
    places += [(1, w_refs[1], i, i) for i in range(0, w_refs[1].shape[0], unit)]
    first = w_refs[1].shape[0]
    places += [(1, w_refs[2], i, first + i) for i in range(0, w_refs[2].shape[0], unit)]
    for side, w_ref, row, at in places:
        dgate_ref, dup_ref, hid_ref = out_refs[3 * side : 3 * side + 3]
        cols = slice(at, at + unit)
        gate = wide(gate_refs[side][:, cols])
        upper = wide(up_refs[side][:, cols])
        hidden_grad = mxu(grads, w_ref[row : row + unit, :], NT)
        sigma = jax.nn.sigmoid(gate)
        silu_value = gate * sigma
        hid_ref[:, cols] = low(silu_value * upper)
        dgate_ref[:, cols] = low(hidden_grad * upper * sigma * (1.0 + gate * (1.0 - sigma)))
        dup_ref[:, cols] = low(hidden_grad * silu_value)


def pass_kernel(where_ref, in_ref, out_ref):
    out_ref[...] = in_ref[...]


def next_blocks(gathered, z, planes):
    rows, width = gathered.shape
    unit = rows // planes
    return pl.pallas_call(
        pass_kernel,
        grid_spec=pltpu.PrefetchScalarGridSpec(
            num_scalar_prefetch=1,
            grid=(planes - 1,),
            in_specs=[pl.BlockSpec((unit, width), lambda i, w: (lax.rem(w[0] + 1 + i, planes), 0))],
            out_specs=pl.BlockSpec((unit, width), lambda i, w: (i, 0)),
        ),
        out_shape=jax.ShapeDtypeStruct((rows - unit, width), gathered.dtype),
        compiler_params=pltpu.CompilerParams(vmem_limit_bytes=VMEM_LIMIT),
        cost_estimate=cost(0, 4 * rows * width),
        name="next_blocks",
    )(z.reshape(1), gathered)


def turned_grad_kernel(count, where_ref, *refs):
    weight_grad_kernel(count, 0, *refs)


def turned_grad(a, bs, z, planes, name):
    rows, m = a.shape
    n = sum(b.shape[1] for b in bs)
    unit = m // planes
    in_specs = [
        pl.BlockSpec((rows, unit), lambda i, w: (0, lax.rem(i + planes - w[0], planes)))
    ]
    for b in bs:
        in_specs.append(
            pl.BlockSpec(b.shape, lambda i, w: (0, 0), pipeline_mode=pl.Buffered(1))
        )
    return pl.pallas_call(
        functools.partial(turned_grad_kernel, len(bs)),
        grid_spec=pltpu.PrefetchScalarGridSpec(
            num_scalar_prefetch=1,
            grid=(planes,),
            in_specs=in_specs,
            out_specs=pl.BlockSpec((unit, n), lambda i, w: (i, 0)),
        ),
        out_shape=jax.ShapeDtypeStruct((m, n), jnp.bfloat16),
        compiler_params=pltpu.CompilerParams(vmem_limit_bytes=VMEM_LIMIT),
        cost_estimate=cost(2 * rows * m * n, 2 * (rows * m + rows * n + m * n)),
        name=name,
    )(z.reshape(1), a, *bs)


def ffn_home_kernel(turned, where_ref, *refs):
    part_refs, out_ref = refs[:4], refs[4]
    step = pl.program_id(0)
    at_col, at_core, at_x = step // 4, lax.rem(step // 2, 2), lax.rem(step, 2)
    other_col = jnp.where(at_col == where_ref[0], 0, 1)
    want = 2 * jnp.where(at_x == where_ref[1], 0, 1) + jnp.where(at_core == where_ref[2], 0, 1)
    quarter = part_refs[0].shape[2] // 2
    for j in range(4):

        @pl.when(want == j)
        def _(part=part_refs[j]):
            for h in range(2):
                start = at_core * quarter if h == 0 else (1 - at_core) * quarter
                place = pl.ds(pl.multiple_of(start, quarter), quarter)
                values = wide(part[other_col, :, h * quarter : (h + 1) * quarter])
                if turned:
                    out_ref[place, :] = values.T
                else:
                    out_ref[:, place] = values


def ffn_home(where, parts, at, unit, turned, name):
    half = parts[0].shape[2]
    whole = pl.BlockSpec((2, unit, half), lambda i, w: (0, at, 0), pipeline_mode=pl.Buffered(1))
    if turned:
        spec, shape = pl.BlockSpec((half, unit), lambda i, w: (0, i)), (half, 8 * unit)
    else:
        spec, shape = pl.BlockSpec((unit, half), lambda i, w: (i, 0)), (8 * unit, half)
    return pl.pallas_call(
        functools.partial(ffn_home_kernel, turned),
        grid_spec=pltpu.PrefetchScalarGridSpec(
            num_scalar_prefetch=1, grid=(8,), in_specs=[whole] * 4, out_specs=spec
        ),
        out_shape=jax.ShapeDtypeStruct(shape, jnp.float32),
        compiler_params=pltpu.CompilerParams(vmem_limit_bytes=VMEM_LIMIT),
        cost_estimate=cost(0, 8 * unit * half * 6),
        name=name,
    )(where, *parts)


def weight_grad_kernel(count, split, *refs):
    a_ref = refs[0]
    b_refs = refs[1 : 1 + count]
    o_refs = refs[1 + count :]
    left = a_ref[...].T
    for i, b in enumerate(b_refs):
        width = b.shape[1]
        acc = low(mxu(left, b[...], NN))
        if split:
            for j in range(split):
                o_refs[0][j] = acc[:, j * width // split : (j + 1) * width // split]
        elif len(o_refs) == 1:
            o_refs[0][:, i * width : (i + 1) * width] = acc
        else:
            o_refs[i][...] = acc


def weight_grad(a, bs, block, name, joined=True, split=0):
    rows, m = a.shape
    n = sum(b.shape[1] for b in bs)
    in_specs = [pl.BlockSpec((rows, block), lambda i: (0, i))]
    for b in bs:
        in_specs.append(
            pl.BlockSpec(b.shape, lambda i: (0, 0), pipeline_mode=pl.Buffered(1))
        )
    if split:
        out_specs = [pl.BlockSpec((split, block, n // split), lambda i: (0, i, 0))]
        shapes = [(split, m, n // split)]
    else:
        widths = [n] if joined else [b.shape[1] for b in bs]
        out_specs = [pl.BlockSpec((block, w), lambda i: (i, 0)) for w in widths]
        shapes = [(m, w) for w in widths]
    outs = pl.pallas_call(
        functools.partial(weight_grad_kernel, len(bs), split),
        grid=(m // block,),
        in_specs=in_specs,
        out_specs=out_specs,
        out_shape=[jax.ShapeDtypeStruct(shape, jnp.bfloat16) for shape in shapes],
        compiler_params=pltpu.CompilerParams(vmem_limit_bytes=VMEM_LIMIT),
        cost_estimate=cost(2 * rows * m * n, 2 * (rows * m + rows * n + m * n)),
        name=name,
    )(a, *bs)
    return outs if len(outs) > 1 else outs[0]


def take(a, index, axis):
    return lax.dynamic_index_in_dim(a, index, axis, keepdims=False)


def in_order(index, mine, other, axis=0):
    first = jnp.where(index == 0, mine, other)
    second = jnp.where(index == 0, other, mine)
    return jnp.stack([first, second], axis=axis)


def spread(a):
    b = swap_col(a)
    return [a, b, swap_core(a), swap_core(b)]


def collect_core(parts):
    own, own_other, send, send_other = parts
    outgoing = low(wide(own_other) + wide(swap_core(send_other)))
    return own, swap_core(send), outgoing


def collect_col(own, got, outgoing):
    return wide(own) + wide(got) + wide(swap_col(outgoing))


def small_sum(v):
    cross = lax.ppermute(v, ("dp", "col"), CROSS_SWAP)
    return (v + swap_core(v)) + (swap_col(v) + cross)


def tree_body(
    tokens,
    out_grad,
    path,
    positions,
    w_query,
    w_key,
    w_value,
    w_out,
    w_gate,
    w_up,
    w_down,
    gain_attn,
    gain_ffn,
):
    dp = lax.axis_index("dp")
    x = dp // 2
    c = lax.rem(dp, 2)
    z = lax.axis_index("row")
    y = lax.axis_index("col")
    micro, local_rows, half = tokens.shape
    quarter = half // 2
    rows = path.shape[1]
    planes = lax.axis_size("row")
    features = 2 * half
    block = 256

    def to_trees(a):
        mine = lax.dynamic_slice_in_dim(a, c * quarter, quarter, 2)
        other = swap_core(lax.dynamic_slice_in_dim(a, (1 - c) * quarter, quarter, 2))
        return in_order(c, mine, other).reshape(planes * local_rows, quarter)

    def of_core(trees):
        trees = trees.reshape(2, micro, local_rows, quarter)
        return take(trees, c, 0), take(trees, 1 - c, 0)

    def by_feature(mine, other):
        return in_order(c, mine, swap_core(other), 2).reshape(micro, local_rows, half)

    groups = w_key.shape[1] // HEAD
    share = quarter // 2
    unit = w_gate.shape[1] // 8

    def project_piece(g):
        at = c * quarter + x * share
        return jnp.concatenate(
            [
                lax.dynamic_slice(w_query, (at, g * 2 * HEAD), (share, 2 * HEAD)),
                lax.dynamic_slice(w_key, (at, g * HEAD), (share, HEAD)),
                lax.dynamic_slice(w_value, (at, g * HEAD), (share, HEAD)),
            ],
            axis=1,
        )

    def mix_piece(g):
        return lax.dynamic_slice(w_out, ((g * 2 + x) * HEAD, c * quarter), (HEAD, quarter))

    def by_core(a):
        return jnp.where(c == 0, a, jnp.concatenate([a[:, quarter:], a[:, :quarter]], axis=1))

    def four(kept, got):
        return jnp.concatenate(
            [kept[:, :quarter], got[:, :quarter], kept[:, quarter:], got[:, quarter:]], axis=1
        )

    project_sent = project_piece(1 - y)
    project_mine = jnp.stack([project_piece(y), swap_col(project_sent)])
    trees = to_trees(tokens)
    block_in = lax.all_to_all(trees, "row", 0, 0, tiled=True)
    def hidden_piece(j, xh):
        at = ((2 * j + c) * 2 + xh) * unit
        return [
            by_core(lax.dynamic_slice_in_dim(w_gate, at, unit, 1).T),
            by_core(lax.dynamic_slice_in_dim(w_up, at, unit, 1).T),
            by_core(lax.dynamic_slice_in_dim(w_down, at, unit, 0)),
        ]

    sent = jnp.concatenate([*hidden_piece(1 - y, x), jnp.tile(mix_piece(1 - y), (1, 2))])
    got = swap_col(after(sent, project_sent))
    project_all = lax.all_gather(project_mine, "row", axis=0)

    marks = jnp.concatenate([path, positions[:, :, None]], axis=2)
    marks = jnp.transpose(marks, (2, 0, 1))
    marks = in_order(c, marks, swap_core(marks), 1).reshape(4, 2 * micro, rows)
    marks = take(marks, z, 1)
    cosine, sine = rope_tables(marks[3])
    sign = jnp.where(jnp.arange(HEAD) < HEAD // 2, -1.0, 1.0).astype(jnp.float32)
    sine = sine * sign[None, :]
    label_col = marks[0][:, None]
    label_rows = jnp.pad(marks, ((0, 4), (0, 0)))

    hidden_mine = [
        four(kept, got[i * unit : (i + 1) * unit])
        for i, kept in enumerate(hidden_piece(y, x))
    ]
    mix_mine = jnp.stack([mix_piece(y), got[3 * unit :, :quarter]])
    near_sent = jnp.concatenate(hidden_piece(1 - y, 1 - x))
    near_got = swap_col(after(near_sent, mix_mine))
    hidden_near = [
        four(kept, near_got[i * unit : (i + 1) * unit])
        for i, kept in enumerate(hidden_piece(y, 1 - x))
    ]

    def gain_order(gain):
        kept = gain.reshape(2, quarter)
        both = jnp.stack([kept, swap_col(kept)], axis=1)
        both = jnp.where(c == 0, both, both[::-1])
        return both.reshape(1, features)

    gain_attn_all = gain_order(gain_attn)
    gain_attn_own = gain_attn_all[:, :quarter]
    gain_ffn_own = lax.dynamic_slice_in_dim(gain_ffn, c * quarter, quarter, 0)[None, :]

    (
        project_all, block_in, mix_mine, gate_piece, up_piece, down_piece,
        gate_near, up_near, down_near, cosine, sine, label_col, label_rows, gain_attn_all,
    ) = lax.optimization_barrier(
        (
            project_all, block_in, mix_mine, *hidden_mine, *hidden_near,
            cosine, sine, label_col, label_rows, gain_attn_all,
        )
    )

    pieces = spread(block_in)
    mix_all = lax.all_gather(mix_mine, "row", axis=0)
    gate_mine = lax.all_gather(gate_piece, "row", axis=0, tiled=True)
    up_mine = lax.all_gather(after(up_piece, mix_all), "row", axis=0, tiled=True)
    down_mine = lax.all_gather(after(down_piece, gate_mine), "row", axis=0, tiled=True)
    gate_next, up_next, down_next = (
        next_blocks(u, z, planes) for u in (gate_mine, up_mine, down_mine)
    )
    gate_far, up_far, down_far = (swap_x(u) for u in (gate_next, up_next, down_next))

    def of_core_pairs(mine, other):
        both = in_order(x, mine, other, 2)
        pairs = both.reshape((2, planes // 2) + both.shape[1:])
        return take(pairs, c, 0), swap_core(take(pairs, 1 - c, 0))

    near, far = of_core_pairs(project_all, swap_x(project_all))
    w_near = near.reshape(groups, half, 4 * HEAD)
    w_far = far.reshape(groups, half, 4 * HEAD)

    normed_attn, qkv, ratio_attn = rows_call(
        project_kernel,
        block,
        [*pieces, cosine, sine],
        [gain_attn_all, w_near, w_far],
        [(features, jnp.bfloat16), (groups * 4 * HEAD, jnp.bfloat16), (1, jnp.float32)],
        2 * rows * features * groups * 4 * HEAD,
        "project",
    )
    near, far = of_core_pairs(mix_all, after(swap_x(mix_all), qkv))
    attn, lse = attend(after(qkv, near), label_col, label_rows, TRUNK, LEAF_BEGIN, block)
    mix_shape = (groups, 2, 2 * HEAD, quarter)
    m_near, m_far = near.reshape(mix_shape), after(far, attn).reshape(mix_shape)
    parts = rows_call(
        mix_kernel,
        2 * block,
        [attn],
        [m_near, m_far],
        [(quarter, jnp.bfloat16)] * 4,
        2 * rows * features * groups * 2 * HEAD,
        "mix",
    )
    cotangent = lax.all_to_all(to_trees(out_grad), "row", 0, 0, tiled=True)
    parts[1] = after(parts[1], cotangent, gate_next)
    own, got, outgoing = collect_core(parts)
    middle = wide(block_in) + collect_col(own, got, outgoing)
    square = small_sum(jnp.sum(middle * middle, axis=1))
    ratio_ffn = lax.rsqrt(square / features + EPSILON)[:, None]
    normed_ffn = middle * ratio_ffn
    ffn_near = after(low(normed_ffn * gain_ffn_own), up_next, gate_far)
    ffn_across = swap_col(ffn_near)
    ffn_pieces = [ffn_near, ffn_across, swap_core(ffn_near), swap_core(ffn_across)]
    grad_near, grad_across = cotangent, swap_col(after(cotangent, ffn_pieces[1]))
    gate_m, up_m, gate_o, up_o = rows_call(
        gate_up_kernel,
        block,
        ffn_pieces,
        [gate_mine, up_mine, gate_near, gate_far, up_near, up_far],
        [(planes * unit, jnp.bfloat16)] * 4,
        2 * rows * features * 4 * planes * unit,
        "gate_up",
        [pltpu.VMEM((block, features), jnp.bfloat16)],
    )
    grad_pieces = [
        grad_near,
        grad_across,
        swap_core(after(grad_near, ffn_pieces[3])),
        swap_core(after(grad_across, gate_m)),
    ]
    dgate_m, dup_m, hid_m, dgate_o, dup_o, hid_o = rows_call(
        hidden_kernel,
        block,
        [*grad_pieces, gate_m, gate_o, up_m, up_o],
        [down_mine, down_near, down_far],
        [(planes * unit, jnp.bfloat16)] * 6,
        2 * rows * features * 2 * planes * unit,
        "hidden",
        [pltpu.VMEM((block, features), jnp.bfloat16)],
    )

    def unit_grad(a, pieces_of, name, before):
        return weight_grad(after(a, before), pieces_of, 2 * block, name)

    def to_row(total):
        return lax.psum_scatter(total, "row", scatter_dimension=0, tiled=True)

    down_other = turned_grad(hid_o, grad_pieces, z, planes, "down_grad_other")
    parts = rows_call(
        functools.partial(sum_out_kernel, 4),
        2 * block,
        [after(dgate_m, down_other), dup_m, dgate_o, dup_o],
        [gate_mine, up_mine, gate_near, gate_far, up_near, up_far],
        [(quarter, jnp.bfloat16)] * 4,
        2 * rows * features * 4 * planes * unit,
        "pair_back",
    )
    gate_other = turned_grad(after(dgate_o, parts[0]), ffn_pieces, z, planes, "gate_grad_other")
    down_own = unit_grad(hid_m, grad_pieces, "down_grad_mine", gate_other)
    parts[1] = after(parts[1], down_own)
    own, got, outgoing = collect_core(parts)
    up_other = turned_grad(after(dup_o, outgoing), ffn_pieces, z, planes, "up_grad_other")
    gate_own = unit_grad(dgate_m, ffn_pieces, "gate_grad_mine", up_other)
    down_total = low(wide(after(down_own, gate_own)) + wide(swap_x(down_other)))
    down_sum = to_row(down_total)
    normed_ffn_grad = collect_col(after(own, down_total), got, outgoing)

    def norm_back(grad, ratio, normed, gain):
        scaled = grad * gain
        inner = small_sum(jnp.sum(scaled * normed, axis=1))[:, None] / features
        return ratio * (scaled - normed * inner), jnp.sum(grad * normed, axis=0)

    middle_back, gain_ffn_part = norm_back(normed_ffn_grad, ratio_ffn, normed_ffn, gain_ffn_own)
    middle_grad = wide(cotangent) + middle_back
    middle_low = low(middle_grad)
    up_own = unit_grad(dup_m, ffn_pieces, "up_grad_mine", middle_low)
    where = jnp.stack([y, x, c]).astype(jnp.int32)

    def unit_halves(total):
        kept = jnp.concatenate([total[:, :quarter], total[:, half : half + quarter]], axis=1)
        sent = jnp.concatenate([total[:, quarter:half], total[:, half + quarter :]], axis=1)
        return kept, sent

    def unit_parts(kept, sent, first, second):
        both = jnp.stack([kept, after(swap_col(sent), first)])
        over = after(swap_x(both), second)
        return [both, swap_core(both), over, swap_core(over)]

    out_parts = rows_call(
        functools.partial(sum_out_kernel, 2),
        2 * block,
        [after(hid_m, up_own), hid_o],
        [down_mine, down_near, down_far],
        [(quarter, jnp.bfloat16)] * 4,
        2 * rows * features * 2 * planes * unit,
        "down",
    )
    middle_across = after(swap_col(middle_low), out_parts[0])
    middle_pieces = [middle_low, middle_across, swap_core(middle_low), swap_core(middle_across)]
    attn_grad = rows_call(
        attn_grad_kernel,
        2 * block,
        middle_pieces,
        [m_near, m_far],
        [(groups * 2 * HEAD, jnp.bfloat16)],
        2 * rows * features * groups * 2 * HEAD,
        "attn_grad",
    )[0]
    gate_total = low(wide(after(gate_own, attn_grad)) + wide(swap_x(gate_other)))
    gate_sum = to_row(gate_total)
    out_parts[1] = after(out_parts[1], gate_total)
    out_own, out_got, out_outgoing = collect_core(out_parts)
    qkv_grad = attend_back(
        qkv, attn, after(attn_grad, out_outgoing), label_col, label_rows, lse, cosine, sine,
        TRUNK, LEAF_BEGIN, block,
    )
    output = low(after(middle, qkv_grad) + collect_col(out_own, out_got, out_outgoing))
    parts = rows_call(
        project_back_kernel,
        2 * block,
        [after(qkv_grad, output)],
        [w_near, w_far],
        [(quarter, jnp.bfloat16)] * 4,
        2 * rows * features * groups * 4 * HEAD,
        "project_back",
    )
    up_total = low(wide(after(up_own, parts[0])) + wide(swap_x(up_other)))
    up_sum = to_row(up_total)
    parts[1] = after(parts[1], up_total)
    output_tree = lax.all_to_all(output, "row", 0, 0, tiled=True)
    own, got, outgoing = collect_core(parts)
    project_grad = weight_grad(
        normed_attn, [after(qkv_grad, outgoing)], 2 * block, "project_grad", split=groups
    )
    mix_grads = weight_grad(
        attn,
        [after(middle_pieces[0], project_grad), *middle_pieces[1:]],
        groups * 2 * HEAD,
        "mix_grad",
        joined=False,
    )

    project_parts = project_grad.reshape(groups, 2, 2, 2, share, 4 * HEAD)
    mix_parts = jnp.stack([m.reshape(groups, 2, HEAD, quarter) for m in mix_grads], axis=1)
    mix_parts = mix_parts.reshape(groups, 2, 2, 2, HEAD, quarter)

    def of_x(index):
        return jnp.concatenate([take(project_parts, index, 3), take(mix_parts, index, 3)], axis=3)

    attn_sent = of_x(1 - x)
    attn_kept = of_x(after(x, attn_sent))
    normed_attn_grad = collect_col(after(own, attn_kept), got, outgoing)
    normed_attn_own = wide(block_in) * ratio_attn
    input_back, gain_attn_part = norm_back(
        normed_attn_grad, ratio_attn, normed_attn_own, gain_attn_own
    )
    input_low = low(middle_grad + input_back)
    input_tree = lax.all_to_all(input_low, "row", 0, 0, tiled=True)
    home_kept, home_sent = unit_halves(
        jnp.concatenate([after(down_sum, input_low), gate_sum])
    )
    output, output_sent = of_core(after(output_tree, home_sent))
    home_both = jnp.stack([home_kept, after(swap_col(home_sent), output_sent)])
    home_over = swap_x(home_both)
    attn_total = low(wide(after(attn_kept, home_both)) + wide(swap_x(attn_sent)))
    by_plane = in_order(c, attn_total[:, 0], swap_core(attn_total[:, 1]))
    by_plane = by_plane.reshape((planes,) + by_plane.shape[2:])
    attn_sum = lax.psum_scatter(by_plane, "row", scatter_dimension=0, tiled=False)
    output = by_feature(after(output, by_plane), output_sent)
    up_kept, up_sent = unit_halves(after(up_sum, output))
    home_over = after(home_over, up_sent)
    home_parts = [home_both, swap_core(home_both), home_over, swap_core(home_over)]
    down_out = ffn_home(where, home_parts, 0, unit, False, "down_home")
    gate_out = ffn_home(where, home_parts, 1, unit, True, "gate_home")
    attn_sum = after(attn_sum, down_out, gate_out)
    home = in_order(y, attn_sum[0], swap_col(attn_sum[1]))
    up_parts = unit_parts(up_kept, up_sent, gate_out, home)
    up_out = ffn_home(where, up_parts, 0, unit, True, "up_home")
    home = in_order(x, home, after(swap_x(home), up_out))
    input_grad = by_feature(*of_core(after(input_tree, up_out)))
    home = in_order(c, home, swap_core(home))
    mix_home = home[:, :, :, share:]
    out_out = wide(jnp.transpose(mix_home, (2, 1, 3, 0, 4)).reshape(groups * 2 * HEAD, half))
    project_home = jnp.transpose(home[:, :, :, :share], (0, 1, 3, 2, 4))
    project_home = project_home.reshape(half, groups, 4 * HEAD)
    query_out = wide(project_home[:, :, : 2 * HEAD].reshape(half, groups * 2 * HEAD))
    key_out = wide(project_home[:, :, 2 * HEAD : 3 * HEAD].reshape(half, groups * HEAD))
    value_out = wide(project_home[:, :, 3 * HEAD :].reshape(half, groups * HEAD))

    gains = jnp.stack([gain_attn_part, gain_ffn_part])
    gains = gains + shift(gains, ROW_SECOND)
    gains = gains + shift(gains, ROW_SWAP)
    gains = gains + swap_x(gains)
    gains = in_order(c, gains, swap_core(gains), 1)
    gain_attn_out = gains[0].reshape(half)
    gain_ffn_out = gains[1].reshape(half)
    return (
        output,
        input_grad,
        query_out,
        key_out,
        value_out,
        out_out,
        gate_out,
        up_out,
        down_out,
        gain_attn_out,
        gain_ffn_out,
    )


def solution(mesh):
    in_specs = (
        P(None, ("dp", "row"), "col"),
        P(None, ("dp", "row"), "col"),
        P(None, "dp", None),
        P(None, "dp"),
        P("col", "row"),
        P("col", "row"),
        P("col", "row"),
        P("row", "col"),
        P("col", "row"),
        P("col", "row"),
        P("row", "col"),
        P("col"),
        P("col"),
    )
    out_specs = (
        P(None, ("dp", "row"), "col"),
        P(None, ("dp", "row"), "col"),
        P("col", "row"),
        P("col", "row"),
        P("col", "row"),
        P("row", "col"),
        P("col", "row"),
        P("col", "row"),
        P("row", "col"),
        P("col"),
        P("col"),
    )
    sizes = dict(mesh.shape)
    fits = sizes == {"dp": 4, "row": 4, "col": 2}
    chosen = tree_body if fits else body
    return jax.shard_map(chosen, mesh=mesh, in_specs=in_specs, out_specs=out_specs, check_vma=False)
```
